32 devices in a mesh: dp: 8 (over y, x, core), head: 4 (over z).
Axes of the slice: x: 2, y: 2, z: 4, core: 2. Of those that a mesh axis runs over, the one named last changes fastest.
Arguments:
- inputs: bfloat16 [16, 1024, 768], P('dp'), may hold values from -6 to 6
- cotangent: bfloat16 [16, 1024, 768], P('dp'), may hold values from -6 to 6
- lengths: int32 [16], P('dp'), may hold values from 100 to 1024, as said below
- proj_master: float32 [3, 768, 768], P(None, 'dp', 'head'), may hold values from -0.3125 to 0.3125
- proj_first: float32 [3, 768, 768], P(None, 'dp', 'head'), may hold values from -0.00024414062 to 0.00024414062
- proj_second: float32 [3, 768, 768], P(None, 'dp', 'head'), may hold values from 7.48811e-09 to 2.9669868e-08
- out_master: float32 [768, 768], P('head', 'dp')
- out_first: float32 [768, 768], P('head', 'dp'), may hold values from -0.00024414062 to 0.00024414062
- out_second: float32 [768, 768], P('head', 'dp'), may hold values from 7.48811e-09 to 2.9669868e-08
- up_master: float32 [768, 3072], P('dp', 'head')
- up_first: float32 [768, 3072], P('dp', 'head'), may hold values from -0.00024414062 to 0.00024414062
- up_second: float32 [768, 3072], P('dp', 'head'), may hold values from 7.48811e-09 to 2.9669868e-08
- down_master: float32 [3072, 768], P('head', 'dp')
- down_first: float32 [3072, 768], P('head', 'dp'), may hold values from -0.00024414062 to 0.00024414062
- down_second: float32 [3072, 768], P('head', 'dp'), may hold values from 7.48811e-09 to 2.9669868e-08
- norm_master: float32 [4, 768], P(None, 'dp')
- norm_first: float32 [4, 768], P(None, 'dp'), may hold values from -0.0007324219 to 0.0007324219
- norm_second: float32 [4, 768], P(None, 'dp'), may hold values from 6.640399e-08 to 2.6844165e-07
Outputs:
- layer_out: bfloat16 [16, 1024, 768], P('dp', 'head')
- input_grad: bfloat16 [16, 1024, 768], P('dp', 'head')
- grad_norm: float32 [], replicated
- proj_new: float32 [3, 768, 768], P(None, 'dp', 'head')
- proj_first_new: float32 [3, 768, 768], P(None, 'dp', 'head')
- proj_second_new: float32 [3, 768, 768], P(None, 'dp', 'head')
- proj_copy: bfloat16 [3, 768, 768], P(None, 'dp', 'head')
- out_new: float32 [768, 768], P('head', 'dp')
- out_first_new: float32 [768, 768], P('head', 'dp')
- out_second_new: float32 [768, 768], P('head', 'dp')
- out_copy: bfloat16 [768, 768], P('head', 'dp')
- up_new: float32 [768, 3072], P('dp', 'head')
- up_first_new: float32 [768, 3072], P('dp', 'head')
- up_second_new: float32 [768, 3072], P('dp', 'head')
- up_copy: bfloat16 [768, 3072], P('dp', 'head')
- down_new: float32 [3072, 768], P('head', 'dp')
- down_first_new: float32 [3072, 768], P('head', 'dp')
- down_second_new: float32 [3072, 768], P('head', 'dp')
- down_copy: bfloat16 [3072, 768], P('head', 'dp')
- norm_new: float32 [4, 768], P(None, 'dp')
- norm_first_new: float32 [4, 768], P(None, 'dp')
- norm_second_new: float32 [4, 768], P(None, 'dp')
- norm_copy: bfloat16 [4, 768], P(None, 'dp')
The draws below stay inside these ranges and needn't reach their ends.
Inputs may be any that keep to these rules, and one draw needn't show every extreme that they name: `lengths`: some sequence is 1024 codons long.
All inputs are finite; a program needn't handle non-finite values.
Results may differ from the reference program's by a relative error of at most 0.014.
The reference program's roundings to bfloat16 on the way count: a program that leaves them out, or rounds other values in their place, can miss the bound.
Values may be sent and summed in bfloat16 or wider, within the bound.
A program may use at most 128 MiB of HBM per device.

```python
import jax
import jax.numpy as jnp
from jax import lax

D = 768
HD = 64
FF = 3072
LEN = 1024
MIN_LEN = 100
STEP = 5
ROWS = 16
PCOUNT = 7077888


def ramp_matrix(key, row_count, col_count, ramp_axis, low_end, scale_all):
    entries = jax.random.normal(key, (row_count, col_count), jnp.float32)
    extent = row_count if ramp_axis == 0 else col_count
    ramp_values = low_end + jnp.arange(extent, dtype=jnp.float32) / (extent - 1)
    if ramp_axis == 0:
        ramp_values = ramp_values[:, None]
    else:
        ramp_values = ramp_values[None, :]
    return entries * ramp_values * scale_all


def draw_lengths(key, part):
    key = jax.random.fold_in(key, 11)
    row_ids = jnp.arange(ROWS, dtype=jnp.int32)
    cap_length = MIN_LEN + (LEN - MIN_LEN) * (ROWS + 2 * row_ids) // (3 * ROWS - 2)
    span_width = cap_length - MIN_LEN + 1
    first_key, second_key = jax.random.split(key)
    first_pick = jax.random.randint(first_key, (ROWS,), 0, 1 << 30, dtype=jnp.int32) % span_width
    second_pick = jax.random.randint(second_key, (ROWS,), 0, 1 << 30, dtype=jnp.int32) % span_width
    picked = MIN_LEN + jnp.maximum(first_pick, second_pick)
    picked = jnp.where(row_ids == ROWS - 1, LEN, picked)
    return picked.astype(jnp.int32)


def draw_out_master(key, part):
    key = jax.random.fold_in(key, 21)
    low_end = 0.5
    return ramp_matrix(key, D, D, 0, low_end, 2.5 / D ** 0.5)


def draw_up_master(key, part):
    key = jax.random.fold_in(key, 22)
    low_end = 0.5
    return ramp_matrix(key, D, FF, 1, low_end, 1.0 / D ** 0.5)


def draw_down_master(key, part):
    key = jax.random.fold_in(key, 23)
    low_end = 0.5
    return ramp_matrix(key, FF, D, 0, low_end, 1.0 / FF ** 0.5)


def draw_norm_master(key, part):
    key = jax.random.fold_in(key, 24)
    factor_key, shift_key = jax.random.split(key)
    factors = jax.random.uniform(factor_key, (4, D), jnp.float32, 0.8, 1.2)
    low_end = 0.5
    shifts = 0.3 * jax.random.normal(shift_key, (4, D), jnp.float32)
    ramp_values = low_end + jnp.arange(D, dtype=jnp.float32) / (D - 1)
    gains = factors * ramp_values[None, :]
    is_gain = (jnp.arange(4) % 2 == 0)[:, None]
    return jnp.where(is_gain, gains, shifts).astype(jnp.float32)


def with_spikes(values, key, source, target, blocks, factor):
    def block_of(position):
        return (jnp.arange(values.shape[position]) // (values.shape[position] // blocks)).reshape((-1,) + (1,) * (values.ndim - 1 - position))

    near = jax.random.permutation(key, blocks)[block_of(target)]
    other_side = (block_of(target) + blocks // 2) % blocks
    return jnp.where((block_of(source) == near) | (block_of(source) == other_side), factor * values, values)


def block_levels(rng, shape, shards, smallest, largest):
    def one(dim, blocks):
        heights = jax.random.uniform(jax.random.fold_in(jax.random.fold_in(rng, 6), dim), (blocks,), jnp.float32, smallest / len(shards), largest / len(shards))
        return jnp.repeat(jnp.exp(heights), shape[dim] // blocks).reshape((-1,) + (1,) * (len(shape) - dim - 1))

    gain = one(*shards[0])
    for cut in shards[1:]:
        gain = gain * one(*cut)
    return gain


def gaussian(own_key, shape, scale, bound, cuts=(), held_as=jnp.bfloat16):
    values = jax.random.normal(own_key, shape, jnp.float32) * scale
    if len(cuts) > 0:
        values = block_levels(own_key, shape, cuts, -0.22, 0.18) * values
    return jnp.clip(values, min=-bound, max=bound).astype(held_as)


def heavy_noise(rng, dims, width, bound, cuts, heavy, held_as=jnp.bfloat16):
    values = width * jax.random.normal(rng, dims, jnp.float32)
    if cuts:
        values = values * block_levels(rng, dims, cuts, -0.22, 0.18)
    return jnp.clip(with_spikes(values, jax.random.fold_in(rng, 3), *heavy), -bound, bound).astype(held_as)


def setup_inputs(seed: int = 0) -> dict:
    arg_keys = jax.random.split(jax.random.key(seed), 19)
    return {
        "inputs": heavy_noise(arg_keys[0], (ROWS, LEN, D), 1.0, 6.0, ((0, 8),), (0, 2, 8, 2.0)),
        "cotangent": heavy_noise(arg_keys[1], (ROWS, LEN, D), 1.0, 6.0, ((0, 8),), (0, 2, 8, 2.0)),
        "lengths": draw_lengths(jax.random.fold_in(arg_keys[18], 71), 0),
        "proj_master": gaussian(arg_keys[3], (3, D, D), (D // 2) ** -0.5, 0.3125, ((1, 8), (2, 4)), jnp.float32),
        "proj_first": gaussian(arg_keys[4], (3, D, D), (0.11 / PCOUNT ** 0.5), 0.00024414062, ((1, 8), (2, 4)), jnp.float32),
        "proj_second": jnp.clip(7.488109687869837e-09 + 2.2181758652095596e-08 * jax.random.uniform(arg_keys[5], (3, D, D), jnp.float32) ** block_levels(arg_keys[5], (3, D, D), ((1, 8), (2, 4)), -0.2, 0.2), 7.488109687869837e-09, 2.9669868339965433e-08),
        "out_master": draw_out_master(jax.random.fold_in(arg_keys[18], 71), 0),
        "out_first": gaussian(arg_keys[7], (D, D), (0.11 / PCOUNT ** 0.5), 0.00024414062, ((0, 4), (1, 8)), jnp.float32),
        "out_second": jnp.clip(7.488109687869837e-09 + 2.2181758652095596e-08 * jax.random.uniform(arg_keys[8], (D, D), jnp.float32) ** block_levels(arg_keys[8], (D, D), ((0, 4), (1, 8)), -0.2, 0.2), 7.488109687869837e-09, 2.9669868339965433e-08),
        "up_master": draw_up_master(jax.random.fold_in(arg_keys[18], 71), 0),
        "up_first": gaussian(arg_keys[10], (D, FF), (0.11 / PCOUNT ** 0.5), 0.00024414062, ((0, 8), (1, 4)), jnp.float32),
        "up_second": jnp.clip(7.488109687869837e-09 + 2.2181758652095596e-08 * jax.random.uniform(arg_keys[11], (D, FF), jnp.float32) ** block_levels(arg_keys[11], (D, FF), ((0, 8), (1, 4)), -0.2, 0.2), 7.488109687869837e-09, 2.9669868339965433e-08),
        "down_master": draw_down_master(jax.random.fold_in(arg_keys[18], 71), 0),
        "down_first": gaussian(arg_keys[13], (FF, D), (0.11 / PCOUNT ** 0.5), 0.00024414062, ((0, 4), (1, 8)), jnp.float32),
        "down_second": jnp.clip(7.488109687869837e-09 + 2.2181758652095596e-08 * jax.random.uniform(arg_keys[14], (FF, D), jnp.float32) ** block_levels(arg_keys[14], (FF, D), ((0, 4), (1, 8)), -0.2, 0.2), 7.488109687869837e-09, 2.9669868339965433e-08),
        "norm_master": draw_norm_master(jax.random.fold_in(arg_keys[18], 71), 0),
        "norm_first": gaussian(arg_keys[16], (4, D), (0.33 / PCOUNT ** 0.5), 0.0007324219, ((1, 8),), jnp.float32),
        "norm_second": jnp.clip(6.640399163870825e-08 + 2.020376612676955e-07 * jax.random.uniform(arg_keys[17], (4, D), jnp.float32) ** block_levels(arg_keys[17], (4, D), ((1, 8),), -0.2, 0.2), 6.640399163870825e-08, 2.6844165290640376e-07),
    }


HIGHEST = lax.Precision.HIGHEST
LN_EPSILON = 1e-05
MASK_FILL = -1e+30
ROPE_BASE = 10000.0
CLIP_LIMIT = 1.0
BETA_FIRST = 0.9
BETA_SECOND = 0.95
ADAM_EPSILON = 1e-08
WEIGHT_DECAY = 0.1
RATE_MATRIX = 0.03
RATE_NORM = 0.3

@jax.custom_vjp
def low(v):
    return lax.optimization_barrier(v.astype(jnp.bfloat16)).astype(jnp.float32)

@jax.custom_vjp
def low_back(v):
    return v

def low_keep(v):
    return (low(v), None)

def low_pass(kept, grad):
    return (grad,)

def back_keep(v):
    return (v, None)

def back_low(kept, grad):
    return (low(grad),)
low.defvjp(low_keep, low_pass)
low_back.defvjp(back_keep, back_low)

def layer_norm(values, gain_row, shift_row):
    center = values - lax.optimization_barrier(jnp.mean(values, axis=-1, keepdims=True))
    spread = lax.optimization_barrier(jnp.mean(center * center, axis=-1, keepdims=True))
    return center * lax.rsqrt(spread + LN_EPSILON) * gain_row + shift_row

def rope_tables(length, head_width):
    places = jnp.arange(length).astype(jnp.float32)
    freq_rates = ROPE_BASE ** (-(jnp.arange(head_width // 2).astype(jnp.float32) * 2.0 / head_width))
    angles = places[:, None] * freq_rates[None, :]
    cosine_table = jnp.concatenate([jnp.cos(angles), jnp.cos(angles)], axis=-1)
    sine_table = jnp.concatenate([jnp.sin(angles), jnp.sin(angles)], axis=-1)
    return (cosine_table, sine_table)

def rotate(values, cosine_table, sine_table):
    half_width = values.shape[-1] // 2
    turned = jnp.concatenate([-values[..., half_width:], values[..., :half_width]], axis=-1)
    return values * cosine_table[:, None, :] + turned * sine_table[:, None, :]

def forward(params, inputs, valid_keys, cosine_table, sine_table):
    proj_w = low(params[0])
    out_w = low(params[1])
    up_w = low(params[2])
    down_w = low(params[3])
    norm_w = low(params[4])
    groups, length, model_width = inputs.shape
    heads_all = model_width // HD
    hidden_one = low(layer_norm(inputs, norm_w[0], norm_w[1]))
    raw_proj = low_back(jnp.einsum('gld,jdc->jglc', hidden_one, proj_w, precision=HIGHEST))
    shaped = raw_proj.reshape(3, groups, length, heads_all, HD)
    queries = low(rotate(shaped[0], cosine_table, sine_table) * HD ** (-0.5))
    key_rows = low(rotate(shaped[1], cosine_table, sine_table))
    value_rows = low(shaped[2])
    scores = low_back(jnp.einsum('gqhd,gkhd->ghqk', queries, key_rows, precision=HIGHEST))
    scores = jnp.where(valid_keys[:, None, None, :], scores, MASK_FILL)
    probs_low = low(jax.nn.softmax(scores, axis=-1))
    mixed_heads = jnp.einsum('ghqk,gkhd->gqhd', probs_low, value_rows, precision=HIGHEST)
    mixed_heads = low(low_back(mixed_heads.reshape(groups, length, model_width)))
    branch = low_back(jnp.einsum('gld,de->gle', mixed_heads, out_w, precision=HIGHEST))
    middle = inputs + branch
    hidden_two = low(layer_norm(middle, norm_w[2], norm_w[3]))
    upper_rows = low_back(jnp.einsum('gld,df->glf', hidden_two, up_w, precision=HIGHEST))
    gated_rows = low(jax.nn.gelu(upper_rows, approximate=False))
    ffn_rows = low_back(jnp.einsum('glf,fd->gld', gated_rows, down_w, precision=HIGHEST))
    return middle + ffn_rows

def adam_update(master, first_old, second_old, gradient, clip_factor, step_rate, decay_rate):
    clipped = gradient * clip_factor
    first_new = BETA_FIRST * first_old + (1.0 - BETA_FIRST) * clipped
    second_new = BETA_SECOND * second_old + (1.0 - BETA_SECOND) * clipped * clipped
    fix_first = 1.0 - BETA_FIRST ** STEP
    fix_second = 1.0 - BETA_SECOND ** STEP
    normalized = first_new / fix_first / (jnp.sqrt(second_new / fix_second) + ADAM_EPSILON)
    master_new = master - step_rate * (normalized + decay_rate * master)
    return (master_new, first_new, second_new, master_new.astype(jnp.bfloat16))

def reference(inputs, cotangent, lengths, proj_master, proj_first, proj_second, out_master, out_first, out_second, up_master, up_first, up_second, down_master, down_first, down_second, norm_master, norm_first, norm_second):
    params = (proj_master, out_master, up_master, down_master, norm_master)
    cosine_table, sine_table = rope_tables(LEN, HD)
    valid_keys = jnp.arange(LEN).astype(jnp.int32)[None, :] < lengths[:, None]
    pair_count = ROWS // 2
    stacked_in = inputs.astype(jnp.float32).reshape(pair_count, 2, LEN, D)
    masked_back = cotangent.astype(jnp.float32) * valid_keys[:, :, None].astype(jnp.float32)
    stacked_back = masked_back.reshape(pair_count, 2, LEN, D)
    stacked_valid = valid_keys.reshape(pair_count, 2, LEN)
    initial = jax.tree.map(lambda tensor: jnp.zeros(tensor.shape, jnp.float32), params)

    def accumulate(totals, block_item):
        block_in, block_back, block_valid = block_item

        def local_layer(weights, values_in):
            return forward(weights, values_in, block_valid, cosine_table, sine_table)
        result, pullback = jax.vjp(local_layer, params, block_in)
        weight_grads, grad_in = pullback(block_back)
        return (jax.tree.map(jnp.add, totals, weight_grads), (result, grad_in))
    totals, (outputs, input_grads) = lax.scan(accumulate, initial, (stacked_in, stacked_back, stacked_valid))
    layer_out = outputs.reshape(ROWS, LEN, D).astype(jnp.bfloat16)
    input_grad = input_grads.reshape(ROWS, LEN, D).astype(jnp.bfloat16)
    squares = jnp.sum(totals[0] * totals[0]) + jnp.sum(totals[1] * totals[1]) + jnp.sum(totals[2] * totals[2])
    squares = squares + jnp.sum(totals[3] * totals[3]) + jnp.sum(totals[4] * totals[4])
    grad_norm = jnp.sqrt(squares)
    clip_factor = jnp.minimum(1.0, CLIP_LIMIT / (grad_norm + 1e-06))
    proj_up = adam_update(proj_master, proj_first, proj_second, totals[0], clip_factor, RATE_MATRIX, WEIGHT_DECAY)
    out_up = adam_update(out_master, out_first, out_second, totals[1], clip_factor, RATE_MATRIX, WEIGHT_DECAY)
    up_up = adam_update(up_master, up_first, up_second, totals[2], clip_factor, RATE_MATRIX, WEIGHT_DECAY)
    down_up = adam_update(down_master, down_first, down_second, totals[3], clip_factor, RATE_MATRIX, WEIGHT_DECAY)
    norm_up = adam_update(norm_master, norm_first, norm_second, totals[4], clip_factor, RATE_NORM, 0.0)
    return (layer_out, input_grad, grad_norm, proj_up[0], proj_up[1], proj_up[2], proj_up[3], out_up[0], out_up[1], out_up[2], out_up[3], up_up[0], up_up[1], up_up[2], up_up[3], down_up[0], down_up[1], down_up[2], down_up[3], norm_up[0], norm_up[1], norm_up[2], norm_up[3])
```

```python
import functools

import jax
import jax.numpy as jnp
import numpy as np
from jax import lax
from jax.experimental import pallas as pl
from jax.experimental.pallas import tpu as pltpu
from jax.sharding import PartitionSpec as P

HD = 64
STEP = 5
LN_EPSILON = 1e-05
MASK_FILL = -1e30
ROPE_BASE = 10000.0
CLIP_LIMIT = 1.0
BETA_FIRST = 0.9
BETA_SECOND = 0.95
ADAM_EPSILON = 1e-08
WEIGHT_DECAY = 0.1
RATE_MATRIX = 0.03
RATE_NORM = 0.3
INV_ROOT_TWO = 0.7071067811865476
INV_ROOT_TWO_PI = 0.3989422804014327

F32 = jnp.float32
BF16 = jnp.bfloat16
MESH = pl.DeviceIdType.MESH
SUB = 256
PIECES = 9


def dot(a, b):
    return lax.dot_general(a, b, (((1,), (0,)), ((), ())), preferred_element_type=F32)


def dot_t(a, b):
    return lax.dot_general(a, b, (((1,), (1,)), ((), ())), preferred_element_type=F32)


def row_mean(v):
    return jnp.mean(v, axis=-1, keepdims=True)


def normalize(v):
    center = v - row_mean(v)
    inverse = lax.rsqrt(row_mean(center * center) + LN_EPSILON)
    return center * inverse, inverse


def lanes(rows):
    return lax.broadcasted_iota(jnp.int32, (rows, 128), 1)


def head_lanes(lane, half):
    return lane < HD if half == 0 else lane >= HD


def three_parts(col):
    hi = col.astype(BF16).astype(F32)
    mid = (col - hi).astype(BF16).astype(F32)
    return hi, mid, col - hi - mid


def spare_columns(lane, base, values, other):
    out = other
    for i, v in reversed(list(enumerate(values))):
        out = jnp.where(lane == base + i, v, out)
    return out


def rope(v, cos, sin_a, sin_b):
    return v * cos + pltpu.roll(v, 96, 1) * sin_a + pltpu.roll(v, 32, 1) * sin_b


def rope_back(v, cos, sin_a, sin_b):
    return v * cos - pltpu.roll(v, 96, 1) * sin_a - pltpu.roll(v, 32, 1) * sin_b


def layer_kernel(inner, T, D, R, *refs):
    (
        x_in, ct_in, lens_in, pack, norm_in, cos_ref, sina_ref, sinb_ref,
        lo_out, ig_out, g_out, gn_out, sq_out,
        W, GA, xs, cc, cT, h1, h1T, h2, h2T, x1, qe, ke, ve, doe, kT,
        opair, osib, o256, wsib, zb, du, dh2, dh2r, dqT, fsend, frecv, dsend, drecv, stage,
        lens_v, nw, nl, gl1, gl2, sl1, sl2, LX, LY, ZL,
        in_s, in_r, o_s, o_r, ws_s, ws_r, d2_s, d2_r, f_s, f_r, d1_s, d1_r, out_s, out_r, n_s, n_r, e_s, e_r,
        s1s, s1r, a2s, a2r, r1s, r1r, r2s, r2r, zss, zsr, loc,
    ) = refs
    RC = 2 * R
    TB = 256
    NB = T // TB
    HALF = T // 2
    d = lax.axis_index("dp")
    z = lax.axis_index("head")
    core = d % 2
    k = d // 2
    own = z // 2
    li = z % 2
    sib = (d + 1 - 2 * core, z)
    n_dp = lax.axis_size("dp")

    def rc(src, dst, ss, rs, dev):
        return pltpu.make_async_remote_copy(
            src_ref=src, dst_ref=dst, send_sem=ss, recv_sem=rs, device_id=dev, device_id_type=MESH
        )

    column = []
    for da in range(2):
        for dz in range(4):
            if da + dz > 0:
                dd = d if da == 0 else sib[0]
                column.append((da * 4 + dz, (dd, (z + dz) % 4)))
    if inner:
        kx = k + 1 - 2 * (k % 2)
        ky = (k + 2) % 4
        kd = 3 - k
        xdev = (2 * kx + core, z)
        ydev = (2 * ky + core, z)
        ddev = (2 * kd + core, z)
        plane = [xdev, ydev, ddev]
    else:
        plane = []
    everyone = [dev for _, dev in column] + plane
    barrier = pltpu.get_barrier_semaphore()
    for dev in everyone:
        pl.semaphore_signal(barrier, inc=1, device_id=dev, device_id_type=MESH)
    pl.semaphore_wait(barrier, len(everyone))

    def in_remote(i):
        src = (x_in.at[li], ct_in.at[li], lens_in)[i]
        dst = (xs, cc, lens_v)[i]
        return rc(src, dst, in_s.at[i], in_r.at[i], sib)

    def in_local(i):
        src = (x_in.at[li], ct_in.at[li], lens_in)[i]
        dst = (xs, cc, lens_v)[i]
        return pltpu.make_async_copy(src, dst, loc.at[i])

    @pl.when(core == own)
    def _():
        for i in (2, 0, 1):
            in_remote(i).start()
            in_local(i).start()

    def piece(s):
        if isinstance(s, int):
            if s < 3:
                return 0, SUB * s
            return 1 + (s - 3) % 2, SUB * ((s - 3) // 2)
        return 1 + (s - 3) % 2, pl.multiple_of(((s - 3) // 2) * SUB, SUB)

    def rows_at(block, size):
        return pl.ds(pl.multiple_of(block * size, 16), size)

    def cols_at(e, col):
        if isinstance(e, int) and isinstance(col, int):
            return pl.ds(e * 768 + col, SUB)
        return pl.ds(pl.multiple_of(e * 768 + col, 128), SUB)

    def ag1(s, dz, a, e, dev):
        j, col = piece(s)
        src = pack.at[j, :, pl.ds(col, SUB)]
        dst = W.at[j, rows_at(2 * k + a, R), cols_at(e, col)]
        return rc(src, dst, s1s.at[s, dz], s1r.at[s, a * 2 + e], dev)

    def ag1_start(s):
        j, col = piece(s)
        for dz in range(1, 4):
            ag1(s, dz, core, li, (2 * k + own, (z + dz) % 4)).start()

        @pl.when(core == own)
        def _():
            pltpu.make_async_copy(
                pack.at[j, :, pl.ds(col, SUB)], W.at[j, rows_at(d, R), cols_at(li, col)], s1r.at[s, core * 2 + li]
            ).start()

        @pl.when(core != own)
        def _():
            ag1(s, 0, core, li, sib).start()

    def ag2(s, e, to, rows, dev, slot):
        j, col = piece(s)
        region = W.at[j, rows_at(rows, RC), cols_at(e, col)]
        return rc(region, region, a2s.at[s, e, to], a2r.at[s, e, slot], dev)

    def ag2_start(s):
        for a in range(2):
            for e in range(2):
                ag1(s, 1, a, e, sib).wait_recv()
        for e in range(2):
            ag2(s, e, 0, k, xdev, 0).start()
            ag2(s, e, 1, k, ydev, 1).start()

    def ag3_start(s):
        ag2(s, 0, 2, kx, ydev, 0).wait_recv()
        ag2(s, 0, 2, kx, ydev, 2).start()
        ag2(s, 1, 2, ky, xdev, 1).wait_recv()
        ag2(s, 1, 2, ky, xdev, 2).start()

    def ag_wait(s):
        ag2(s, 0, 1, ky, ydev, 1).wait_recv()
        ag2(s, 0, 2, kd, ydev, 2).wait_recv()
        ag2(s, 1, 0, kx, xdev, 0).wait_recv()
        ag2(s, 1, 2, kd, xdev, 2).wait_recv()

    def ag_drain(s):
        for dz in range(1, 4):
            ag1(s, dz, core, li, sib).wait_send()

        @pl.when(core != own)
        def _():
            ag1(s, 0, core, li, sib).wait_send()

        for e in range(2):
            for to in range(3):
                ag2(s, e, to, k, xdev, to).wait_send()

    if inner:
        for s in range(PIECES):
            ag1_start(s)
        nl[pl.ds(d, 1)] = norm_in[...].reshape(1, 8, 128)
        rc(nl.at[pl.ds(d, 1)], nl.at[pl.ds(d, 1)], n_s.at[0], n_r.at[0], sib).start()
        rc(nl.at[pl.ds(d, 1)], nl.at[pl.ds(sib[0], 1)], n_s.at[0], n_r.at[0], sib).wait()
        for i, dev in enumerate(plane):
            rc(nl.at[pl.ds(2 * k, 2)], nl.at[pl.ds(2 * k, 2)], n_s.at[1 + i], n_r.at[1 + i], dev).start()
    else:
        w_copy = pltpu.make_async_copy(pack, W, loc.at[3])
        w_copy.start()

    @pl.when(core == own)
    def _():
        for i in range(3):
            in_local(i).wait()

    @pl.when(core != own)
    def _():
        for i in range(3):
            in_remote(i).wait_recv()

    if inner:
        for i, kk in enumerate((kx, ky, kd)):
            rc(nl.at[pl.ds(2 * kk, 2)], nl.at[pl.ds(2 * kk, 2)], n_s.at[1 + i], n_r.at[1 + i], plane[i]).wait()
        nw[...] = jnp.zeros_like(nw)

        def place(i, carry):
            r_i = lax.broadcasted_iota(jnp.int32, (128, D), 0)
            c_i = lax.broadcasted_iota(jnp.int32, (128, D), 1)
            sel = jnp.where((r_i < R) & (c_i == r_i + i * R), 1.0, 0.0).astype(BF16)
            nw[...] += dot(nl[i].astype(BF16), sel)
            return carry

        lax.fori_loop(0, 8, place, 0)
    else:
        nw[...] = norm_in[...]

    length = lens_v[0:1, 0:1]

    def row_valid(start, rows):
        ids = (lax.broadcasted_iota(jnp.int32, (rows, 1), 0) + start).astype(F32)
        return ids < length

    def at(i, size=TB):
        return pl.ds(pl.multiple_of(i * size, size), size)

    def norm_one(i, carry):
        rows = at(i)
        n, _ = normalize(xs[rows, :].astype(F32))
        h = (n * nw[0:1, :] + nw[1:2, :]).astype(BF16)
        h1[rows, :] = h
        h1T[:, rows] = h.T
        c = jnp.where(row_valid(i * TB, TB), cc[rows, :].astype(F32), 0.0).astype(BF16)
        cc[rows, :] = c
        cT[:, rows] = c.T
        return carry

    lax.fori_loop(0, NB, norm_one, 0)

    if inner:
        ag2_start(0)
        ag2_start(1)
        ag3_start(0)
        ag2_start(2)
        ag3_start(1)
        ag_wait(0)
        ag3_start(2)
        ag_wait(1)
    else:
        w_copy.wait()

    lane = lanes(TB)
    low = lane < HD

    def make_pair(p):
        def block(i, carry):
            rows = at(i)
            h = h1[rows, :]
            cos, sa, sb = cos_ref[rows, :], sina_ref[rows, :], sinb_ref[rows, :]
            if p < 2:
                raw = dot(h, W[0, :, p * 768 : p * 768 + 384])
                q, kk, v = raw[:, :128], raw[:, 128:256], raw[:, 256:]
                q = rope(q, cos, sa, sb)
                kk = rope(kk, cos, sa, sb)
            else:
                r0 = dot(h, W[0, :, 384:640])
                r1 = dot(h, W[0, :, 768 + 384 : 768 + 640])
                ra = rope(r0[:, :128], cos, sa, sb)
                rb = rope(r1[:, :128], cos, sa, sb)
                q = jnp.where(low, ra, pltpu.roll(rb, 64, 1))
                kk = jnp.where(low, pltpu.roll(ra, 64, 1), rb)
                v = jnp.where(low, r0[:, 128:], pltpu.roll(r1[:, 128:], 64, 1))
            q = q * HD**-0.5
            bias = jnp.where(row_valid(i * TB, TB), 0.0, MASK_FILL)
            kT[p, :, rows] = kk.astype(BF16).T
            for half in range(2):
                mine = head_lanes(lane, half)
                base = HD - HD * half
                hh = 2 * p + half
                qe[hh, rows, :] = jnp.where(mine, q, jnp.where(lane == base, 1.0, 0.0)).astype(BF16)
                ke[hh, rows, :] = jnp.where(mine, kk, jnp.where(lane == base, bias, 1.0)).astype(BF16)
                ve[hh, rows, :] = jnp.where(mine, v, 1.0).astype(BF16)
            return carry

        lax.fori_loop(0, NB, block, 0)

    def attend(p, i):
        rows = at(i)
        outs = []
        for half in range(2):
            hh = 2 * p + half
            mine = head_lanes(lane, half)
            base = HD - HD * half
            q = qe[hh, rows, :]
            s = dot_t(q, ke[hh])
            top = jnp.max(s, axis=-1, keepdims=True)
            ex = jnp.exp(s - top).astype(BF16)
            o = dot(ex, ve[hh])
            total = o[:, base : base + 1]
            outs.append(o * (1.0 / total))
            hi, mid, lo = three_parts(top + jnp.log(total))
            extra = spare_columns(lane, base, (1.0, -hi, -mid, -lo), 0.0)
            qe[hh, rows, :] = jnp.where(mine, q.astype(F32), extra).astype(BF16)
        opair[p, rows, :] = jnp.where(low, outs[0], outs[1]).astype(BF16)

    def o_copy(p):
        return rc(opair.at[p], osib.at[p], o_s.at[p], o_r.at[p], sib)

    def ws_copy(e):
        return rc(W.at[0, :, pl.ds(e * 768 + 512, 256)], wsib.at[e], ws_s.at[e], ws_r.at[e], sib)

    for p in range(3):
        if inner and p == 2:
            ag_wait(2)
        make_pair(p)

        def attend_two(i, carry, p=p):
            s = 3 + 2 * p + i
            if inner:
                ag2_start(s)
            attend(p, 2 * i)
            if inner:
                ag3_start(s)
            attend(p, 2 * i + 1)
            return carry

        lax.fori_loop(0, NB // 2, attend_two, 0)
        o_copy(p).start()
        if p == 2:
            for e in range(2):
                ws_copy(e).start()

    def wide_o(pairs, e, rows):
        single = pairs[2, rows, :].astype(F32)
        if e == 0:
            single = pltpu.roll(single, 64, 1)
        single = jnp.where(low, 0.0, single).astype(BF16)
        return jnp.concatenate([single, pairs[e, rows, :]], axis=1)

    for p in range(3):
        o_copy(p).wait()
    for e in range(2):
        ws_copy(e).wait()

    def project_out(i, carry):
        rows = at(i)
        acc = xs[rows, :].astype(F32)
        for e in range(2):
            mine = wide_o(opair, e, rows)
            o256[e, rows, :] = mine
            acc = acc + dot_t(mine, W[0, :, e * 768 + 512 : e * 768 + 768])
            acc = acc + dot_t(wide_o(osib, e, rows), wsib[e])
        x1[rows, :] = acc
        n, _ = normalize(acc)
        h = (n * nw[2:3, :] + nw[3:4, :]).astype(BF16)
        h2[rows, :] = h
        h2T[:, rows] = h.T
        return carry

    lax.fori_loop(0, NB, project_out, 0)

    for i3 in range(3):
        if inner:
            ag_wait(3 + 2 * i3)
            ag_wait(4 + 2 * i3)

        def hidden(i, carry, i3=i3):
            rows = at(i % NB)
            cols = cols_at(i // NB, SUB * i3)
            u = dot(h2[rows, :], W[1, :, cols])
            dz = dot(cc[rows, :], W[2, :, cols])
            cumulative = 0.5 * (1.0 + lax.erf(u * INV_ROOT_TWO))
            slope = cumulative + u * jnp.exp(-0.5 * u * u) * INV_ROOT_TWO_PI
            zb[rows, cols] = (u * cumulative).astype(BF16)
            du[rows, cols] = (dz * slope).astype(BF16)
            return carry

        lax.fori_loop(0, 2 * NB, hidden, 0)

    def d2_copy(i):
        return rc(h1.at[at(i), :], dh2r.at[at(i), :], d2_s.at[i], d2_r.at[i], sib)

    def back_two(i, carry):
        rows = at(i)
        v = dot_t(du[rows, :], W[1])
        dh2[rows, :] = v
        h1[rows, :] = v.astype(BF16)
        d2_copy(i).start()
        return carry

    lax.fori_loop(0, NB, back_two, 0)

    other = 1 - core

    def half_rows(which, i):
        return pl.ds(pl.multiple_of(which * HALF + i * TB, TB), TB)

    def f_copy():
        return rc(fsend, frecv, f_s.at[0], f_r.at[0], sib)

    def ffn_other(i, carry):
        fsend[at(i), :] = dot_t(zb[half_rows(other, i), :], W[2]).astype(BF16)
        return carry

    lax.fori_loop(0, NB // 2, ffn_other, 0)
    f_copy().start()

    def grad(s):
        return GA if isinstance(s, int) and s < 3 else W.at[piece(s)[0]]

    def rs1(s, e, b, rows, dev):
        src = grad(s).at[rows_at(rows, RC), cols_at(e, piece(s)[1])]
        return rc(src, LX.at[s, e, b], r1s.at[s, e, b], r1r.at[s, e, b], dev)

    def rs1_start(s):
        rs1(s, 0, 1, kd, xdev).start()
        rs1(s, 1, 1, kd, ydev).start()
        rs1(s, 0, 0, kx, xdev).start()
        rs1(s, 1, 0, ky, ydev).start()

    def rs2(s, e, dev):
        return rc(LX.at[s, e, 1], LY.at[s, e], r2s.at[s, e], r2r.at[s, e], dev)

    def rs2_start(s):
        for e, near, far, dev in ((0, kx, ky, ydev), (1, ky, kx, xdev)):
            rs1(s, e, 1, far, dev).wait_recv()
            mine = grad(s)[rows_at(far, RC), cols_at(e, piece(s)[1])].astype(F32)
            LX[s, e, 1] = (LX[s, e, 1].astype(F32) + mine).astype(BF16)
            rs2(s, e, dev).start()

    def rs3(s, e, a, dev):
        return rc(LX.at[s, e, 0, pl.ds(a * R, R)], ZL.at[s, z], zss.at[s, e * 2 + a], zsr.at[s, z], dev)

    def rs3_start(s):
        for e in range(2):
            rs1(s, e, 0, k, xdev).wait_recv()
            rs2(s, e, ydev).wait_recv()
            mine = grad(s)[rows_at(k, RC), cols_at(e, piece(s)[1])].astype(F32)
            LX[s, e, 0] = (LX[s, e, 0].astype(F32) + LY[s, e].astype(F32) + mine).astype(BF16)
            zt = 2 * core + e
            for a in range(2):
                here = (core == a) & (zt == z)

                @pl.when(here)
                def _(a=a, e=e):
                    pltpu.make_async_copy(LX.at[s, e, 0, pl.ds(a * R, R)], ZL.at[s, z], zsr.at[s, z]).start()

                @pl.when(jnp.logical_not(here))
                def _(a=a, e=e, zt=zt):
                    rs3(s, e, a, (2 * k + a, zt)).start()

    def rs4(s):
        j, col = piece(s)
        total = jnp.zeros((R, SUB), F32)
        for zz in range(4):
            rc(LX.at[s, 0, 0, pl.ds(0, R)], ZL.at[s, zz], zss.at[s, 0], zsr.at[s, zz], sib).wait_recv()
            total = total + ZL[s, zz].astype(F32)
        g_out[j, :, pl.ds(col, SUB)] = total
        return total

    def rs_drain(s):
        for e in range(2):
            for b in range(2):
                rs1(s, e, b, k, xdev).wait_send()
            rs2(s, e, ydev).wait_send()
            zt = 2 * core + e
            for a in range(2):

                @pl.when(jnp.logical_not((core == a) & (zt == z)))
                def _(a=a, e=e):
                    rs3(s, e, a, sib).wait_send()

    def out_copy(ref, which, qi, slot):
        src = stage.at[which, pl.ds(qi * (T // 4), T // 4), :]
        return rc(src, ref.at[li], out_s.at[which, qi], out_r.at[which, slot], (2 * k + own, 2 * core + qi))

    def out_start(ref, which):
        for qi in range(2):
            here = (core == own) & (li == qi)

            @pl.when(here)
            def _(qi=qi):
                src = stage.at[which, pl.ds(qi * (T // 4), T // 4), :]
                pltpu.make_async_copy(src, ref.at[li], out_r.at[which, li]).start()

            @pl.when(jnp.logical_not(here))
            def _(qi=qi):
                out_copy(ref, which, qi, li).start()

    def out_wait(ref, which):
        for slot in range(2):
            src = stage.at[which, pl.ds(0, T // 4), :]
            rc(src, ref.at[slot], out_s.at[which, 0], out_r.at[which, slot], sib).wait_recv()
        for qi in range(2):

            @pl.when(jnp.logical_not((core == own) & (li == qi)))
            def _(qi=qi):
                out_copy(ref, which, qi, 0).wait_send()

    if inner:

        def drain(s, carry):
            ag_drain(s)
            return carry

        for s in range(3):
            ag_drain(s)
        lax.fori_loop(3, PIECES, drain, 0)

    def grad_up(i, carry):
        for e in range(2):
            cols = cols_at(e, pl.multiple_of(i * SUB, SUB))
            W[1, :, cols] = dot(h2T[...], du[:, cols]).astype(BF16)
        if inner:
            rs1_start(3 + 2 * i)
        return carry

    lax.fori_loop(0, 3, grad_up, 0)

    f_copy().wait()

    def ffn_final(i, carry):
        rows = half_rows(core, i)
        y = x1[rows, :] + dot_t(zb[rows, :], W[2]) + frecv[at(i), :].astype(F32)
        stage[0, at(i), :] = y.astype(BF16)
        return carry

    lax.fori_loop(0, NB // 2, ffn_final, 0)
    out_start(lo_out, 0)

    def grad_down(i, carry):
        for e in range(2):
            cols = cols_at(e, pl.multiple_of(i * SUB, SUB))
            W[2, :, cols] = dot(cT[...], zb[:, cols]).astype(BF16)
        if inner:
            rs1_start(4 + 2 * i)
        return carry

    lax.fori_loop(0, 3, grad_down, 0)

    gn_out[...] = jnp.zeros_like(gn_out)

    def norm_back_two(i, carry):
        rows = at(i)
        d2_copy(i).wait()
        e2 = dh2[rows, :] + dh2r[rows, :].astype(F32)
        n, r = normalize(x1[rows, :])
        m = e2 * nw[2:3, :]
        dx = cc[rows, :].astype(F32) + r * (m - row_mean(m) - n * row_mean(m * n))
        dh2[rows, :] = dx
        low_dx = dx.astype(BF16)
        h2[rows, :] = low_dx
        h2T[:, rows] = low_dx.T
        count = jnp.where(i // (NB // 2) == core, 1.0, 0.0)
        gn_out[2:3, :] += count * jnp.sum(e2 * n, axis=0, keepdims=True)
        gn_out[3:4, :] += count * jnp.sum(e2, axis=0, keepdims=True)
        return carry

    lax.fori_loop(0, NB, norm_back_two, 0)
    da, daT = h2, h2T

    def do_block(i, carry):
        rows = at(i)
        parts = [dot(da[rows, :], W[0, :, e * 768 + 512 : e * 768 + 768]) for e in range(2)]
        pairs = [parts[0][:, 128:], parts[1][:, 128:], jnp.where(low, pltpu.roll(parts[0][:, :128], 64, 1), parts[1][:, :128])]
        for p in range(3):
            g = pairs[p].astype(BF16).astype(F32)
            prod = g * opair[p, rows, :].astype(F32)
            for half in range(2):
                mine = head_lanes(lane, half)
                base = HD - HD * half
                delta = jnp.sum(jnp.where(mine, prod, 0.0), axis=-1, keepdims=True)
                hi, mid, lo = three_parts(delta)
                extra = spare_columns(lane, base + 1, (-hi, -mid, -lo), 0.0)
                doe[2 * p + half, rows, :] = jnp.where(mine, g, extra).astype(BF16)
        return carry

    lax.fori_loop(0, NB, do_block, 0)

    def back_keys(p, i):
        rows = at(i)
        cos, sa, sb = cos_ref[rows, :], sina_ref[rows, :], sinb_ref[rows, :]
        dks, dvs = [], []
        for half in range(2):
            hh = 2 * p + half
            sT = dot_t(ke[hh, rows, :], qe[hh])
            pT = jnp.exp(sT)
            dpT = dot_t(ve[hh, rows, :], doe[hh])
            dsT = (pT * dpT).astype(BF16)
            dvs.append(dot(pT.astype(BF16), doe[hh]))
            dks.append(dot(dsT, qe[hh]))
            part = dot(kT[p, half * HD : half * HD + HD, rows], dsT)
            dqT[half * HD : half * HD + HD, :] += part
        dk = rope_back(jnp.where(low, dks[0], dks[1]), cos, sa, sb)
        dv = jnp.where(low, dvs[0], dvs[1])
        put_draw(p, rows, None, dk, dv)

    def put_draw(p, rows, dq, dk, dv):
        if p < 2:
            for i, v in enumerate((dq, dk, dv)):
                if v is not None:
                    du[rows, p * 768 + 128 * i : p * 768 + 128 * i + 128] = v.astype(BF16)
            return
        if dk is not None:
            du[rows, 640:768] = dk.astype(BF16)
            du[rows, 512:640] = jnp.where(low, dv, 0.0).astype(BF16)
            du[rows, 768 + 512 : 768 + 640] = jnp.where(low, pltpu.roll(dv, 64, 1), 0.0).astype(BF16)
        if dq is not None:
            dk = du[rows, 640:768].astype(F32)
            du[rows, 384:512] = jnp.where(low, dq, pltpu.roll(dk, 64, 1)).astype(BF16)
            du[rows, 768 + 384 : 768 + 512] = jnp.where(low, pltpu.roll(dq, 64, 1), dk).astype(BF16)

    def put_queries(p):
        def block(i, carry):
            rows = at(i)
            cos, sa, sb = cos_ref[rows, :], sina_ref[rows, :], sinb_ref[rows, :]
            dq = dqT[:, rows].T * HD**-0.5
            put_draw(p, rows, rope_back(dq, cos, sa, sb), None, None)
            return carry

        lax.fori_loop(0, NB, block, 0)

    for step, p in enumerate((2, 0, 1)):
        dqT[...] = jnp.zeros_like(dqT)

        def back_step(i, carry, p=p, step=step):
            back_keys(p, 2 * i)
            if inner:
                rs2_start(3 + 2 * step + i)
            back_keys(p, 2 * i + 1)
            if inner:
                rs3_start(3 + 2 * step + i)
            return carry

        lax.fori_loop(0, NB // 2, back_step, 0)
        put_queries(p)
        if p == 2:
            for e in range(2):
                b = e * 768
                GA[:, b + 384 : b + 512] = dot(h1T[...], du[:, b + 384 : b + 512]).astype(BF16)
                wide = dot(daT[...], o256[e])
                GA[:, b + 640 : b + 768] = wide[:, 128:].astype(BF16)
                GA[:, b + 512 : b + 640] = (wide[:, :128] + dot(h1T[...], du[:, b + 512 : b + 640])).astype(BF16)
            if inner:
                rs1_start(2)
        else:
            b = p * 768
            GA[:, b : b + 384] = dot(h1T[...], du[:, b : b + 384]).astype(BF16)
            if inner and p == 0:
                rs2_start(2)
    if inner:
        rs1_start(0)
        rs1_start(1)
        rs3_start(2)

    def back_one(rows):
        return dot_t(du[rows, 0:640], W[0, :, 0:640]) + dot_t(du[rows, 768 : 768 + 640], W[0, :, 768 : 768 + 640])

    def d1_copy():
        return rc(dsend, drecv, d1_s.at[0], d1_r.at[0], sib)

    def one_other(i, carry):
        dsend[at(i), :] = back_one(half_rows(other, i)).astype(BF16)
        return carry

    lax.fori_loop(0, NB // 2, one_other, 0)
    d1_copy().start()

    def one_mine(i, carry):
        rows = half_rows(core, i)
        x1[rows, :] = back_one(rows)
        return carry

    lax.fori_loop(0, NB // 2, one_mine, 0)
    if inner:
        rs2_start(0)
        rs2_start(1)
    d1_copy().wait()

    def norm_back_one(i, carry):
        rows = half_rows(core, i)
        e1 = x1[rows, :] + drecv[at(i), :].astype(F32)
        n, r = normalize(xs[rows, :].astype(F32))
        m = e1 * nw[0:1, :]
        dx = dh2[rows, :] + r * (m - row_mean(m) - n * row_mean(m * n))
        stage[1, at(i), :] = dx.astype(BF16)
        gn_out[0:1, :] += jnp.sum(e1 * n, axis=0, keepdims=True)
        gn_out[1:2, :] += jnp.sum(e1, axis=0, keepdims=True)
        return carry

    lax.fori_loop(0, NB // 2, norm_back_one, 0)
    out_start(ig_out, 1)

    def sum_everywhere(ref, l1, l2, which):
        l1[0] = ref[...]
        for slot, dev in column:
            rc(l1.at[0], l1.at[slot], e_s.at[which, slot], e_r.at[which, slot], dev).start()
        total = l1[0]
        for slot, dev in column:
            rc(l1.at[0], l1.at[slot], e_s.at[which, slot], e_r.at[which, slot], dev).wait()
            total = total + l1[slot]
        l2[0] = total
        for i, dev in enumerate(plane):
            rc(l2.at[0], l2.at[1 + i], e_s.at[which, 8 + i], e_r.at[which, 8 + i], dev).start()
        for i, dev in enumerate(plane):
            rc(l2.at[0], l2.at[1 + i], e_s.at[which, 8 + i], e_r.at[which, 8 + i], dev).wait()
            total = total + l2[1 + i]
        ref[...] = total

    if inner:
        rs3_start(0)
        rs3_start(1)
        sum_everywhere(gn_out, gl1, gl2, 0)
        squares = jnp.zeros((R, SUB), F32)

        def last(s, acc):
            g = rs4(s)
            return acc + g * g

        squares = lax.fori_loop(3, PIECES, last, squares)
        for s in (2, 0, 1):
            squares = last(s, squares)
        total = jnp.sum(squares, axis=0, keepdims=True)
        total = total[:, :128] + total[:, 128:]
        sq_out[...] = jnp.where(lax.broadcasted_iota(jnp.int32, (8, 128), 0) == 0, total, 0.0)
        sum_everywhere(sq_out, sl1, sl2, 1)

        def drain_rs(s, carry):
            rs_drain(s)
            return carry

        for s in range(3):
            rs_drain(s)
        lax.fori_loop(3, PIECES, drain_rs, 0)
    else:
        sq_out[...] = jnp.zeros_like(sq_out)
        for j in range(3):
            g_copy = pltpu.make_async_copy(GA if j == 0 else W.at[j], g_out.at[j], loc.at[3 + j])
            g_copy.start()
            g_copy.wait()
    out_wait(lo_out, 0)
    out_wait(ig_out, 1)

    @pl.when(core == own)
    def _():
        for i in range(3):
            in_remote(i).wait_send()


def rope_tables(length):
    places = np.arange(length, dtype=np.float32)
    rates = (ROPE_BASE ** (-(np.arange(HD // 2, dtype=np.float32) * 2.0 / HD))).astype(np.float32)
    angles = places[:, None] * rates[None, :]
    cos = np.tile(np.cos(angles), (1, 4)).astype(np.float32)
    sin = np.tile(np.sin(angles), (1, 4)).astype(np.float32)
    first = (np.arange(128) % HD < HD // 2)[None, :]
    return cos, np.where(first, -sin, 0.0).astype(np.float32), np.where(first, 0.0, sin).astype(np.float32)


def adam_update(master, first_old, second_old, gradient, clip_factor, step_rate, decay_rate):
    clipped = gradient * clip_factor
    first_new = BETA_FIRST * first_old + (1.0 - BETA_FIRST) * clipped
    second_new = BETA_SECOND * second_old + (1.0 - BETA_SECOND) * clipped * clipped
    fix_first = 1.0 - BETA_FIRST**STEP
    fix_second = 1.0 - BETA_SECOND**STEP
    normalized = first_new / fix_first / (jnp.sqrt(second_new / fix_second) + ADAM_EPSILON)
    master_new = master - step_rate * (normalized + decay_rate * master)
    return (master_new, first_new, second_new, master_new.astype(BF16))


def per_device(
    inputs,
    cotangent,
    lengths,
    proj_master,
    proj_first,
    proj_second,
    out_master,
    out_first,
    out_second,
    up_master,
    up_first,
    up_second,
    down_master,
    down_first,
    down_second,
    norm_master,
    norm_first,
    norm_second,
):
    _, T, D = inputs.shape
    R = proj_master.shape[1]
    n_dp = lax.axis_size("dp")
    inner = n_dp == 8
    d = lax.axis_index("dp")
    z = lax.axis_index("head")
    core, own, li = d % 2, z // 2, z % 2
    out_t = out_master.T
    attn = jnp.concatenate(
        [proj_master[0, :, :128], proj_master[1, :, :128], proj_master[2, :, :128]]
        + [proj_master[0, :, 128:], proj_master[1, :, 128:], proj_master[2, :, 128:]]
        + [out_t[:, 128:], out_t[:, :128]],
        axis=1,
    )
    pack = jnp.stack([attn, up_master, down_master.T]).astype(BF16)
    norm_low = norm_master.astype(BF16).astype(F32)
    lens = jnp.broadcast_to(lax.dynamic_index_in_dim(lengths, li, 0).astype(F32).reshape(1, 1), (8, 128))
    if inner:
        norm_in = jnp.pad(norm_low, ((0, 4), (0, 128 - R)))
    else:
        norm_in = jnp.pad(lax.all_gather(norm_master, "dp", axis=1, tiled=True), ((0, 4), (0, 0)))
        norm_in = norm_in.astype(BF16).astype(F32)
        full = lax.all_gather(pack, "dp", axis=1, tiled=True)
        every = lax.all_gather(full, "head", axis=0)
        pair = lax.dynamic_slice_in_dim(every, 2 * core, 2, 0)
        pack = jnp.concatenate([pair[0], pair[1]], axis=2)
    cos, sin_a, sin_b = rope_tables(T)

    hbm = pl.BlockSpec(memory_space=pl.ANY)
    vmem = pl.BlockSpec(memory_space=pltpu.VMEM)
    dma = pltpu.SemaphoreType.DMA
    quarter = T // 4
    g_shape = (3, R, 768) if inner else (3, D, 1536)
    out_shape = (
        jax.ShapeDtypeStruct((2, quarter, D), BF16),
        jax.ShapeDtypeStruct((2, quarter, D), BF16),
        jax.ShapeDtypeStruct(g_shape, F32 if inner else BF16),
        jax.ShapeDtypeStruct((8, D), F32),
        jax.ShapeDtypeStruct((8, 128), F32),
    )
    HALF = T // 2
    NB = T // 256
    bf = lambda *s: pltpu.VMEM(s, BF16)
    ff = lambda *s: pltpu.VMEM(s, F32)
    RC = 2 * R
    pieces = PIECES if inner else 1
    lx_rows = RC if inner else 16
    zl_rows = R if inner else 16
    scratch = [
        bf(3, D, 1536), bf(D, 1536), bf(T, D), bf(T, D), bf(D, T), bf(T, D), bf(D, T), bf(T, D), bf(D, T), ff(T, D),
        bf(6, T, 128), bf(6, T, 128), bf(6, T, 128), bf(6, T, 128), bf(3, 128, T),
        bf(3, T, 128), bf(3, T, 128), bf(2, T, 256), bf(2, D, 256), bf(T, 1536), bf(T, 1536), ff(T, D), bf(T, D), ff(128, T),
        bf(HALF, D), bf(HALF, D), bf(HALF, D), bf(HALF, D), bf(2, HALF, D),
        ff(8, 128), ff(8, D), ff(8, 8, 128), ff(8, 8, D), ff(4, 8, D), ff(8, 8, 128), ff(4, 8, 128),
        bf(pieces, 2, 2, lx_rows, SUB), bf(pieces, 2, lx_rows, SUB), bf(pieces, 4, zl_rows, SUB),
        dma((3,)), dma((3,)), dma((3,)), dma((3,)), dma((2,)), dma((2,)), dma((NB,)), dma((NB,)),
        dma((1,)), dma((1,)), dma((1,)), dma((1,)), dma((2, 2)), dma((2, 2)), dma((4,)), dma((4,)), dma((2, 11)), dma((2, 11)),
        dma((pieces, 4)), dma((pieces, 4)), dma((pieces, 2, 3)), dma((pieces, 2, 3)),
        dma((pieces, 2, 2)), dma((pieces, 2, 2)), dma((pieces, 2)), dma((pieces, 2)), dma((pieces, 4)), dma((pieces, 4)),
        dma((6,)),
    ]
    layer_out, input_grad, grads, gn, sq = pl.pallas_call(
        functools.partial(layer_kernel, inner, T, D, R),
        out_shape=out_shape,
        in_specs=[hbm, hbm, vmem, vmem if inner else hbm, vmem, vmem, vmem, vmem],
        out_specs=(hbm, hbm, vmem if inner else hbm, vmem, vmem),
        scratch_shapes=scratch,
        compiler_params=pltpu.CompilerParams(
            collective_id=0, has_side_effects=True, vmem_limit_bytes=63 * 2**20
        ),
        name="layer",
    )(inputs, cotangent, lens, pack, norm_in, jnp.asarray(cos), jnp.asarray(sin_a), jnp.asarray(sin_b))

    if inner:
        gn = gn[:4]
        squares = jnp.sum(sq)
    else:
        spread = jnp.stack([grads[:, :, :768], grads[:, :, 768:]]).astype(F32)
        empty = jnp.zeros((4,) + spread.shape[1:], F32)
        spread = lax.dynamic_update_slice_in_dim(empty, spread, 2 * core, 0)
        mine = lax.psum_scatter(spread, "head", scatter_dimension=0, tiled=False)
        grads = lax.psum_scatter(mine, "dp", scatter_dimension=1, tiled=True)
        gn = lax.psum(gn[:4], ("dp", "head"))
        squares = lax.psum(jnp.sum(grads * grads), ("dp", "head"))
    squares = squares + jnp.sum(gn * gn)
    gn_mine = lax.dynamic_slice_in_dim(gn, d * R, R, 1)
    a = grads[0]
    g_proj = jnp.stack([jnp.concatenate([a[:, 128 * j : 128 * j + 128], a[:, 384 + 64 * j : 448 + 64 * j]], axis=1) for j in range(3)])
    g_out = jnp.concatenate([a[:, 640:], a[:, 576:640]], axis=1).T
    g_up = grads[1]
    g_down = grads[2].T
    grad_norm = jnp.sqrt(squares)
    clip_factor = jnp.minimum(1.0, CLIP_LIMIT / (grad_norm + 1e-06))
    proj_up = adam_update(proj_master, proj_first, proj_second, g_proj, clip_factor, RATE_MATRIX, WEIGHT_DECAY)
    out_up = adam_update(out_master, out_first, out_second, g_out, clip_factor, RATE_MATRIX, WEIGHT_DECAY)
    up_up = adam_update(up_master, up_first, up_second, g_up, clip_factor, RATE_MATRIX, WEIGHT_DECAY)
    down_up = adam_update(down_master, down_first, down_second, g_down, clip_factor, RATE_MATRIX, WEIGHT_DECAY)
    norm_up = adam_update(norm_master, norm_first, norm_second, gn_mine, clip_factor, RATE_NORM, 0.0)
    return (layer_out, input_grad, grad_norm) + proj_up + out_up + up_up + down_up + norm_up


def solution(mesh):
    proj, wide, tall, norms = P(None, "dp", "head"), P("dp", "head"), P("head", "dp"), P(None, "dp")
    tokens = P("dp", None, None)
    placed = (tokens, tokens, P("dp")) + (proj,) * 3 + (tall,) * 3 + (wide,) * 3 + (tall,) * 3 + (norms,) * 3
    quarters = P("dp", "head", None)
    return jax.shard_map(
        per_device,
        mesh=mesh,
        in_specs=placed,
        out_specs=(quarters, quarters, P()) + (proj,) * 4 + (tall,) * 4 + (wide,) * 4 + (tall,) * 4 + (norms,) * 4,
        check_vma=False,
    )
```

```python
import functools

import jax
import jax.numpy as jnp
import numpy as np
from jax import lax
from jax.experimental import pallas as pl
from jax.experimental.pallas import tpu as pltpu
from jax.sharding import PartitionSpec as P

HD = 64
STEP = 5
LN_EPSILON = 1e-05
MASK_FILL = -1e30
ROPE_BASE = 10000.0
CLIP_LIMIT = 1.0
BETA_FIRST = 0.9
BETA_SECOND = 0.95
ADAM_EPSILON = 1e-08
WEIGHT_DECAY = 0.1
RATE_MATRIX = 0.03
RATE_NORM = 0.3
INV_ROOT_TWO = 0.7071067811865476
INV_ROOT_TWO_PI = 0.3989422804014327

F32 = jnp.float32
BF16 = jnp.bfloat16
MESH = pl.DeviceIdType.MESH
SUB = 256
PIECES = 9


def dot(a, b):
    return lax.dot_general(a, b, (((1,), (0,)), ((), ())), preferred_element_type=F32)


def dot_t(a, b):
    return lax.dot_general(a, b, (((1,), (1,)), ((), ())), preferred_element_type=F32)


def row_mean(v):
    return jnp.mean(v, axis=-1, keepdims=True)


def normalize(v):
    center = v - row_mean(v)
    inverse = lax.rsqrt(row_mean(center * center) + LN_EPSILON)
    return center * inverse, inverse


def lanes(rows):
    return lax.broadcasted_iota(jnp.int32, (rows, 128), 1)


def head_lanes(lane, half):
    return lane < HD if half == 0 else lane >= HD


def three_parts(col):
    hi = col.astype(BF16).astype(F32)
    mid = (col - hi).astype(BF16).astype(F32)
    return hi, mid, col - hi - mid


def spare_columns(lane, base, values, other):
    out = other
    for i, v in reversed(list(enumerate(values))):
        out = jnp.where(lane == base + i, v, out)
    return out


def turned(v, first):
    return jnp.where(first, pltpu.roll(v, 96, 1), pltpu.roll(v, 32, 1))


def rope(v, cos, sin, first):
    return v * cos + turned(v, first) * sin


def rope_back(v, cos, sin, first):
    return v * cos - turned(v, first) * sin


def run(name, count, body):
    with jax.named_scope(name):
        lax.fori_loop(0, count, body, 0)


def layer_kernel(inner, T, D, R, *refs):
    (
        x_in, ct_in, lens_in, tables_in, norm_in, *rest
    ) = refs
    if inner:
        *masters_in, lo_out, ig_out, g_out, small_out = rest[:8]
        rest = rest[8:]
    else:
        w_in, lo_out, ig_out, g_out, small_out = rest[:5]
        rest = rest[5:]
    (
        W, GA, xs, cc, cT, h1, h1T, h2, h2T, x1, qe, ke, ve, doe, kT,
        opair, osib, wsib, zb, du, dh2, dh2r, dqT, facc, fsend, frecv, drecv, stage,
        lens_s, lens_v, pack, nw, nl, gl1, gl2, sl1, sl2, LX, LY, ZL,
        in_s, in_r, o_s, o_r, ws_s, ws_r, d2_s, d2_r, f_s, f_r, d1_s, d1_r, out_s, out_r, n_s, n_r, e_s, e_r,
        s1s, s1r, a2s, a2r, r1s, r1r, r2s, r2r, zss, zsr, loc,
        tables, norm_m, proj_m, out_m, up_m, down_m, gn_out, sq_out, gbuf, squares_ref,
    ) = rest
    RC = 2 * R
    TB = 256
    NB = T // TB
    HALF = T // 2
    d = lax.axis_index("dp")
    z = lax.axis_index("head")
    core = d % 2
    k = d // 2
    own = z // 2
    li = z % 2
    sib = (d + 1 - 2 * core, z)
    master_copies = []
    if inner:
        for i, (src, dst) in enumerate(zip(masters_in, (proj_m, out_m, up_m, down_m))):
            master_copies.append(pltpu.make_async_copy(src, dst, loc.at[4 + i]))
    norm_copy = pltpu.make_async_copy(norm_in, norm_m, loc.at[8])
    table_copy = pltpu.make_async_copy(tables_in, tables, loc.at[9])
    for copy in master_copies + [norm_copy, table_copy]:
        copy.start()
    cos_ref, sin_ref = tables.at[0], tables.at[1]
    lens_s[...] = jnp.full((8, 128), lens_in[li].astype(F32))

    def rc(src, dst, ss, rs, dev):
        return pltpu.make_async_remote_copy(
            src_ref=src, dst_ref=dst, send_sem=ss, recv_sem=rs, device_id=dev, device_id_type=MESH
        )

    column = []
    for da in range(2):
        for dz in range(4):
            if da + dz > 0:
                dd = d if da == 0 else sib[0]
                column.append((da * 4 + dz, (dd, (z + dz) % 4)))
    if inner:
        kx = k + 1 - 2 * (k % 2)
        ky = (k + 2) % 4
        kd = 3 - k
        xdev = (2 * kx + core, z)
        ydev = (2 * ky + core, z)
        ddev = (2 * kd + core, z)
        plane = [xdev, ydev, ddev]
    else:
        plane = []
    everyone = [dev for _, dev in column] + plane
    barrier = pltpu.get_barrier_semaphore()
    for dev in everyone:
        pl.semaphore_signal(barrier, inc=1, device_id=dev, device_id_type=MESH)
    pl.semaphore_wait(barrier, len(everyone))

    def in_remote(i):
        src = (x_in.at[li], ct_in.at[li], lens_s)[i]
        dst = (xs, cc, lens_v)[i]
        return rc(src, dst, in_s.at[i], in_r.at[i], sib)

    def in_local(i):
        src = (x_in.at[li], ct_in.at[li], lens_s)[i]
        dst = (xs, cc, lens_v)[i]
        return pltpu.make_async_copy(src, dst, loc.at[i])

    @pl.when(core == own)
    def _():
        for i in (2, 0, 1):
            in_remote(i).start()
            in_local(i).start()

    def piece(s):
        if isinstance(s, int):
            if s < 3:
                return 0, SUB * s
            return 1 + (s - 3) % 2, SUB * ((s - 3) // 2)
        return 1 + (s - 3) % 2, pl.multiple_of(((s - 3) // 2) * SUB, SUB)

    def rows_at(block, size):
        return pl.ds(pl.multiple_of(block * size, 16), size)

    def cols_at(e, col):
        if isinstance(e, int) and isinstance(col, int):
            return pl.ds(e * 768 + col, SUB)
        return pl.ds(pl.multiple_of(e * 768 + col, 128), SUB)

    def ag1(s, dz, a, e, dev):
        j, col = piece(s)
        src = pack.at[j, :, pl.ds(col, SUB)]
        dst = W.at[j, rows_at(2 * k + a, R), cols_at(e, col)]
        return rc(src, dst, s1s.at[s, dz], s1r.at[s, a * 2 + e], dev)

    def ag1_start(s):
        j, col = piece(s)
        for dz in range(1, 4):
            ag1(s, dz, core, li, (2 * k + own, (z + dz) % 4)).start()

        @pl.when(core == own)
        def _():
            pltpu.make_async_copy(
                pack.at[j, :, pl.ds(col, SUB)], W.at[j, rows_at(d, R), cols_at(li, col)], s1r.at[s, core * 2 + li]
            ).start()

        @pl.when(core != own)
        def _():
            ag1(s, 0, core, li, sib).start()

    def ag2(s, e, to, rows, dev, slot):
        j, col = piece(s)
        region = W.at[j, rows_at(rows, RC), cols_at(e, col)]
        return rc(region, region, a2s.at[s, e, to], a2r.at[s, e, slot], dev)

    def ag2_start(s):
        for a in range(2):
            for e in range(2):
                ag1(s, 1, a, e, sib).wait_recv()
        for e in range(2):
            ag2(s, e, 0, k, xdev, 0).start()
            ag2(s, e, 1, k, ydev, 1).start()

    def ag3_start(s):
        ag2(s, 0, 2, kx, ydev, 0).wait_recv()
        ag2(s, 0, 2, kx, ydev, 2).start()
        ag2(s, 1, 2, ky, xdev, 1).wait_recv()
        ag2(s, 1, 2, ky, xdev, 2).start()

    def ag_wait(s):
        ag2(s, 0, 1, ky, ydev, 1).wait_recv()
        ag2(s, 0, 2, kd, ydev, 2).wait_recv()
        ag2(s, 1, 0, kx, xdev, 0).wait_recv()
        ag2(s, 1, 2, kd, xdev, 2).wait_recv()

    def ag_drain(s):
        for dz in range(1, 4):
            ag1(s, dz, core, li, sib).wait_send()

        @pl.when(core != own)
        def _():
            ag1(s, 0, core, li, sib).wait_send()

        for e in range(2):
            for to in range(3):
                ag2(s, e, to, k, xdev, to).wait_send()

    if inner:
        for copy in master_copies[:2]:
            copy.wait()
        out_t = jnp.concatenate([out_m[...], jnp.zeros((192, 128 - R), F32)], axis=1).T[:R]
        tail_q, tail_k, tail_v = (proj_m[j, :, 128:192] for j in range(3))
        for j in range(3):
            pack[0, :, 128 * j : 128 * j + 128] = proj_m[j, :, :128].astype(BF16)
        pack[0, :, 384:512] = jnp.concatenate([tail_q, tail_k], axis=1).astype(BF16)
        pack[0, :, 512:640] = jnp.concatenate([tail_v, out_t[:, 128:]], axis=1).astype(BF16)
        pack[0, :, 640:768] = out_t[:, :128].astype(BF16)
        for s in range(3):
            ag1_start(s)
        norm_copy.wait()
        nl[pl.ds(d, 1)] = jnp.zeros((1, 8, 128), F32)
        nl[pl.ds(d, 1), 0:4, 0:R] = norm_m[...].astype(BF16).astype(F32).reshape(1, 4, R)
        rc(nl.at[pl.ds(d, 1)], nl.at[pl.ds(d, 1)], n_s.at[0], n_r.at[0], sib).start()
        for copy in master_copies[2:]:
            copy.wait()
        pack[1] = up_m[...].astype(BF16)
        pack[2] = down_m[...].astype(BF16)
        for s in range(3, PIECES):
            ag1_start(s)
        rc(nl.at[pl.ds(d, 1)], nl.at[pl.ds(sib[0], 1)], n_s.at[0], n_r.at[0], sib).wait()
        for i, dev in enumerate(plane):
            rc(nl.at[pl.ds(2 * k, 2)], nl.at[pl.ds(2 * k, 2)], n_s.at[1 + i], n_r.at[1 + i], dev).start()
        ag2_start(0)
    else:
        w_copy = pltpu.make_async_copy(w_in, W, loc.at[3])
        w_copy.start()

    @pl.when(core == own)
    def _():
        for i in range(3):
            in_local(i).wait()

    @pl.when(core != own)
    def _():
        for i in range(3):
            in_remote(i).wait_recv()

    if inner:
        for i, kk in enumerate((kx, ky, kd)):
            rc(nl.at[pl.ds(2 * kk, 2)], nl.at[pl.ds(2 * kk, 2)], n_s.at[1 + i], n_r.at[1 + i], plane[i]).wait()
        nw[...] = jnp.concatenate([nl[i][:, :R] for i in range(8)], axis=1)
    else:
        norm_copy.wait()
        nw[...] = norm_m[...]

    length = lens_v[0:1, 0:1]

    def row_valid(start, rows):
        ids = (lax.broadcasted_iota(jnp.int32, (rows, 1), 0) + start).astype(F32)
        return ids < length

    def at(i, size=TB):
        return pl.ds(pl.multiple_of(i * size, size), size)

    def norm_one(i, carry):
        rows = at(i)
        n, _ = normalize(xs[rows, :].astype(F32))
        h = (n * nw[0:1, :] + nw[1:2, :]).astype(BF16)
        h1[rows, :] = h
        h1T[:, rows] = h.T
        return carry

    def mask_cotangent(i, carry):
        rows = at(i)
        c = jnp.where(row_valid(i * TB, TB), cc[rows, :].astype(F32), 0.0).astype(BF16)
        cc[rows, :] = c
        cT[:, rows] = c.T
        return carry

    if inner:
        ag2_start(1)
        ag3_start(0)
    run("norm_one", NB // 2, norm_one)
    if inner:
        ag2_start(2)
    run("norm_one", NB // 2, lambda i, carry: norm_one(i + NB // 2, carry))
    if inner:
        ag3_start(1)
    else:
        w_copy.wait()
    run("mask_cotangent", NB, mask_cotangent)
    table_copy.wait()
    if inner:
        ag_wait(0)
        ag3_start(2)
        ag2_start(3)
        ag_wait(1)
        ag2_start(4)

    lane = lanes(TB)
    low = lane < HD
    first = lane % HD < HD // 2

    def make_pair(p):
        def block(i, carry):
            rows = at(i)
            h = h1[rows, :]
            cos, sin = cos_ref[rows, :], sin_ref[rows, :]
            if p < 2:
                raw = dot(h, W[0, :, p * 768 : p * 768 + 384])
                q, kk, v = raw[:, :128], raw[:, 128:256], raw[:, 256:]
                q = rope(q, cos, sin, first)
                kk = rope(kk, cos, sin, first)
            else:
                r0 = dot(h, W[0, :, 384:640])
                r1 = dot(h, W[0, :, 768 + 384 : 768 + 640])
                ra = rope(r0[:, :128], cos, sin, first)
                rb = rope(r1[:, :128], cos, sin, first)
                q = jnp.where(low, ra, pltpu.roll(rb, 64, 1))
                kk = jnp.where(low, pltpu.roll(ra, 64, 1), rb)
                v = jnp.where(low, r0[:, 128:], pltpu.roll(r1[:, 128:], 64, 1))
            q = q * HD**-0.5
            bias = jnp.where(row_valid(i * TB, TB), 0.0, MASK_FILL)
            kT[p, :, rows] = kk.astype(BF16).T
            for half in range(2):
                mine = head_lanes(lane, half)
                base = HD - HD * half
                hh = 2 * p + half
                qe[hh, rows, :] = jnp.where(mine, q, jnp.where(lane == base, 1.0, 0.0)).astype(BF16)
                ke[hh, rows, :] = jnp.where(mine, kk, jnp.where(lane == base, bias, 1.0)).astype(BF16)
                ve[hh, rows, :] = jnp.where(mine, v, 1.0).astype(BF16)
            return carry

        run("make_pair", NB, block)

    def attend(p, i):
        rows = at(i)
        outs = []
        for half in range(2):
            hh = 2 * p + half
            mine = head_lanes(lane, half)
            base = HD - HD * half
            q = qe[hh, rows, :]
            s = dot_t(q, ke[hh])
            top = jnp.max(s, axis=-1, keepdims=True)
            ex = jnp.exp(s - top).astype(BF16)
            o = dot(ex, ve[hh])
            total = o[:, base : base + 1]
            outs.append(o * (1.0 / total))
            hi, mid, lo = three_parts(top + jnp.log(total))
            extra = spare_columns(lane, base, (1.0, -hi, -mid, -lo), 0.0)
            qe[hh, rows, :] = jnp.where(mine, q.astype(F32), extra).astype(BF16)
        opair[p, rows, :] = jnp.where(low, outs[0], outs[1]).astype(BF16)

    def o_copy(p):
        return rc(opair.at[p], osib.at[p], o_s.at[p], o_r.at[p], sib)

    def ws_copy(e):
        return rc(W.at[0, :, pl.ds(e * 768 + 512, 256)], wsib.at[e], ws_s.at[e], ws_r.at[e], sib)

    for p in range(3):
        if inner and p == 1:
            ag3_start(3)
        if inner and p == 2:
            ag_wait(2)
            ag2_start(8)
        make_pair(p)

        def attend_two(i, carry, p=p):
            attend(p, 2 * i)
            if inner and p == 0:
                ag2_start(5 + i)
            if inner and p == 1:
                pl.when(i == 0)(lambda: ag2_start(7))
                pl.when(i == 1)(lambda: ag3_start(4))
            if inner and p == 2:
                pl.when(i == 0)(lambda: ag3_start(5))
            attend(p, 2 * i + 1)
            return carry

        run("attend_two", NB // 2, attend_two)
        o_copy(p).start()
        if p == 2:
            for e in range(2):
                ws_copy(e).start()

    def wide_o(pairs, e, rows):
        single = pairs[2, rows, :].astype(F32)
        if e == 0:
            single = pltpu.roll(single, 64, 1)
        single = jnp.where(low, 0.0, single).astype(BF16)
        return jnp.concatenate([single, pairs[e, rows, :]], axis=1)

    for p in range(3):
        o_copy(p).wait()
    for e in range(2):
        ws_copy(e).wait()
    if inner:
        ag3_start(6)

    def project_out(i, carry):
        rows = at(i)
        acc = xs[rows, :].astype(F32)
        for e in range(2):
            acc = acc + dot_t(wide_o(opair, e, rows), W[0, :, e * 768 + 512 : e * 768 + 768])
            acc = acc + dot_t(wide_o(osib, e, rows), wsib[e])
        x1[rows, :] = acc
        n, _ = normalize(acc)
        h = (n * nw[2:3, :] + nw[3:4, :]).astype(BF16)
        h2[rows, :] = h
        h2T[:, rows] = h.T
        return carry

    run("project_out", NB, project_out)
    if inner:
        ag3_start(7)

    def grad(s):
        return GA if isinstance(s, int) and s < 3 else W.at[piece(s)[0]]

    def ways(s, e):
        flip = isinstance(s, int) and s == 1
        one, two = ((kx, xdev), (ky, ydev)) if e == int(flip) else ((ky, ydev), (kx, xdev))
        return one, two

    def rs1(s, e, b, rows, dev):
        src = grad(s).at[rows_at(rows, RC), cols_at(e, piece(s)[1])]
        return rc(src, LX.at[s, e, b], r1s.at[s, e, b], r1r.at[s, e, b], dev)

    def rs1_half(s, e):
        (near, dev), _ = ways(s, e)
        rs1(s, e, 1, kd, dev).start()
        rs1(s, e, 0, near, dev).start()

    def rs2(s, e, dev):
        return rc(LX.at[s, e, 1], LY.at[s, e], r2s.at[s, e], r2r.at[s, e], dev)

    def rs2_half(s, e):
        _, (far, dev) = ways(s, e)
        rs1(s, e, 1, far, dev).wait_recv()
        mine = grad(s)[rows_at(far, RC), cols_at(e, piece(s)[1])].astype(F32)
        LX[s, e, 1] = (LX[s, e, 1].astype(F32) + mine).astype(BF16)
        rs2(s, e, dev).start()

    def rs3(s, e, a, dev):
        return rc(LX.at[s, e, 0, pl.ds(a * R, R)], ZL.at[s, z], zss.at[s, e * 2 + a], zsr.at[s, z], dev)

    def rs3_half(s, e):
        rs1(s, e, 0, k, xdev).wait_recv()
        rs2(s, e, ydev).wait_recv()
        mine = grad(s)[rows_at(k, RC), cols_at(e, piece(s)[1])].astype(F32)
        LX[s, e, 0] = (LX[s, e, 0].astype(F32) + LY[s, e].astype(F32) + mine).astype(BF16)
        zt = 2 * core + e
        for a in range(2):
            here = (core == a) & (zt == z)

            @pl.when(here)
            def _(a=a, e=e):
                pltpu.make_async_copy(LX.at[s, e, 0, pl.ds(a * R, R)], ZL.at[s, z], zsr.at[s, z]).start()

            @pl.when(jnp.logical_not(here))
            def _(a=a, e=e, zt=zt):
                rs3(s, e, a, (2 * k + a, zt)).start()

    def rs1_start(s):
        for e in range(2):
            rs1_half(s, e)

    def rs2_start(s):
        for e in range(2):
            rs2_half(s, e)

    def rs3_start(s):
        for e in range(2):
            rs3_half(s, e)

    def rs4(s):
        j, col = piece(s)
        total = jnp.zeros((R, SUB), F32)
        for zz in range(4):
            rc(LX.at[s, 0, 0, pl.ds(0, R)], ZL.at[s, zz], zss.at[s, 0], zsr.at[s, zz], sib).wait_recv()
            total = total + ZL[s, zz].astype(F32)
        gbuf[j, :, pl.ds(col, SUB)] = total
        pltpu.make_async_copy(gbuf.at[j, :, pl.ds(col, SUB)], g_out.at[j, :, pl.ds(col, SUB)], loc.at[10]).start()
        return total

    def rs_drain(s):
        for e in range(2):
            for b in range(2):
                rs1(s, e, b, k, xdev).wait_send()
            rs2(s, e, ydev).wait_send()
            zt = 2 * core + e
            for a in range(2):

                @pl.when(jnp.logical_not((core == a) & (zt == z)))
                def _(a=a, e=e):
                    rs3(s, e, a, sib).wait_send()

    def out_copy(ref, which, qi, slot):
        src = stage.at[which, pl.ds(pl.multiple_of(qi * (T // 4), T // 4), T // 4), :]
        return rc(src, ref.at[li], out_s.at[which, qi], out_r.at[which, slot], (2 * k + own, 2 * core + qi))

    def out_start(ref, which, qi):
        here = (core == own) & (li == qi)

        @pl.when(here)
        def _():
            src = stage.at[which, pl.ds(pl.multiple_of(qi * (T // 4), T // 4), T // 4), :]
            pltpu.make_async_copy(src, ref.at[li], out_r.at[which, li]).start()

        @pl.when(jnp.logical_not(here))
        def _():
            out_copy(ref, which, qi, li).start()

    def out_wait(ref, which):
        for slot in range(2):
            src = stage.at[which, pl.ds(0, T // 4), :]
            rc(src, ref.at[slot], out_s.at[which, 0], out_r.at[which, slot], sib).wait_recv()
        for qi in range(2):

            @pl.when(jnp.logical_not((core == own) & (li == qi)))
            def _(qi=qi):
                out_copy(ref, which, qi, 0).wait_send()

    def d2_copy(i):
        return rc(h1.at[at(i), :], dh2r.at[at(i), :], d2_s.at[i], d2_r.at[i], sib)

    if inner:
        for s in range(3):
            ag_drain(s)

    for i3 in range(3):
        if inner:
            ag_wait(3 + 2 * i3)
            ag_wait(4 + 2 * i3)
        wide_cols = [cols_at(e, SUB * i3) for e in range(2)]

        def hidden(i, carry, i3=i3):
            rows = at(i % NB)
            e = i // NB
            cols = cols_at(e, SUB * i3)
            here = pl.ds(pl.multiple_of(e * SUB, SUB), SUB)
            u = dot(h2[rows, :], W[1, :, cols])
            dz = dot(cc[rows, :], W[2, :, cols])
            cumulative = 0.5 * (1.0 + lax.erf(u * INV_ROOT_TWO))
            slope = cumulative + u * jnp.exp(-0.5 * u * u) * INV_ROOT_TWO_PI
            zb[rows, here] = (u * cumulative).astype(BF16)
            du[rows, here] = (dz * slope).astype(BF16)
            return carry

        run("hidden", 2 * NB, hidden)
        if inner and i3 == 0:
            ag3_start(8)
        if inner and i3 == 2:
            rs2_start(3)

        def back_two(i, carry, i3=i3, wide_cols=wide_cols):
            rows = at(i)
            v = dot_t(du[rows, 0:SUB], W[1, :, wide_cols[0]]) + dot_t(du[rows, SUB : 2 * SUB], W[1, :, wide_cols[1]])
            f = dot_t(zb[rows, 0:SUB], W[2, :, wide_cols[0]]) + dot_t(zb[rows, SUB : 2 * SUB], W[2, :, wide_cols[1]])
            if i3 > 0:
                v = v + dh2[rows, :]
                f = f + facc[rows, :]
            dh2[rows, :] = v
            facc[rows, :] = f
            if i3 == 2:
                h1[rows, :] = v.astype(BF16)
                d2_copy(i).start()
            return carry

        run("back_two", NB, back_two)
        if inner:
            ag_drain(3 + 2 * i3)
            ag_drain(4 + 2 * i3)

        def grad_ffn(e, carry, i3=i3):
            here = pl.ds(pl.multiple_of(e * SUB, SUB), SUB)
            W[1, :, cols_at(e, SUB * i3)] = dot(h2T[...], du[:, here]).astype(BF16)
            W[2, :, cols_at(e, SUB * i3)] = dot(cT[...], zb[:, here]).astype(BF16)
            return carry

        run("grad_ffn", 2, grad_ffn)
        if inner:
            rs1_start(3 + 2 * i3)
            rs1_start(4 + 2 * i3)

    other = 1 - core

    def half_rows(which, i):
        return pl.ds(pl.multiple_of(which * HALF + i * TB, TB), TB)

    def f_copy():
        return rc(fsend, frecv, f_s.at[0], f_r.at[0], sib)

    def ffn_other(i, carry):
        fsend[at(i), :] = facc[half_rows(other, i), :].astype(BF16)
        return carry

    run("ffn_other", NB // 2, ffn_other)
    f_copy().start()
    f_copy().wait()

    def ffn_final(i, carry):
        rows = half_rows(core, i)
        y = x1[rows, :] + facc[rows, :] + frecv[at(i), :].astype(F32)
        stage[0, at(i), :] = y.astype(BF16)
        out_start(lo_out, 0, i)
        return carry

    run("ffn_final", NB // 2, ffn_final)

    gn_out[...] = jnp.zeros_like(gn_out)

    def norm_back_two(i, carry):
        rows = at(i)
        d2_copy(i).wait()
        e2 = dh2[rows, :] + dh2r[rows, :].astype(F32)
        n, r = normalize(x1[rows, :])
        m = e2 * nw[2:3, :]
        dx = cc[rows, :].astype(F32) + r * (m - row_mean(m) - n * row_mean(m * n))
        dh2[rows, :] = dx
        low_dx = dx.astype(BF16)
        h2[rows, :] = low_dx
        h2T[:, rows] = low_dx.T
        count = jnp.where(i // (NB // 2) == core, 1.0, 0.0)
        gn_out[2:3, :] += count * jnp.sum(e2 * n, axis=0, keepdims=True)
        gn_out[3:4, :] += count * jnp.sum(e2, axis=0, keepdims=True)
        return carry

    run("norm_back_two", NB, norm_back_two)
    da, daT = h2, h2T
    if inner:
        rs2_start(4)
        rs3_start(3)

    def do_block(i, carry):
        rows = at(i)
        for e in range(2):
            zb[rows, e * 256 : e * 256 + 256] = wide_o(opair, e, rows)
        parts = [dot(da[rows, :], W[0, :, e * 768 + 512 : e * 768 + 768]) for e in range(2)]
        pairs = [parts[0][:, 128:], parts[1][:, 128:], jnp.where(low, pltpu.roll(parts[0][:, :128], 64, 1), parts[1][:, :128])]
        for p in range(3):
            g = pairs[p].astype(BF16).astype(F32)
            prod = g * opair[p, rows, :].astype(F32)
            for half in range(2):
                mine = head_lanes(lane, half)
                base = HD - HD * half
                delta = jnp.sum(jnp.where(mine, prod, 0.0), axis=-1, keepdims=True)
                hi, mid, lo = three_parts(delta)
                extra = spare_columns(lane, base + 1, (-hi, -mid, -lo), 0.0)
                doe[2 * p + half, rows, :] = jnp.where(mine, g, extra).astype(BF16)
        return carry

    run("do_block", NB, do_block)
    if inner:
        rs2_start(5)
        rs2_start(6)

    def back_keys(p, i):
        rows = at(i)
        cos, sin = cos_ref[rows, :], sin_ref[rows, :]
        dks, dvs = [], []
        for half in range(2):
            hh = 2 * p + half
            sT = dot_t(ke[hh, rows, :], qe[hh])
            pT = jnp.exp(sT)
            dpT = dot_t(ve[hh, rows, :], doe[hh])
            dsT = (pT * dpT).astype(BF16)
            dvs.append(dot(pT.astype(BF16), doe[hh]))
            dks.append(dot(dsT, qe[hh]))
            part = dot(kT[p, half * HD : half * HD + HD, rows], dsT)
            dqT[half * HD : half * HD + HD, :] += part
        dk = rope_back(jnp.where(low, dks[0], dks[1]), cos, sin, first)
        dv = jnp.where(low, dvs[0], dvs[1])
        put_draw(p, rows, None, dk, dv)

    def put_draw(p, rows, dq, dk, dv):
        if p < 2:
            for i, v in enumerate((dq, dk, dv)):
                if v is not None:
                    du[rows, p * 768 + 128 * i : p * 768 + 128 * i + 128] = v.astype(BF16)
            return
        if dk is not None:
            du[rows, 640:768] = dk.astype(BF16)
            du[rows, 512:640] = jnp.where(low, dv, 0.0).astype(BF16)
            du[rows, 768 + 512 : 768 + 640] = jnp.where(low, pltpu.roll(dv, 64, 1), 0.0).astype(BF16)
        if dq is not None:
            dk = du[rows, 640:768].astype(F32)
            du[rows, 384:512] = jnp.where(low, dq, pltpu.roll(dk, 64, 1)).astype(BF16)
            du[rows, 768 + 384 : 768 + 512] = jnp.where(low, pltpu.roll(dq, 64, 1), dk).astype(BF16)

    def put_queries(p):
        def block(i, carry):
            rows = at(i)
            cos, sin = cos_ref[rows, :], sin_ref[rows, :]
            dq = dqT[:, rows].T * HD**-0.5
            put_draw(p, rows, rope_back(dq, cos, sin, first), None, None)
            return carry

        run("put_queries", NB, block)

    def back_pair(p, pumps):
        dqT[...] = jnp.zeros_like(dqT)

        def pump(i, half):
            if inner:
                for step in range(NB // 2):
                    if 2 * step + half in pumps:
                        pl.when(i == step)(pumps[2 * step + half])

        def back_step(i, carry):
            back_keys(p, 2 * i)
            pump(i, 0)
            back_keys(p, 2 * i + 1)
            pump(i, 1)
            return carry

        run("back_step", NB // 2, back_step)
        put_queries(p)

    def several(*steps):
        def go():
            for f, *of in steps:
                f(*of)

        return go

    back_pair(2, {1: several((rs2_start, 7)), 3: several((rs2_start, 8), (rs3_start, 4))})

    def grad_attn_two(e, carry):
        b = e * 768
        for col in (384, 512):
            here = pl.ds(pl.multiple_of(b + col, 128), 128)
            v = dot(h1T[...], du[:, here])
            if col == 512:
                wide = dot(daT[...], zb[:, pl.ds(pl.multiple_of(e * 256, 256), 256)])
                GA[:, pl.ds(pl.multiple_of(b + 640, 128), 128)] = wide[:, 128:].astype(BF16)
                v = v + wide[:, :128]
            GA[:, here] = v.astype(BF16)
        return carry

    run("grad_attn", 2, grad_attn_two)
    if inner:
        rs1_start(2)
        rs3_start(5)

    def grad_attn(p):
        def one(i, carry, b=p * 768):
            GA[:, b : b + 384] = dot(h1T[...], du[:, b : b + 384]).astype(BF16)
            return carry

        run("grad_attn", 1, one)

    back_pair(0, {0: several((rs3_start, 6)), 2: several((rs3_start, 7)), 3: several((rs3_start, 8))})
    grad_attn(0)
    squares_ref[...] = jnp.zeros_like(squares_ref)

    def four(s):
        g = rs4(s)
        squares_ref[...] += g * g

    if inner:
        rs1_half(0, 0)
        rs1_half(1, 0)
    back_pair(1, {0: several((rs2_start, 2)), 3: several((rs2_half, 0, 0), (rs2_half, 1, 0), (rs3_start, 2))})
    grad_attn(1)
    if inner:
        rs1_half(0, 1)
        rs1_half(1, 1)

    def back_one(rows):
        return dot_t(du[rows, 0:640], W[0, :, 0:640]) + dot_t(du[rows, 768 : 768 + 640], W[0, :, 768 : 768 + 640])

    def d1_copy(i):
        return rc(fsend.at[at(i), :], drecv.at[at(i), :], d1_s.at[i], d1_r.at[i], sib)

    def one_other(i, carry):
        fsend[at(i), :] = back_one(half_rows(other, i)).astype(BF16)
        d1_copy(i).start()
        return carry

    run("one_other", NB // 2, one_other)

    def one_mine(i, carry):
        rows = half_rows(core, i)
        x1[rows, :] = back_one(rows)
        return carry

    run("one_mine", NB // 2, one_mine)
    if inner:
        rs3_half(0, 0)
        rs3_half(1, 0)

    def norm_back_one(i, carry):
        rows = half_rows(core, i)
        d1_copy(i).wait()
        e1 = x1[rows, :] + drecv[at(i), :].astype(F32)
        n, r = normalize(xs[rows, :].astype(F32))
        m = e1 * nw[0:1, :]
        dx = dh2[rows, :] + r * (m - row_mean(m) - n * row_mean(m * n))
        stage[1, at(i), :] = dx.astype(BF16)
        gn_out[0:1, :] += jnp.sum(e1 * n, axis=0, keepdims=True)
        gn_out[1:2, :] += jnp.sum(e1, axis=0, keepdims=True)
        return carry

    run("norm_back_one", 1, norm_back_one)
    out_start(ig_out, 1, 0)
    run("norm_back_one", NB // 2 - 1, lambda i, carry: norm_back_one(i + 1, carry))

    def sum_first(l1, which):
        return [rc(l1.at[0], l1.at[slot], e_s.at[which, slot], e_r.at[which, slot], dev) for slot, dev in column]

    def sum_plane(l2, which):
        return [rc(l2.at[0], l2.at[1 + i], e_s.at[which, 8 + i], e_r.at[which, 8 + i], dev) for i, dev in enumerate(plane)]

    def sum_start(ref, l1, l2, which):
        l1[0] = ref[...]
        for copy in sum_first(l1, which):
            copy.start()

    def sum_second(l1, l2, which):
        for copy in sum_first(l1, which):
            copy.wait()
        total = l1[0]
        for slot in range(1, 8):
            total = total + l1[slot]
        l2[0] = total
        for copy in sum_plane(l2, which):
            copy.start()

    def sum_end(ref, l1, l2, which):
        for copy in sum_plane(l2, which):
            copy.wait()
        total = l2[0]
        for i in range(1, 4):
            total = total + l2[i]
        ref[...] = total

    if inner:
        sum_start(gn_out, gl1, gl2, 0)
        rs2_half(0, 1)
        rs2_half(1, 1)
        for s in range(3, PIECES):
            four(s)
        rs3_half(0, 1)
        rs3_half(1, 1)
    out_start(ig_out, 1, 1)
    if inner:
        sum_second(gl1, gl2, 0)
        four(2)
        sum_end(gn_out, gl1, gl2, 0)
        four(0)
        four(1)
        total = jnp.sum(squares_ref[...], axis=0, keepdims=True)
        total = total[:, :128] + total[:, 128:]
        sq_out[...] = jnp.where(lax.broadcasted_iota(jnp.int32, (8, 128), 0) == 0, total, 0.0)
        sum_start(sq_out, sl1, sl2, 1)
        sum_second(sl1, sl2, 1)

        def drain_rs(s, carry):
            rs_drain(s)
            return carry

        for s in range(3):
            rs_drain(s)
        lax.fori_loop(3, PIECES, drain_rs, 0)
        sum_end(sq_out, sl1, sl2, 1)
        gn_out[4:5, 0:128] = jnp.sum(sq_out[...], axis=0, keepdims=True)
        pltpu.make_async_copy(gbuf, g_out, loc.at[10]).wait()
    else:
        for j in range(3):
            g_copy = pltpu.make_async_copy(GA if j == 0 else W.at[j], g_out.at[j], loc.at[3 + j])
            g_copy.start()
            g_copy.wait()
    small_copy = pltpu.make_async_copy(gn_out, small_out, loc.at[11])
    small_copy.start()
    small_copy.wait()
    out_wait(lo_out, 0)
    out_wait(ig_out, 1)

    @pl.when(core == own)
    def _():
        for i in range(3):
            in_remote(i).wait_send()


def rope_tables(length):
    places = np.arange(length, dtype=np.float32)
    rates = (ROPE_BASE ** (-(np.arange(HD // 2, dtype=np.float32) * 2.0 / HD))).astype(np.float32)
    angles = places[:, None] * rates[None, :]
    cos = np.tile(np.cos(angles), (1, 4)).astype(np.float32)
    sin = np.tile(np.sin(angles), (1, 4)).astype(np.float32)
    first = (np.arange(128) % HD < HD // 2)[None, :]
    return np.stack([cos, np.where(first, -sin, sin)]).astype(np.float32)


def adam_update(refs, outs, gradient, clip_factor, step_rate, decay_rate):
    master, first_old, second_old = (ref[...] for ref in refs)
    clipped = gradient * clip_factor
    first_new = BETA_FIRST * first_old + (1.0 - BETA_FIRST) * clipped
    second_new = BETA_SECOND * second_old + (1.0 - BETA_SECOND) * clipped * clipped
    fix_first = 1.0 - BETA_FIRST**STEP
    fix_second = 1.0 - BETA_SECOND**STEP
    normalized = first_new / fix_first / (jnp.sqrt(second_new / fix_second) + ADAM_EPSILON)
    master_new = master - step_rate * (normalized + decay_rate * master)
    for out, v in zip(outs, (master_new, first_new, second_new, master_new.astype(BF16))):
        out[...] = v


def update_kernel(R, shapes, g_in, small_in, lo_in, ig_in, *refs):
    param_ins, refs = refs[:15], refs[15:]
    lo_out, ig_out, norm_out = refs[:3]
    param_outs, refs = refs[3:23], refs[23:]
    g, small, params, outs, in_sems, out_sems = refs[0], refs[1], refs[2:17], refs[17:37], refs[37], refs[38]
    passing = [(lo_in, refs[39].at[0], lo_out), (ig_in, refs[39].at[1], ig_out)]
    copies = [pltpu.make_async_copy(src, via, in_sems.at[17 + i]) for i, (src, via, _) in enumerate(passing)]
    ins = [pltpu.make_async_copy(g_in, g, in_sems.at[15]), pltpu.make_async_copy(small_in, small, in_sems.at[16])]
    ins += [pltpu.make_async_copy(src, dst, in_sems.at[i]) for i, (src, dst) in enumerate(zip(param_ins, params))]
    for copy in ins + copies:
        copy.start()
    for copy in ins + copies:
        copy.wait()
    copies = [pltpu.make_async_copy(via, dst, out_sems.at[20 + i]) for i, (_, via, dst) in enumerate(passing)]
    for copy in copies:
        copy.start()
    gn_all = small[0:4, :]
    squares = jnp.sum(small[4:5, 0:128], keepdims=True) + jnp.sum(gn_all * gn_all, keepdims=True)
    grad_norm = jnp.sqrt(squares)
    norm_out[...] = grad_norm
    clip_factor = jnp.minimum(1.0, CLIP_LIMIT / (grad_norm + 1e-06))

    def transposed(v):
        return jnp.concatenate([v, jnp.zeros((128 - R, v.shape[1]), F32)], axis=0).T[:, :R]

    a = g[0]
    g_proj = [jnp.concatenate([a[:, 128 * j : 128 * j + 128], a[:, 384 + 64 * j : 448 + 64 * j]], axis=1) for j in range(3)]
    g_out = transposed(jnp.concatenate([a[:, 640:], a[:, 576:640]], axis=1))
    D = gn_all.shape[1]
    first_row = lax.axis_index("dp") * R
    r_i = lax.broadcasted_iota(jnp.int32, (D, 128), 0)
    c_i = lax.broadcasted_iota(jnp.int32, (D, 128), 1)
    sel = jnp.where((r_i == c_i + first_row) & (c_i < R), 1.0, 0.0).astype(BF16)
    g_norm = sum(dot(part.astype(BF16), sel) for part in three_parts(small[...]))[:4, :R]

    def update(i, gradient, rate, decay, index=None):
        ins, results = params[3 * i : 3 * i + 3], outs[4 * i : 4 * i + 4]
        if index is not None:
            ins, results = [r.at[index] for r in ins], [r.at[index] for r in results]
        adam_update(ins, results, gradient, clip_factor, rate, decay)
        if index is None or index == 2:
            for n in range(4 * i, 4 * i + 4):
                copies.append(pltpu.make_async_copy(outs[n], param_outs[n], out_sems.at[n]))
                copies[-1].start()

    update(2, g[1], RATE_MATRIX, WEIGHT_DECAY)
    update(3, g[2], RATE_MATRIX, WEIGHT_DECAY)
    for j in range(3):
        update(0, g_proj[j], RATE_MATRIX, WEIGHT_DECAY, j)
    update(1, g_out, RATE_MATRIX, WEIGHT_DECAY)
    update(4, g_norm, RATE_NORM, 0.0)
    for copy in copies:
        copy.wait()


def per_device(
    inputs,
    cotangent,
    lengths,
    proj_master,
    proj_first,
    proj_second,
    out_master,
    out_first,
    out_second,
    up_master,
    up_first,
    up_second,
    down_master,
    down_first,
    down_second,
    norm_master,
    norm_first,
    norm_second,
):
    _, T, D = inputs.shape
    R = proj_master.shape[1]
    n_dp = lax.axis_size("dp")
    inner = n_dp == 8
    d = lax.axis_index("dp")
    z = lax.axis_index("head")
    core = d % 2
    if inner:
        norm_in = norm_master
        extra = (proj_master, out_master, up_master, down_master.T)
    else:
        out_t = out_master.T
        attn = jnp.concatenate(
            [proj_master[0, :, :128], proj_master[1, :, :128], proj_master[2, :, :128]]
            + [proj_master[0, :, 128:], proj_master[1, :, 128:], proj_master[2, :, 128:]]
            + [out_t[:, 128:], out_t[:, :128]],
            axis=1,
        )
        pack = jnp.stack([attn, up_master, down_master.T]).astype(BF16)
        norm_in = jnp.pad(lax.all_gather(norm_master, "dp", axis=1, tiled=True), ((0, 4), (0, 0)))
        norm_in = norm_in.astype(BF16).astype(F32)
        full = lax.all_gather(pack, "dp", axis=1, tiled=True)
        every = lax.all_gather(full, "head", axis=0)
        pair = lax.dynamic_slice_in_dim(every, 2 * core, 2, 0)
        w_in = jnp.concatenate([pair[0], pair[1]], axis=2)
        extra = (w_in,)

    hbm = pl.BlockSpec(memory_space=pltpu.HBM)
    dma = pltpu.SemaphoreType.DMA
    quarter = T // 4
    g_shape = (3, R, 768) if inner else (3, D, 1536)
    out_shape = (
        jax.ShapeDtypeStruct((2, quarter, D), BF16),
        jax.ShapeDtypeStruct((2, quarter, D), BF16),
        jax.ShapeDtypeStruct(g_shape, F32 if inner else BF16),
        jax.ShapeDtypeStruct((8, D), F32),
    )
    HALF = T // 2
    NB = T // 256
    bf = lambda *s: pltpu.VMEM(s, BF16)
    ff = lambda *s: pltpu.VMEM(s, F32)
    RC = 2 * R
    pieces = PIECES if inner else 1
    lx_rows = RC if inner else 16
    zl_rows = R if inner else 16
    RL = R if inner else 8
    scratch = [
        bf(3, D, 1536), bf(D, 1536), bf(T, D), bf(T, D), bf(D, T), bf(T, D), bf(D, T), bf(T, D), bf(D, T), ff(T, D),
        bf(6, T, 128), bf(6, T, 128), bf(6, T, 128), bf(6, T, 128), bf(3, 128, T),
        bf(3, T, 128), bf(3, T, 128), bf(2, D, 256), bf(T, 2 * SUB), bf(T, 1536), ff(T, D), bf(T, D), ff(128, T), ff(T, D),
        bf(HALF, D), bf(HALF, D), bf(HALF, D), bf(2, HALF, D),
        ff(8, 128), ff(8, 128), bf(3, zl_rows, 768), ff(8, D), ff(8, 8, 128), ff(8, 8, D), ff(4, 8, D), ff(8, 8, 128), ff(4, 8, 128),
        bf(pieces, 2, 2, lx_rows, SUB), bf(pieces, 2, lx_rows, SUB), bf(pieces, 4, zl_rows, SUB),
        dma((3,)), dma((3,)), dma((3,)), dma((3,)), dma((2,)), dma((2,)), dma((NB,)), dma((NB,)),
        dma((1,)), dma((1,)), dma((NB,)), dma((NB,)), dma((2, 2)), dma((2, 2)), dma((4,)), dma((4,)), dma((2, 11)), dma((2, 11)),
        dma((pieces, 4)), dma((pieces, 4)), dma((pieces, 2, 3)), dma((pieces, 2, 3)),
        dma((pieces, 2, 2)), dma((pieces, 2, 2)), dma((pieces, 2)), dma((pieces, 2)), dma((pieces, 4)), dma((pieces, 4)),
        dma((12,)),
        ff(2, T, 128), ff(*norm_in.shape), ff(3, RL, 192), ff(192, RL), ff(RL, 768), ff(RL, 768), ff(8, D), ff(8, 128), ff(3, RL, 768), ff(RL, SUB),
    ]
    layer_out, input_grad, grads, small = pl.pallas_call(
        functools.partial(layer_kernel, inner, T, D, R),
        out_shape=out_shape,
        in_specs=[hbm, hbm, pl.BlockSpec(memory_space=pltpu.SMEM)] + [hbm] * (2 + len(extra)),
        out_specs=(hbm,) * 4,
        scratch_shapes=scratch,
        compiler_params=pltpu.CompilerParams(
            collective_id=0, has_side_effects=True, vmem_limit_bytes=63 * 2**20
        ),
        name="layer",
    )(inputs, cotangent, lengths, jnp.asarray(rope_tables(T)), norm_in, *extra)

    if not inner:
        spread = jnp.stack([grads[:, :, :768], grads[:, :, 768:]]).astype(F32)
        empty = jnp.zeros((4,) + spread.shape[1:], F32)
        spread = lax.dynamic_update_slice_in_dim(empty, spread, 2 * core, 0)
        mine = lax.psum_scatter(spread, "head", scatter_dimension=0, tiled=False)
        grads = lax.psum_scatter(mine, "dp", scatter_dimension=1, tiled=True)
        squares = lax.psum(jnp.sum(grads * grads), ("dp", "head"))
        small = lax.psum(small, ("dp", "head")).at[4, 0].set(squares)
    params = (
        (proj_master, proj_first, proj_second),
        (out_master, out_first, out_second),
        (up_master, up_first, up_second),
        (down_master.T, down_first.T, down_second.T),
        (norm_master, norm_first, norm_second),
    )
    shapes = []
    for group in params:
        shapes += [(v.shape, F32) for v in group] + [(group[0].shape, BF16)]
    out_shapes = [((2, quarter, D), BF16)] * 2 + [((1, 1), F32)] + shapes
    flat = [v for group in params for v in group]
    outs = pl.pallas_call(
        functools.partial(update_kernel, R, shapes),
        out_shape=tuple(jax.ShapeDtypeStruct(*v) for v in out_shapes),
        in_specs=[hbm] * 19,
        out_specs=tuple([hbm] * 2 + [pl.BlockSpec(memory_space=pltpu.VMEM)] + [hbm] * 20),
        scratch_shapes=[ff(*grads.shape), ff(8, D)]
        + [ff(*v.shape) for v in flat]
        + [pltpu.VMEM(*v) for v in shapes]
        + [dma((19,)), dma((22,)), bf(2, 2, quarter, D)],
        compiler_params=pltpu.CompilerParams(vmem_limit_bytes=63 * 2**20),
        name="update",
    )(grads, small, layer_out, input_grad, *flat)
    down = tuple(v.T for v in outs[15:19])
    return tuple(outs[:2]) + (outs[2].reshape(()),) + tuple(outs[3:15]) + down + tuple(outs[19:])


def solution(mesh):
    proj, wide, tall, norms = P(None, "dp", "head"), P("dp", "head"), P("head", "dp"), P(None, "dp")
    tokens = P("dp", None, None)
    placed = (tokens, tokens, P("dp")) + (proj,) * 3 + (tall,) * 3 + (wide,) * 3 + (tall,) * 3 + (norms,) * 3
    quarters = P("dp", "head", None)
    return jax.shard_map(
        per_device,
        mesh=mesh,
        in_specs=placed,
        out_specs=(quarters, quarters, P()) + (proj,) * 4 + (tall,) * 4 + (wide,) * 4 + (tall,) * 4 + (norms,) * 4,
        check_vma=False,
    )
```

```python
import functools

import jax
import jax.numpy as jnp
import numpy as np
from jax import lax
from jax.experimental import pallas as pl
from jax.experimental.pallas import tpu as pltpu
from jax.sharding import PartitionSpec as P

HD = 64
STEP = 5
LN_EPSILON = 1e-05
MASK_FILL = -1e30
ROPE_BASE = 10000.0
CLIP_LIMIT = 1.0
BETA_FIRST = 0.9
BETA_SECOND = 0.95
ADAM_EPSILON = 1e-08
WEIGHT_DECAY = 0.1
RATE_MATRIX = 0.03
RATE_NORM = 0.3
INV_ROOT_TWO = 0.7071067811865476
INV_ROOT_TWO_PI = 0.3989422804014327

F32 = jnp.float32
BF16 = jnp.bfloat16
MESH = pl.DeviceIdType.MESH
SUB = 256
PIECES = 9


def dot(a, b):
    return lax.dot_general(a, b, (((1,), (0,)), ((), ())), preferred_element_type=F32)


def dot_t(a, b):
    return lax.dot_general(a, b, (((1,), (1,)), ((), ())), preferred_element_type=F32)


def row_mean(v):
    return jnp.mean(v, axis=-1, keepdims=True)


def normalize(v):
    center = v - row_mean(v)
    inverse = lax.rsqrt(row_mean(center * center) + LN_EPSILON)
    return center * inverse, inverse


def lanes(rows):
    return lax.broadcasted_iota(jnp.int32, (rows, 128), 1)


def head_lanes(lane, half):
    return lane < HD if half == 0 else lane >= HD


def three_parts(col):
    hi = col.astype(BF16).astype(F32)
    mid = (col - hi).astype(BF16).astype(F32)
    return hi, mid, col - hi - mid


def spare_columns(lane, base, values, other):
    out = other
    for i, v in reversed(list(enumerate(values))):
        out = jnp.where(lane == base + i, v, out)
    return out


def turned(v, first):
    return jnp.where(first, pltpu.roll(v, 96, 1), pltpu.roll(v, 32, 1))


def rope(v, cos, sin, first):
    return v * cos + turned(v, first) * sin


def rope_back(v, cos, sin, first):
    return v * cos - turned(v, first) * sin


def run(name, count, body):
    with jax.named_scope(name):
        lax.fori_loop(0, count, body, 0)


def layer_kernel(inner, T, D, R, *refs):
    (
        x_in, ct_in, lens_in, tables_in, norm_in, *rest
    ) = refs
    if inner:
        *masters_in, lo_out, ig_out, g_out, small_out = rest[:8]
        rest = rest[8:]
    else:
        w_in, lo_out, ig_out, g_out, small_out = rest[:5]
        rest = rest[5:]
    (
        W, GA, xs, cc, cT, h1, h1T, h2, h2T, x1, qe, ke, ve, kT,
        opair, osib, wsib, zb, du, dh2, dh2r, dqT, facc, fsend, frecv, drecv, stage,
        lens_s, lens_v, pack, nw, nl, gl1, gl2, sl, LX, LY, PZ, ZL,
        in_s, in_r, o_s, o_r, ws_s, ws_r, d2_s, d2_r, f_s, f_r, d1_s, d1_r, out_s, out_r, n_s, n_r, e_s, e_r, q_s, q_r, las, lar, lbs, lbr, part,
        s1s, s1r, a2s, a2r, r1s, r1r, r2s, r2r, pzs, pzr, zss, zsr, loc,
        tables, norm_m, proj_m, out_m, up_m, down_m, gn_out, ga_out, squares_ref,
    ) = rest
    RC = 2 * R
    TB = 256
    NB = T // TB
    HALF = T // 2
    d = lax.axis_index("dp")
    z = lax.axis_index("head")
    core = d % 2
    k = d // 2
    own = z // 2
    li = z % 2
    sib = (d + 1 - 2 * core, z)
    master_copies = []
    if inner:
        for i, (src, dst) in enumerate(zip(masters_in, (proj_m, out_m, up_m, down_m))):
            master_copies.append(pltpu.make_async_copy(src, dst, loc.at[4 + i]))
    norm_copy = pltpu.make_async_copy(norm_in, norm_m, loc.at[8])
    table_copy = pltpu.make_async_copy(tables_in, tables, loc.at[9])
    for copy in master_copies + [norm_copy, table_copy]:
        copy.start()
    cos_ref, sin_ref = tables.at[0], tables.at[1]
    lens_s[...] = jnp.full((8, 128), lens_in[li].astype(F32))

    def rc(src, dst, ss, rs, dev):
        return pltpu.make_async_remote_copy(
            src_ref=src, dst_ref=dst, send_sem=ss, recv_sem=rs, device_id=dev, device_id_type=MESH
        )

    column = []
    for da in range(2):
        for dz in range(4):
            if da + dz > 0:
                dd = d if da == 0 else sib[0]
                column.append((da * 4 + dz, (dd, (z + dz) % 4)))
    if inner:
        kx = k + 1 - 2 * (k % 2)
        ky = (k + 2) % 4
        kd = 3 - k
        xdev = (2 * kx + core, z)
        ydev = (2 * ky + core, z)
        ddev = (2 * kd + core, z)
        plane = [xdev, ydev, ddev]
    else:
        plane = []
    far = []
    if inner:
        for dk in range(4):
            for da in range(2):
                for dz in range(4):
                    if dk + da + dz > 0:
                        far.append((dk * 8 + da * 4 + dz, (2 * ((k + dk) % 4) + (core + da) % 2, (z + dz) % 4)))
    everyone = [dev for _, dev in far] if inner else [dev for _, dev in column]
    barrier = pltpu.get_barrier_semaphore()
    for dev in everyone:
        pl.semaphore_signal(barrier, inc=1, device_id=dev, device_id_type=MESH)
    pl.semaphore_wait(barrier, len(everyone))

    def in_remote(i):
        src = (x_in.at[li], ct_in.at[li], lens_s)[i]
        dst = (xs, cc, lens_v)[i]
        return rc(src, dst, in_s.at[i], in_r.at[i], sib)

    def in_local(i):
        src = (x_in.at[li], ct_in.at[li], lens_s)[i]
        dst = (xs, cc, lens_v)[i]
        return pltpu.make_async_copy(src, dst, loc.at[i])

    @pl.when(core == own)
    def _():
        for i in (2, 0, 1):
            in_remote(i).start()
            in_local(i).start()

    def piece(s):
        if isinstance(s, int):
            if s < 3:
                return 0, SUB * s
            return 1 + (s - 3) % 2, SUB * ((s - 3) // 2)
        return 1 + (s - 3) % 2, pl.multiple_of(((s - 3) // 2) * SUB, SUB)

    def rows_at(block, size):
        return pl.ds(pl.multiple_of(block * size, 16), size)

    def cols_at(e, col):
        if isinstance(e, int) and isinstance(col, int):
            return pl.ds(e * 768 + col, SUB)
        return pl.ds(pl.multiple_of(e * 768 + col, 128), SUB)

    def ag1(s, dz, a, e, dev):
        j, col = piece(s)
        src = pack.at[j, :, pl.ds(col, SUB)]
        dst = W.at[j, rows_at(2 * k + a, R), cols_at(e, col)]
        return rc(src, dst, s1s.at[s, dz], s1r.at[s, a * 2 + e], dev)

    def ag1_start(s):
        j, col = piece(s)
        for dz in range(1, 4):
            ag1(s, dz, core, li, (2 * k + own, (z + dz) % 4)).start()

        @pl.when(core == own)
        def _():
            pltpu.make_async_copy(
                pack.at[j, :, pl.ds(col, SUB)], W.at[j, rows_at(d, R), cols_at(li, col)], s1r.at[s, core * 2 + li]
            ).start()

        @pl.when(core != own)
        def _():
            ag1(s, 0, core, li, sib).start()

    def ag2(s, e, to, rows, dev, slot):
        j, col = piece(s)
        region = W.at[j, rows_at(rows, RC), cols_at(e, col)]
        return rc(region, region, a2s.at[s, e, to], a2r.at[s, e, slot], dev)

    def ag2_start(s):
        for a in range(2):
            for e in range(2):
                ag1(s, 1, a, e, sib).wait_recv()
        for e in range(2):
            ag2(s, e, 0, k, xdev, 0).start()
            ag2(s, e, 1, k, ydev, 1).start()

    def ag3_start(s):
        ag2(s, 0, 2, kx, ydev, 0).wait_recv()
        ag2(s, 0, 2, kx, ydev, 2).start()
        ag2(s, 1, 2, ky, xdev, 1).wait_recv()
        ag2(s, 1, 2, ky, xdev, 2).start()

    def ag_wait(s):
        if s == LAST:
            last_wait()
            return
        ag2(s, 0, 1, ky, ydev, 1).wait_recv()
        ag2(s, 0, 2, kd, ydev, 2).wait_recv()
        ag2(s, 1, 0, kx, xdev, 0).wait_recv()
        ag2(s, 1, 2, kd, xdev, 2).wait_recv()

    LAST = PIECES - 1

    def last_first(i):
        src = pack.at[2, :, pl.ds(2 * SUB, SUB)]
        return rc(src, part.at[k], las.at[i], lar.at[i], plane[i])

    def last_second(dz, a, e, kk, dev):
        dst = W.at[2, rows_at(2 * kk + a, R), cols_at(e, 2 * SUB)]
        return rc(part.at[kk], dst, lbs.at[dz, kk], lbr.at[a * 2 + e, kk], dev)

    def last_start():
        part[k] = pack[2, :, 2 * SUB :]
        for i in range(3):
            last_first(i).start()

    def last_forward():
        for i in range(3):
            last_first(i).wait_recv()
        for kk in range(4):
            for dz in range(1, 4):
                last_second(dz, core, li, kk, (2 * k + own, (z + dz) % 4)).start()

            @pl.when(core == own)
            def _(kk=kk):
                dst = W.at[2, rows_at(2 * kk + core, R), cols_at(li, 2 * SUB)]
                pltpu.make_async_copy(part.at[kk], dst, lbr.at[core * 2 + li, kk]).start()

            @pl.when(core != own)
            def _(kk=kk):
                last_second(0, core, li, kk, sib).start()

    def last_wait():
        for kk in range(4):
            for a in range(2):
                for e in range(2):
                    last_second(1, a, e, kk, sib).wait_recv()

    def last_drain():
        for i in range(3):
            last_first(i).wait_send()
        for kk in range(4):
            for dz in range(1, 4):
                last_second(dz, core, li, kk, sib).wait_send()

            @pl.when(core != own)
            def _(kk=kk):
                last_second(0, core, li, kk, sib).wait_send()

    def ag_drain(s):
        if s == LAST:
            last_drain()
            return
        for dz in range(1, 4):
            ag1(s, dz, core, li, sib).wait_send()

        @pl.when(core != own)
        def _():
            ag1(s, 0, core, li, sib).wait_send()

        for e in range(2):
            for to in range(3):
                ag2(s, e, to, k, xdev, to).wait_send()

    if inner:
        for copy in master_copies[:2]:
            copy.wait()
        out_t = jnp.concatenate([out_m[...], jnp.zeros((192, 128 - R), F32)], axis=1).T[:R]
        tail_q, tail_k, tail_v = (proj_m[j, :, 128:192] for j in range(3))
        for j in range(3):
            pack[0, :, 128 * j : 128 * j + 128] = proj_m[j, :, :128].astype(BF16)
        pack[0, :, 384:512] = jnp.concatenate([tail_q, tail_k], axis=1).astype(BF16)
        pack[0, :, 512:640] = jnp.concatenate([tail_v, out_t[:, 128:]], axis=1).astype(BF16)
        pack[0, :, 640:768] = out_t[:, :128].astype(BF16)
        for s in range(3):
            ag1_start(s)
        norm_copy.wait()
        nl[pl.ds(d, 1)] = jnp.zeros((1, 8, 128), F32)
        nl[pl.ds(d, 1), 0:4, 0:R] = norm_m[...].astype(BF16).astype(F32).reshape(1, 4, R)
        rc(nl.at[pl.ds(d, 1)], nl.at[pl.ds(d, 1)], n_s.at[0], n_r.at[0], sib).start()
        for copy in master_copies[2:]:
            copy.wait()
        pack[1] = up_m[...].astype(BF16)
        pack[2] = down_m[...].astype(BF16)
        last_start()
        for s in range(3, LAST):
            ag1_start(s)
        rc(nl.at[pl.ds(d, 1)], nl.at[pl.ds(sib[0], 1)], n_s.at[0], n_r.at[0], sib).wait()
        for i, dev in enumerate(plane):
            rc(nl.at[pl.ds(2 * k, 2)], nl.at[pl.ds(2 * k, 2)], n_s.at[1 + i], n_r.at[1 + i], dev).start()
        ag2_start(0)
        last_forward()
    else:
        w_copy = pltpu.make_async_copy(w_in, W, loc.at[3])
        w_copy.start()

    @pl.when(core == own)
    def _():
        for i in range(3):
            in_local(i).wait()

    @pl.when(core != own)
    def _():
        for i in range(3):
            in_remote(i).wait_recv()

    if inner:
        for i, kk in enumerate((kx, ky, kd)):
            rc(nl.at[pl.ds(2 * kk, 2)], nl.at[pl.ds(2 * kk, 2)], n_s.at[1 + i], n_r.at[1 + i], plane[i]).wait()
        nw[...] = jnp.concatenate([nl[i][:, :R] for i in range(8)], axis=1)
    else:
        norm_copy.wait()
        nw[...] = norm_m[...]

    length = lens_v[0:1, 0:1]

    def row_valid(start, rows):
        ids = (lax.broadcasted_iota(jnp.int32, (rows, 1), 0) + start).astype(F32)
        return ids < length

    def at(i, size=TB):
        return pl.ds(pl.multiple_of(i * size, size), size)

    def norm_one(i, carry):
        rows = at(i)
        n, _ = normalize(xs[rows, :].astype(F32))
        h = (n * nw[0:1, :] + nw[1:2, :]).astype(BF16)
        h1[rows, :] = h
        h1T[:, rows] = h.T
        return carry

    def mask_cotangent(i, carry):
        rows = at(i)
        c = jnp.where(row_valid(i * TB, TB), cc[rows, :].astype(F32), 0.0).astype(BF16)
        cc[rows, :] = c
        cT[:, rows] = c.T
        return carry

    if inner:
        ag2_start(1)
    run("norm_one", NB, norm_one)
    if inner:
        ag3_start(0)
    run("mask_cotangent", NB, mask_cotangent)
    table_copy.wait()
    if inner:
        ag3_start(1)
        ag2_start(2)
        ag2_start(3)
        ag_wait(0)
        ag_wait(1)
    else:
        w_copy.wait()

    lane = lanes(TB)
    low = lane < HD
    first = lane % HD < HD // 2

    def make_pair(p):
        if p < 2:
            raw = dot(h1[...], W[0, :, p * 768 : p * 768 + 384])
        else:
            r0 = dot(h1[...], W[0, :, 384:640])
            r1 = dot(h1[...], W[0, :, 768 + 384 : 768 + 640])
        for i in range(NB):
            rows = slice(i * TB, i * TB + TB)
            cos, sin = cos_ref[rows, :], sin_ref[rows, :]
            if p < 2:
                q = rope(raw[rows, :128], cos, sin, first)
                kk = rope(raw[rows, 128:256], cos, sin, first)
                v = raw[rows, 256:]
            else:
                ra = rope(r0[rows, :128], cos, sin, first)
                rb = rope(r1[rows, :128], cos, sin, first)
                q = jnp.where(low, ra, pltpu.roll(rb, 64, 1))
                kk = jnp.where(low, pltpu.roll(ra, 64, 1), rb)
                v = jnp.where(low, r0[rows, 128:], pltpu.roll(r1[rows, 128:], 64, 1))
            q = q * HD**-0.5
            bias = jnp.where(row_valid(i * TB, TB), 0.0, MASK_FILL)
            kT[p, :, rows] = kk.astype(BF16).T
            for half in range(2):
                mine = head_lanes(lane, half)
                base = HD - HD * half
                hh = 2 * p + half
                qe[hh, rows, :] = jnp.where(mine, q, jnp.where(lane == base, 1.0, 0.0)).astype(BF16)
                ke[hh, rows, :] = jnp.where(mine, kk, jnp.where(lane == base, bias, 1.0)).astype(BF16)
                ve[hh, rows, :] = jnp.where(mine, v, 1.0).astype(BF16)

    def attend(p, i):
        units = [(at(2 * i + b), 2 * p + half, half) for b in range(2) for half in range(2)]
        scores = [dot_t(qe[hh, rows, :], ke[hh]) for rows, hh, _ in units]
        outs = []
        for (rows, hh, half), s in zip(units, scores):
            mine = head_lanes(lane, half)
            base = HD - HD * half
            top = jnp.max(s, axis=-1, keepdims=True)
            ex = jnp.exp(s - top).astype(BF16)
            o = dot(ex, ve[hh])
            total = o[:, base : base + 1]
            outs.append(o * (1.0 / total))
            hi, mid, lo = three_parts(top + jnp.log(total))
            extra = spare_columns(lane, base, (1.0, -hi, -mid, -lo), 0.0)
            qe[hh, rows, :] = jnp.where(mine, qe[hh, rows, :].astype(F32), extra).astype(BF16)
        for b in range(2):
            opair[p, units[2 * b][0], :] = jnp.where(low, outs[2 * b], outs[2 * b + 1]).astype(BF16)

    def o_copy(p):
        return rc(opair.at[p], osib.at[p], o_s.at[p], o_r.at[p], sib)

    def ws_copy(e):
        return rc(W.at[0, :, pl.ds(e * 768 + 512, 256)], wsib.at[e], ws_s.at[e], ws_r.at[e], sib)

    for p in range(3):
        if inner and p == 2:
            ag_wait(2)
        if p == 2:
            for e in range(2):
                ws_copy(e).start()
        make_pair(p)

        def attend_two(i, carry, p=p):
            attend(p, i)
            return carry

        run("attend_two", NB // 2, attend_two)
        o_copy(p).start()
        if inner:
            ag3_start(2 + p)
            ag2_start(4 + p)

    def wide_o(pairs, e, rows):
        single = pairs[2, rows, :].astype(F32)
        if e == 0:
            single = pltpu.roll(single, 64, 1)
        single = jnp.where(low, 0.0, single).astype(BF16)
        return jnp.concatenate([single, pairs[e, rows, :]], axis=1)

    for p in range(3):
        o_copy(p).wait()
    for e in range(2):
        ws_copy(e).wait()

    def widen(i, carry):
        rows = at(i)
        for e in range(2):
            du[rows, e * 256 : e * 256 + 256] = wide_o(opair, e, rows)
            du[rows, e * 256 + 512 : e * 256 + 768] = wide_o(osib, e, rows)
        return carry

    run("widen", NB, widen)

    def project_out(i, carry):
        cols = pl.ds(pl.multiple_of(i * 256, 256), 256)
        acc = xs[:, cols].astype(F32)
        for e in range(2):
            acc = acc + dot_t(du[:, e * 256 : e * 256 + 256], W[0, cols, e * 768 + 512 : e * 768 + 768])
            acc = acc + dot_t(du[:, e * 256 + 512 : e * 256 + 768], wsib[e, cols, :])
        x1[:, cols] = acc
        return carry

    run("project_out", D // 256, project_out)

    def norm_two(i, carry):
        rows = at(i)
        n, _ = normalize(x1[rows, :])
        h = (n * nw[2:3, :] + nw[3:4, :]).astype(BF16)
        h2[rows, :] = h
        h2T[:, rows] = h.T
        return carry

    run("norm_two", NB, norm_two)

    def grad(s):
        return GA if isinstance(s, int) and s < 3 else W.at[piece(s)[0]]

    def ways(s, e):
        flip = isinstance(s, int) and s == 1
        one, two = ((kx, xdev), (ky, ydev)) if e == int(flip) else ((ky, ydev), (kx, xdev))
        return one, two

    def rs1(s, e, b, rows, dev):
        src = grad(s).at[rows_at(rows, RC), cols_at(e, piece(s)[1])]
        return rc(src, LX.at[s, e, b], r1s.at[s, e, b], r1r.at[s, e, b], dev)

    def rs1_half(s, e):
        (near, dev), _ = ways(s, e)
        rs1(s, e, 1, kd, dev).start()
        rs1(s, e, 0, near, dev).start()

    def rs2(s, e, dev):
        return rc(LX.at[s, e, 1], LY.at[s, e], r2s.at[s, e], r2r.at[s, e], dev)

    def rs2_half(s, e):
        _, (far, dev) = ways(s, e)
        rs1(s, e, 1, far, dev).wait_recv()
        mine = grad(s)[rows_at(far, RC), cols_at(e, piece(s)[1])].astype(F32)
        LX[s, e, 1] = (LX[s, e, 1].astype(F32) + mine).astype(BF16)
        rs2(s, e, dev).start()

    def rs3(s, e):
        near = z + 1 - 2 * li
        return rc(LX.at[s, e, 0], PZ.at[s], pzs.at[s], pzr.at[s], (d, near))

    def rs3_half(s, e):
        rs1(s, e, 0, k, xdev).wait_recv()
        rs2(s, e, ydev).wait_recv()
        mine = grad(s)[rows_at(k, RC), cols_at(e, piece(s)[1])].astype(F32)
        LX[s, e, 0] = (LX[s, e, 0].astype(F32) + LY[s, e].astype(F32) + mine).astype(BF16)

        @pl.when(li != e)
        def _():
            rs3(s, e).start()

    def to_owner(s, a):
        slot = jnp.where(core == own, 0, 1)
        src = LX.at[s, li, 0, pl.ds(a * R, R)]
        return src, slot, rc(src, ZL.at[s, slot], zss.at[s, a], zsr.at[s, slot], (2 * k + a, 2 * core + li))

    def rs3_second(s):
        rs3(s, 0).wait_recv()
        LX[s, li, 0] = (LX[s, li, 0].astype(F32) + PZ[s].astype(F32)).astype(BF16)
        for a in range(2):
            here = (core == a) & (core == own)

            @pl.when(here)
            def _(a=a):
                src, slot, _ = to_owner(s, a)
                pltpu.make_async_copy(src, ZL.at[s, slot], zsr.at[s, slot]).start()

            @pl.when(jnp.logical_not(here))
            def _(a=a):
                to_owner(s, a)[2].start()

    def rs1_start(s):
        for e in range(2):
            rs1_half(s, e)

    def rs2_start(s):
        for e in range(2):
            rs2_half(s, e)

    def rs3_start(s):
        for e in range(2):
            rs3_half(s, e)

    def rs4(s):
        j, col = piece(s)
        total = jnp.zeros((R, SUB), F32)
        for slot in range(2):
            src = LX.at[s, 0, 0, pl.ds(0, R)]
            rc(src, ZL.at[s, slot], zss.at[s, 0], zsr.at[s, slot], sib).wait_recv()
            total = total + ZL[s, slot].astype(F32)
        cols = pl.ds(col, SUB)
        gbuf = (ga_out, up_m, down_m)[j]
        gbuf[:, cols] = total
        pltpu.make_async_copy(gbuf.at[:, cols], g_out.at[j, :, cols], loc.at[10 + j]).start()
        return total

    def rs_drain(s):
        for e in range(2):
            for b in range(2):
                rs1(s, e, b, k, xdev).wait_send()
            rs2(s, e, ydev).wait_send()
        rs3(s, 0).wait_send()
        for a in range(2):

            @pl.when(jnp.logical_not((core == a) & (core == own)))
            def _(a=a):
                to_owner(s, a)[2].wait_send()

    PARTS = 4
    PR = T // 4 // PARTS

    def out_part(ref, which, qi, part, slot):
        src = stage.at[pl.ds(pl.multiple_of(qi * (T // 4) + part * PR, PR), PR), :]
        dst = ref.at[slot, pl.ds(part * PR, PR), :]
        return src, dst, out_s.at[which, qi, part], out_r.at[which, slot, part]

    def out_here(qi):
        return (core == own) & (li == qi)

    def out_start(ref, which, qi, parts=range(PARTS)):
        @pl.when(out_here(qi))
        def _():
            for part in parts:
                src, dst, _, rs = out_part(ref, which, qi, part, li)
                pltpu.make_async_copy(src, dst, rs).start()

        @pl.when(jnp.logical_not(out_here(qi)))
        def _():
            for part in parts:
                rc(*out_part(ref, which, qi, part, li), (2 * k + own, 2 * core + qi)).start()

    def out_recv(ref, which, slot):
        for part in range(PARTS):
            rc(*out_part(ref, which, 0, part, slot), sib).wait_recv()

    def out_sent(ref, which):
        for qi in range(2):
            pl.when(out_here(qi))(functools.partial(out_recv, ref, which, qi))

            @pl.when(jnp.logical_not(out_here(qi)))
            def _(qi=qi):
                for part in range(PARTS):
                    rc(*out_part(ref, which, qi, part, 0), sib).wait_send()

    def out_wait(ref, which):
        for slot in range(2):
            pl.when(jnp.logical_not(out_here(slot)))(functools.partial(out_recv, ref, which, slot))

    def d2_copy(i):
        cols = pl.ds(pl.multiple_of(i * 256, 256), 256)
        return rc(h1.at[:, cols], dh2r.at[:, cols], d2_s.at[i], d2_r.at[i], sib)

    if inner:
        for s in range(3):
            ag_drain(s)

    for i3 in range(3):
        if inner:
            if i3 == 0:
                ag3_start(5)
                ag2_start(7)
            if i3 == 1:
                ag3_start(7)
                rs1_start(3)
                rs1_start(4)
            ag_wait(3 + 2 * i3)
            ag_wait(4 + 2 * i3)
        wide_cols = [cols_at(e, SUB * i3) for e in range(2)]

        def hidden(e, carry, i3=i3):
            cols = cols_at(e, SUB * i3)
            here = pl.ds(pl.multiple_of(e * SUB, SUB), SUB)
            u = dot(h2[...], W[1, :, cols])
            dz = dot(cc[...], W[2, :, cols])
            cumulative = 0.5 * (1.0 + lax.erf(u * INV_ROOT_TWO))
            slope = cumulative + u * jnp.exp(-0.5 * u * u) * INV_ROOT_TWO_PI
            zb[:, here] = (u * cumulative).astype(BF16)
            du[:, here] = (dz * slope).astype(BF16)
            return carry

        run("hidden", 2, hidden)
        if inner and i3 == 2:
            rs2_start(3)
            rs1_start(5)

        def back_two(i, carry, i3=i3, wide_cols=wide_cols):
            cols = pl.ds(pl.multiple_of(i * 256, 256), 256)
            v = dot_t(du[:, 0:SUB], W[1, cols, wide_cols[0]]) + dot_t(du[:, SUB : 2 * SUB], W[1, cols, wide_cols[1]])
            if i3 > 0:
                v = v + dh2[:, cols]
            dh2[:, cols] = v
            if i3 == 2:
                h1[:, cols] = v.astype(BF16)
                d2_copy(i).start()
            return carry

        run("back_two", D // 256, back_two)

        def ffn_part(i, carry, i3=i3, wide_cols=wide_cols):
            cols = pl.ds(pl.multiple_of(i * 256, 256), 256)
            f = dot_t(zb[:, 0:SUB], W[2, cols, wide_cols[0]]) + dot_t(zb[:, SUB : 2 * SUB], W[2, cols, wide_cols[1]])
            if i3 > 0:
                f = f + facc[:, cols]
            facc[:, cols] = f
            return carry

        run("ffn_part", D // 256, ffn_part)
        if inner and i3 == 0:
            ag3_start(6)
        if inner:
            ag_drain(3 + 2 * i3)
            ag_drain(4 + 2 * i3)

        def grad_ffn(e, carry, i3=i3):
            here = pl.ds(pl.multiple_of(e * SUB, SUB), SUB)
            W[1, :, cols_at(e, SUB * i3)] = dot(h2T[...], du[:, here]).astype(BF16)
            W[2, :, cols_at(e, SUB * i3)] = dot(cT[...], zb[:, here]).astype(BF16)
            return carry

        run("grad_ffn", 2, grad_ffn)

    other = 1 - core

    def half_rows(which, i):
        return pl.ds(pl.multiple_of(which * HALF + i * TB, TB), TB)

    def f_copy():
        return rc(fsend, frecv, f_s.at[0], f_r.at[0], sib)

    def ffn_other(i, carry):
        fsend[at(i), :] = facc[half_rows(other, i), :].astype(BF16)
        return carry

    run("ffn_other", NB // 2, ffn_other)
    f_copy().start()
    if inner:
        rs2_start(4)
        rs1_start(6)

    gn_out[...] = jnp.zeros_like(gn_out)

    for i in range(D // 256):
        d2_copy(i).wait()

    def norm_back_two(i, carry):
        rows = at(i)
        e2 = dh2[rows, :] + dh2r[rows, :].astype(F32)
        n, r = normalize(x1[rows, :])
        m = e2 * nw[2:3, :]
        dx = cc[rows, :].astype(F32) + r * (m - row_mean(m) - n * row_mean(m * n))
        dh2[rows, :] = dx
        low_dx = dx.astype(BF16)
        h2[rows, :] = low_dx
        h2T[:, rows] = low_dx.T
        count = jnp.where(i // (NB // 2) == core, 1.0, 0.0)
        gn_out[2:3, :] += count * jnp.sum(e2 * n, axis=0, keepdims=True)
        gn_out[3:4, :] += count * jnp.sum(e2, axis=0, keepdims=True)
        return carry

    run("norm_back_two", NB, norm_back_two)
    da, daT, doe = h2, h2T, cc
    if inner:
        rs3_start(3)

    parts = [dot(da[...], W[0, :, e * 768 + 512 : e * 768 + 768]) for e in range(2)]
    for i in range(NB):
        rows = slice(i * TB, i * TB + TB)
        for e in range(2):
            zb[rows, e * 256 : e * 256 + 256] = wide_o(opair, e, rows)
        singles = jnp.where(low, pltpu.roll(parts[0][rows, :128], 64, 1), parts[1][rows, :128])
        pairs = [parts[0][rows, 128:], parts[1][rows, 128:], singles]
        for p in range(3):
            g = pairs[p].astype(BF16).astype(F32)
            prod = g * opair[p, rows, :].astype(F32)
            for half in range(2):
                mine = head_lanes(lane, half)
                base = HD - HD * half
                hh = 2 * p + half
                delta = jnp.sum(jnp.where(mine, prod, 0.0), axis=-1, keepdims=True)
                hi, mid, lo = three_parts(delta)
                extra = spare_columns(lane, base + 1, (-hi, -mid, -lo), 0.0)
                doe[rows, hh * 128 : hh * 128 + 128] = jnp.where(mine, g, extra).astype(BF16)
    if inner:
        rs2_start(5)
        rs1_start(7)
    f_copy().wait()

    def ffn_final(i, carry):
        rows = half_rows(core, i)
        y = x1[rows, :] + facc[rows, :] + frecv[at(i), :].astype(F32)
        stage[at(i), :] = y.astype(BF16)
        out_start(lo_out, 0, i)
        return carry

    run("ffn_final", NB // 2, ffn_final)


    def back_keys(p, i):
        rows = at(i)
        cos, sin = cos_ref[rows, :], sin_ref[rows, :]
        dks, dvs = [], []
        for half in range(2):
            hh = 2 * p + half
            sT = dot_t(ke[hh, rows, :], qe[hh])
            pT = jnp.exp(sT)
            do = doe[:, hh * 128 : hh * 128 + 128]
            dpT = dot_t(ve[hh, rows, :], do)
            dsT = (pT * dpT).astype(BF16)
            dvs.append(dot(pT.astype(BF16), do))
            dks.append(dot(dsT, qe[hh]))
            part = dot(kT[p, half * HD : half * HD + HD, rows], dsT)
            dqT[half * HD : half * HD + HD, :] += part
        dk = rope_back(jnp.where(low, dks[0], dks[1]), cos, sin, first)
        dv = jnp.where(low, dvs[0], dvs[1])
        put_draw(p, rows, None, dk, dv)

    def put_draw(p, rows, dq, dk, dv):
        if p < 2:
            for i, v in enumerate((dq, dk, dv)):
                if v is not None:
                    du[rows, p * 768 + 128 * i : p * 768 + 128 * i + 128] = v.astype(BF16)
            return
        if dk is not None:
            du[rows, 640:768] = dk.astype(BF16)
            du[rows, 512:640] = jnp.where(low, dv, 0.0).astype(BF16)
            du[rows, 768 + 512 : 768 + 640] = jnp.where(low, pltpu.roll(dv, 64, 1), 0.0).astype(BF16)
        if dq is not None:
            dk = du[rows, 640:768].astype(F32)
            du[rows, 384:512] = jnp.where(low, dq, pltpu.roll(dk, 64, 1)).astype(BF16)
            du[rows, 768 + 384 : 768 + 512] = jnp.where(low, pltpu.roll(dq, 64, 1), dk).astype(BF16)

    def put_queries(p):
        def block(i, carry):
            rows = at(i)
            cos, sin = cos_ref[rows, :], sin_ref[rows, :]
            dq = dqT[:, rows].T * HD**-0.5
            put_draw(p, rows, rope_back(dq, cos, sin, first), None, None)
            return carry

        run("put_queries", NB, block)

    def back_pair(p, pumps):
        dqT[...] = jnp.zeros_like(dqT)

        def pump(i, half):
            if inner:
                for step in range(NB // 2):
                    if 2 * step + half in pumps:
                        pl.when(i == step)(pumps[2 * step + half])

        def back_step(i, carry):
            back_keys(p, 2 * i)
            pump(i, 0)
            back_keys(p, 2 * i + 1)
            pump(i, 1)
            return carry

        run("back_step", NB // 2, back_step)
        put_queries(p)

    def several(*steps):
        def go():
            for f, *of in steps:
                f(*of)

        return go

    back_pair(2, {1: several((rs2_start, 6)), 3: several((rs1_start, 8), (rs3_start, 4), (rs3_second, 3))})

    def grad_attn_two(e, carry):
        b = e * 768
        for col in (384, 512):
            here = pl.ds(pl.multiple_of(b + col, 128), 128)
            v = dot(h1T[...], du[:, here])
            if col == 512:
                wide = dot(daT[...], zb[:, pl.ds(pl.multiple_of(e * 256, 256), 256)])
                GA[:, pl.ds(pl.multiple_of(b + 640, 128), 128)] = wide[:, 128:].astype(BF16)
                v = v + wide[:, :128]
            GA[:, here] = v.astype(BF16)
        return carry

    run("grad_attn", 2, grad_attn_two)
    if inner:
        rs1_start(2)

    def grad_attn(p):
        def one(i, carry, b=p * 768):
            GA[:, b : b + 384] = dot(h1T[...], du[:, b : b + 384]).astype(BF16)
            return carry

        run("grad_attn", 1, one)

    back_pair(0, {0: several((rs2_start, 7)), 2: several((rs3_start, 5), (rs3_second, 4))})
    grad_attn(0)
    squares_ref[...] = jnp.zeros_like(squares_ref)

    def four(s):
        g = rs4(s)
        squares_ref[...] += g * g

    if inner:
        rs1_half(0, 0)
        rs1_half(1, 0)
    back_pair(
        1,
        {
            0: several((rs2_start, 8), (four, 3)),
            1: several((rs3_start, 6), (rs3_second, 5)),
            2: several((four, 4)),
            3: several((rs2_half, 0, 0), (rs2_half, 1, 0), (rs3_start, 7), (rs3_second, 6)),
        },
    )
    grad_attn(1)
    if inner:
        rs1_half(0, 1)
        rs1_half(1, 1)

    def back_one(rows):
        return dot_t(du[rows, 0:640], W[0, :, 0:640]) + dot_t(du[rows, 768 : 768 + 640], W[0, :, 768 : 768 + 640])

    def d1_copy():
        return rc(fsend, drecv, d1_s.at[0], d1_r.at[0], sib)

    def one_other(i, carry):
        fsend[...] = back_one(pl.ds(pl.multiple_of(other * HALF, HALF), HALF)).astype(BF16)
        return carry

    run("one_other", 1, one_other)
    d1_copy().start()
    if inner:
        rs2_start(2)
        rs3_start(8)

    def one_mine(i, carry):
        rows = pl.ds(pl.multiple_of(core * HALF, HALF), HALF)
        x1[rows, :] = back_one(rows)
        return carry

    run("one_mine", 1, one_mine)
    if inner:
        rs3_second(7)

    d1_copy().wait()

    def norm_back_one(i, carry):
        rows = half_rows(core, i)
        e1 = x1[rows, :] + drecv[at(i), :].astype(F32)
        n, r = normalize(xs[rows, :].astype(F32))
        m = e1 * nw[0:1, :]
        dx = dh2[rows, :] + r * (m - row_mean(m) - n * row_mean(m * n))
        stage[at(i), :] = dx.astype(BF16)
        gn_out[0:1, :] += jnp.sum(e1 * n, axis=0, keepdims=True)
        gn_out[1:2, :] += jnp.sum(e1, axis=0, keepdims=True)
        return carry

    out_sent(lo_out, 0)
    run("norm_back_one", 1, norm_back_one)
    out_start(ig_out, 1, 0, range(2))
    run("norm_back_one", NB // 2 - 1, lambda i, carry: norm_back_one(i + 1, carry))

    def sum_first(l1, which):
        return [rc(l1.at[0], l1.at[slot], e_s.at[which, slot], e_r.at[which, slot], dev) for slot, dev in column]

    def sum_plane(l2, which):
        return [rc(l2.at[0], l2.at[1 + i], e_s.at[which, 8 + i], e_r.at[which, 8 + i], dev) for i, dev in enumerate(plane)]

    def sum_all():
        return [rc(sl.at[0], sl.at[slot], q_s.at[slot], q_r.at[slot], dev) for slot, dev in far]

    def sum_start(ref, l1, l2, which):
        l1[0] = ref[...]
        for copy in sum_first(l1, which):
            copy.start()

    def sum_second(l1, l2, which):
        for copy in sum_first(l1, which):
            copy.wait()
        total = l1[0]
        for slot in range(1, 8):
            total = total + l1[slot]
        l2[0] = total
        for copy in sum_plane(l2, which):
            copy.start()

    def sum_end(ref, l1, l2, which):
        for copy in sum_plane(l2, which):
            copy.wait()
        total = l2[0]
        for i in range(1, 4):
            total = total + l2[i]
        ref[...] = total

    if inner:
        sum_start(gn_out, gl1, gl2, 0)
        rs2_half(0, 1)
        rs2_half(1, 1)
        rs3_start(2)
        rs3_half(0, 0)
        rs3_half(1, 0)
    out_start(ig_out, 1, 0, range(2, 4))
    if inner:
        for s in range(5, 8):
            four(s)
        rs3_half(0, 1)
        rs3_half(1, 1)
        rs3_second(8)
        rs3_second(2)
    out_start(ig_out, 1, 1, range(1))
    if inner:
        sum_second(gl1, gl2, 0)
        rs3_second(0)
        rs3_second(1)
    out_start(ig_out, 1, 1, range(1, 4))
    if inner:
        four(8)
        four(2)
        four(0)
        four(1)
        total = jnp.sum(squares_ref[...], axis=0, keepdims=True)
        total = total[:, :128] + total[:, 128:]
        sl[0] = total
        for copy in sum_all():
            copy.start()
        sum_end(gn_out, gl1, gl2, 0)

        def drain_rs(s, carry):
            rs_drain(s)
            return carry

        for s in range(3):
            rs_drain(s)
        lax.fori_loop(3, PIECES, drain_rs, 0)
        for copy in sum_all():
            copy.wait()
        gn_out[4:5, 0:128] = jnp.sum(sl[...], axis=0)
        for j, gbuf in enumerate((ga_out, up_m, down_m)):
            pltpu.make_async_copy(gbuf, g_out.at[j], loc.at[10 + j]).wait()
    else:
        for j in range(3):
            g_copy = pltpu.make_async_copy(GA if j == 0 else W.at[j], g_out.at[j], loc.at[3 + j])
            g_copy.start()
            g_copy.wait()
    small_copy = pltpu.make_async_copy(gn_out, small_out, loc.at[13])
    small_copy.start()
    small_copy.wait()
    out_wait(lo_out, 0)
    out_sent(ig_out, 1)
    out_wait(ig_out, 1)

    @pl.when(core == own)
    def _():
        for i in range(3):
            in_remote(i).wait_send()


def rope_tables(length):
    places = np.arange(length, dtype=np.float32)
    rates = (ROPE_BASE ** (-(np.arange(HD // 2, dtype=np.float32) * 2.0 / HD))).astype(np.float32)
    angles = places[:, None] * rates[None, :]
    cos = np.tile(np.cos(angles), (1, 4)).astype(np.float32)
    sin = np.tile(np.sin(angles), (1, 4)).astype(np.float32)
    first = (np.arange(128) % HD < HD // 2)[None, :]
    return np.stack([cos, np.where(first, -sin, sin)]).astype(np.float32)


def adam_update(refs, outs, gradient, clip_factor, step_rate, decay_rate):
    master, first_old, second_old = (ref[...] for ref in refs)
    clipped = gradient * clip_factor
    first_new = BETA_FIRST * first_old + (1.0 - BETA_FIRST) * clipped
    second_new = BETA_SECOND * second_old + (1.0 - BETA_SECOND) * clipped * clipped
    fix_first = 1.0 - BETA_FIRST**STEP
    fix_second = 1.0 - BETA_SECOND**STEP
    normalized = first_new / fix_first / (jnp.sqrt(second_new / fix_second) + ADAM_EPSILON)
    master_new = master - step_rate * (normalized + decay_rate * master)
    for out, v in zip(outs, (master_new, first_new, second_new, master_new.astype(BF16))):
        out[...] = v


def update_kernel(R, shapes, g_in, small_in, lo_in, ig_in, *refs):
    param_ins, refs = refs[:15], refs[15:]
    lo_out, ig_out, norm_out = refs[:3]
    param_outs, refs = refs[3:23], refs[23:]
    g, small, params, outs, in_sems, out_sems = refs[0], refs[1], refs[2:17], refs[17:37], refs[37], refs[38]
    passing = [(lo_in, refs[39].at[0], lo_out), (ig_in, refs[39].at[1], ig_out)]
    copies = [pltpu.make_async_copy(src, via, in_sems.at[17 + i]) for i, (src, via, _) in enumerate(passing)]
    ins = [pltpu.make_async_copy(g_in, g, in_sems.at[15]), pltpu.make_async_copy(small_in, small, in_sems.at[16])]
    ins += [pltpu.make_async_copy(src, dst, in_sems.at[i]) for i, (src, dst) in enumerate(zip(param_ins, params))]
    for copy in ins + copies:
        copy.start()
    for copy in ins + copies:
        copy.wait()
    copies = [pltpu.make_async_copy(via, dst, out_sems.at[20 + i]) for i, (_, via, dst) in enumerate(passing)]
    for copy in copies:
        copy.start()
    gn_all = small[0:4, :]
    squares = jnp.sum(small[4:5, 0:128], keepdims=True) + jnp.sum(gn_all * gn_all, keepdims=True)
    grad_norm = jnp.sqrt(squares)
    norm_out[...] = grad_norm
    clip_factor = jnp.minimum(1.0, CLIP_LIMIT / (grad_norm + 1e-06))

    def transposed(v):
        return jnp.concatenate([v, jnp.zeros((128 - R, v.shape[1]), F32)], axis=0).T[:, :R]

    a = g[0]
    g_proj = [jnp.concatenate([a[:, 128 * j : 128 * j + 128], a[:, 384 + 64 * j : 448 + 64 * j]], axis=1) for j in range(3)]
    g_out = transposed(jnp.concatenate([a[:, 640:], a[:, 576:640]], axis=1))
    D = gn_all.shape[1]
    first_row = lax.axis_index("dp") * R
    r_i = lax.broadcasted_iota(jnp.int32, (D, 128), 0)
    c_i = lax.broadcasted_iota(jnp.int32, (D, 128), 1)
    sel = jnp.where((r_i == c_i + first_row) & (c_i < R), 1.0, 0.0).astype(BF16)
    g_norm = sum(dot(part.astype(BF16), sel) for part in three_parts(small[...]))[:4, :R]

    def update(i, gradient, rate, decay, index=None):
        ins, results = params[3 * i : 3 * i + 3], outs[4 * i : 4 * i + 4]
        if index is not None:
            ins, results = [r.at[index] for r in ins], [r.at[index] for r in results]
        adam_update(ins, results, gradient, clip_factor, rate, decay)
        if index is None or index == 2:
            for n in range(4 * i, 4 * i + 4):
                copies.append(pltpu.make_async_copy(outs[n], param_outs[n], out_sems.at[n]))
                copies[-1].start()

    update(2, g[1], RATE_MATRIX, WEIGHT_DECAY)
    update(3, g[2], RATE_MATRIX, WEIGHT_DECAY)
    for j in range(3):
        update(0, g_proj[j], RATE_MATRIX, WEIGHT_DECAY, j)
    update(1, g_out, RATE_MATRIX, WEIGHT_DECAY)
    update(4, g_norm, RATE_NORM, 0.0)
    for copy in copies:
        copy.wait()


def per_device(
    inputs,
    cotangent,
    lengths,
    proj_master,
    proj_first,
    proj_second,
    out_master,
    out_first,
    out_second,
    up_master,
    up_first,
    up_second,
    down_master,
    down_first,
    down_second,
    norm_master,
    norm_first,
    norm_second,
):
    _, T, D = inputs.shape
    R = proj_master.shape[1]
    n_dp = lax.axis_size("dp")
    inner = n_dp == 8
    d = lax.axis_index("dp")
    z = lax.axis_index("head")
    core = d % 2
    if inner:
        norm_in = norm_master
        extra = (proj_master, out_master, up_master, down_master.T)
    else:
        out_t = out_master.T
        attn = jnp.concatenate(
            [proj_master[0, :, :128], proj_master[1, :, :128], proj_master[2, :, :128]]
            + [proj_master[0, :, 128:], proj_master[1, :, 128:], proj_master[2, :, 128:]]
            + [out_t[:, 128:], out_t[:, :128]],
            axis=1,
        )
        pack = jnp.stack([attn, up_master, down_master.T]).astype(BF16)
        norm_in = jnp.pad(lax.all_gather(norm_master, "dp", axis=1, tiled=True), ((0, 4), (0, 0)))
        norm_in = norm_in.astype(BF16).astype(F32)
        full = lax.all_gather(pack, "dp", axis=1, tiled=True)
        every = lax.all_gather(full, "head", axis=0)
        pair = lax.dynamic_slice_in_dim(every, 2 * core, 2, 0)
        w_in = jnp.concatenate([pair[0], pair[1]], axis=2)
        extra = (w_in,)

    hbm = pl.BlockSpec(memory_space=pltpu.HBM)
    dma = pltpu.SemaphoreType.DMA
    quarter = T // 4
    g_shape = (3, R, 768) if inner else (3, D, 1536)
    out_shape = (
        jax.ShapeDtypeStruct((2, quarter, D), BF16),
        jax.ShapeDtypeStruct((2, quarter, D), BF16),
        jax.ShapeDtypeStruct(g_shape, F32 if inner else BF16),
        jax.ShapeDtypeStruct((8, D), F32),
    )
    HALF = T // 2
    NB = T // 256
    bf = lambda *s: pltpu.VMEM(s, BF16)
    ff = lambda *s: pltpu.VMEM(s, F32)
    RC = 2 * R
    pieces = PIECES if inner else 1
    lx_rows = RC if inner else 16
    zl_rows = R if inner else 16
    RL = R if inner else 8
    scratch = [
        bf(3, D, 1536), bf(D, 1536), bf(T, D), bf(T, D), bf(D, T), bf(T, D), bf(D, T), bf(T, D), bf(D, T), ff(T, D),
        bf(6, T, 128), bf(6, T, 128), bf(6, T, 128), bf(3, 128, T),
        bf(3, T, 128), bf(3, T, 128), bf(2, D, 256), bf(T, 2 * SUB), bf(T, 1536), ff(T, D), bf(T, D), ff(128, T), ff(T, D),
        bf(HALF, D), bf(HALF, D), bf(HALF, D), bf(HALF, D),
        ff(8, 128), ff(8, 128), bf(3, zl_rows, 768), ff(8, D), ff(8, 8, 128), ff(8, 8, D), ff(4, 8, D), ff(4 * n_dp, 1, 128),
        bf(pieces, 2, 2, lx_rows, SUB), bf(pieces, 2, lx_rows, SUB), bf(pieces, lx_rows, SUB), bf(pieces, 2, zl_rows, SUB),
        dma((3,)), dma((3,)), dma((3,)), dma((3,)), dma((2,)), dma((2,)), dma((NB,)), dma((NB,)),
        dma((1,)), dma((1,)), dma((NB,)), dma((NB,)), dma((2, 2, 4)), dma((2, 2, 4)), dma((4,)), dma((4,)), dma((1, 11)), dma((1, 11)), dma((4 * n_dp,)), dma((4 * n_dp,)),
        dma((3,)), dma((3,)), dma((4, 4)), dma((4, 4)), bf(4, zl_rows, SUB),
        dma((pieces, 4)), dma((pieces, 4)), dma((pieces, 2, 3)), dma((pieces, 2, 3)),
        dma((pieces, 2, 2)), dma((pieces, 2, 2)), dma((pieces, 2)), dma((pieces, 2)), dma((pieces,)), dma((pieces,)), dma((pieces, 2)), dma((pieces, 2)),
        dma((14,)),
        ff(2, T, 128), ff(*norm_in.shape), ff(3, RL, 192), ff(192, RL), ff(RL, 768), ff(RL, 768), ff(8, D), ff(RL, 768), ff(RL, SUB),
    ]
    layer_out, input_grad, grads, small = pl.pallas_call(
        functools.partial(layer_kernel, inner, T, D, R),
        out_shape=out_shape,
        in_specs=[hbm, hbm, pl.BlockSpec(memory_space=pltpu.SMEM)] + [hbm] * (2 + len(extra)),
        out_specs=(hbm,) * 4,
        scratch_shapes=scratch,
        compiler_params=pltpu.CompilerParams(
            collective_id=0, has_side_effects=True, vmem_limit_bytes=63 * 2**20
        ),
        name="layer",
    )(inputs, cotangent, lengths, jnp.asarray(rope_tables(T)), norm_in, *extra)

    if not inner:
        spread = jnp.stack([grads[:, :, :768], grads[:, :, 768:]]).astype(F32)
        empty = jnp.zeros((4,) + spread.shape[1:], F32)
        spread = lax.dynamic_update_slice_in_dim(empty, spread, 2 * core, 0)
        mine = lax.psum_scatter(spread, "head", scatter_dimension=0, tiled=False)
        grads = lax.psum_scatter(mine, "dp", scatter_dimension=1, tiled=True)
        squares = lax.psum(jnp.sum(grads * grads), ("dp", "head"))
        small = lax.psum(small, ("dp", "head")).at[4, 0].set(squares)
    params = (
        (proj_master, proj_first, proj_second),
        (out_master, out_first, out_second),
        (up_master, up_first, up_second),
        (down_master.T, down_first.T, down_second.T),
        (norm_master, norm_first, norm_second),
    )
    shapes = []
    for group in params:
        shapes += [(v.shape, F32) for v in group] + [(group[0].shape, BF16)]
    out_shapes = [((2, quarter, D), BF16)] * 2 + [((1, 1), F32)] + shapes
    flat = [v for group in params for v in group]
    outs = pl.pallas_call(
        functools.partial(update_kernel, R, shapes),
        out_shape=tuple(jax.ShapeDtypeStruct(*v) for v in out_shapes),
        in_specs=[hbm] * 19,
        out_specs=tuple([hbm] * 2 + [pl.BlockSpec(memory_space=pltpu.VMEM)] + [hbm] * 20),
        scratch_shapes=[ff(*grads.shape), ff(8, D)]
        + [ff(*v.shape) for v in flat]
        + [pltpu.VMEM(*v) for v in shapes]
        + [dma((19,)), dma((22,)), bf(2, 2, quarter, D)],
        compiler_params=pltpu.CompilerParams(vmem_limit_bytes=63 * 2**20),
        name="update",
    )(grads, small, layer_out, input_grad, *flat)
    down = tuple(v.T for v in outs[15:19])
    return tuple(outs[:2]) + (outs[2].reshape(()),) + tuple(outs[3:15]) + down + tuple(outs[19:])


def solution(mesh):
    proj, wide, tall, norms = P(None, "dp", "head"), P("dp", "head"), P("head", "dp"), P(None, "dp")
    tokens = P("dp", None, None)
    placed = (tokens, tokens, P("dp")) + (proj,) * 3 + (tall,) * 3 + (wide,) * 3 + (tall,) * 3 + (norms,) * 3
    quarters = P("dp", "head", None)
    return jax.shard_map(
        per_device,
        mesh=mesh,
        in_specs=placed,
        out_specs=(quarters, quarters, P()) + (proj,) * 4 + (tall,) * 4 + (wide,) * 4 + (tall,) * 4 + (norms,) * 4,
        check_vma=False,
    )
```

```python
import functools

import jax
import jax.numpy as jnp
import numpy as np
from jax import lax
from jax.experimental import pallas as pl
from jax.experimental.pallas import tpu as pltpu
from jax.sharding import PartitionSpec as P

HD = 64
STEP = 5
LN_EPSILON = 1e-05
MASK_FILL = -1e30
ROPE_BASE = 10000.0
CLIP_LIMIT = 1.0
BETA_FIRST = 0.9
BETA_SECOND = 0.95
ADAM_EPSILON = 1e-08
WEIGHT_DECAY = 0.1
RATE_MATRIX = 0.03
RATE_NORM = 0.3
INV_ROOT_TWO = 0.7071067811865476
INV_ROOT_TWO_PI = 0.3989422804014327

F32 = jnp.float32
BF16 = jnp.bfloat16
MESH = pl.DeviceIdType.MESH
SUB = 256
PIECES = 9


SCHEDULE = {
    "bt1": (("first", 3),),
    "ch1": (("first", 5),),
    "bt2": (("first", 4),),
    "fp2": (("second", 3),),
    "fo": (("second", 5), ("first", 6), ("first", 8),),
    "bk21": (("plane", 5), ("second", 4),),
    "pq2": (("second", 8),),
    "ga2": (("first", 2),),
    "bk01": (("plane", 3), ("plane", 4), ("second", 6),),
    "bk03": (("second", 2),),
    "pq0": (("plane", 8), ("first", 7),),
    "bk11": (("pair", 4), ("plane", 2), ("pair", 5), ("plane", 6),),
    "bk12": (("pair", 8), ("second", 7), ("pair", 3),),
    "oo": (("first_half", 1, 0), ("pair", 2),),
    "om": (("first_half", 1, 1), ("first_half", 0, 0), ("plane", 7), ("first_half", 0, 1), ("pair", 6), ("owner", 8),),
    "n0": (("out", 3),),
    "n1": (
        ("owner", 5),
        ("second_half", 1, 1),
        ("pair", 7),
        ("out", 0),
        ("owner", 4),
        ("owner", 3),
        ("out", 7),
        ("owner", 2),
        ("second_half", 1, 0),
        ("out", 4),
        ("second_half", 0, 0),
        ("owner", 6),
        ("second_half", 0, 1),
        ("plane_half", 1, 1),
        ("out", 5),
        ("owner", 7),
        ("plane_half", 0, 1),
        ("out", 2),
        ("plane_half", 1, 0),
        ("plane_half", 0, 0),
        ("pair", 1),
        ("norms",),
        ("pair", 0),
        ("out", 6),
        ("owner", 1),
        ("out", 1),
        ("owner", 0),
    ),
}


def dot(a, b):
    return lax.dot_general(a, b, (((1,), (0,)), ((), ())), preferred_element_type=F32)


def dot_t(a, b):
    return lax.dot_general(a, b, (((1,), (1,)), ((), ())), preferred_element_type=F32)


def row_mean(v):
    return jnp.mean(v, axis=-1, keepdims=True)


def normalize(v):
    center = v - row_mean(v)
    inverse = lax.rsqrt(row_mean(center * center) + LN_EPSILON)
    return center * inverse, inverse


def lanes(rows):
    return lax.broadcasted_iota(jnp.int32, (rows, 128), 1)


def head_lanes(lane, half):
    return lane < HD if half == 0 else lane >= HD


def three_parts(col):
    hi = col.astype(BF16).astype(F32)
    mid = (col - hi).astype(BF16).astype(F32)
    return hi, mid, col - hi - mid


def spare_columns(lane, base, values, other):
    out = other
    for i, v in reversed(list(enumerate(values))):
        out = jnp.where(lane == base + i, v, out)
    return out


def turned(v, first):
    return jnp.where(first, pltpu.roll(v, 96, 1), pltpu.roll(v, 32, 1))


def rope(v, cos, sin, first):
    return v * cos + turned(v, first) * sin


def rope_back(v, cos, sin, first):
    return v * cos - turned(v, first) * sin


def run(name, count, body):
    with jax.named_scope(name):
        lax.fori_loop(0, count, body, 0)


def layer_kernel(inner, T, D, R, *refs):
    (
        x_in, ct_in, lens_in, tables_in, norm_in, *rest
    ) = refs
    if inner:
        *masters_in, lo_out, ig_out, g_out, small_out = rest[:8]
        rest = rest[8:]
    else:
        w_in, lo_out, ig_out, g_out, small_out = rest[:5]
        rest = rest[5:]
    (
        W, GA, xs, cc, cT, h1, h1T, h2, h2T, x1, qe, ke, ve, kT,
        opair, osib, wsib, zb, du, dh2, dh2r, dqT, facc, fsend, frecv, drecv, stage,
        lens_s, lens_v, pack, nw, nl, gl1, gl2, sl, LX, LY, PZ, ZL,
        in_s, in_r, o_s, o_r, ws_s, ws_r, d2_s, d2_r, f_s, f_r, d1_s, d1_r, out_s, out_r, n_s, n_r, e_s, e_r, q_s, q_r, las, lar, lbs, lbr, part,
        s1s, s1r, a2s, a2r, r1s, r1r, r2s, r2r, pzs, pzr, zss, zsr, loc,
        tables, norm_m, proj_m, out_m, up_m, down_m, gn_out, ga_out, squares_ref,
    ) = rest
    RC = 2 * R
    TB = 256
    NB = T // TB
    HALF = T // 2
    d = lax.axis_index("dp")
    z = lax.axis_index("head")
    core = d % 2
    k = d // 2
    own = z // 2
    li = z % 2
    sib = (d + 1 - 2 * core, z)
    master_copies = []
    if inner:
        for i, (src, dst) in enumerate(zip(masters_in, (proj_m, out_m, up_m, down_m))):
            master_copies.append(pltpu.make_async_copy(src, dst, loc.at[4 + i]))
    norm_copy = pltpu.make_async_copy(norm_in, norm_m, loc.at[8])
    table_copy = pltpu.make_async_copy(tables_in, tables, loc.at[9])
    for copy in master_copies + [norm_copy, table_copy]:
        copy.start()
    cos_ref, sin_ref = tables.at[0], tables.at[1]
    lens_s[...] = jnp.full((8, 128), lens_in[li].astype(F32))

    def rc(src, dst, ss, rs, dev):
        return pltpu.make_async_remote_copy(
            src_ref=src, dst_ref=dst, send_sem=ss, recv_sem=rs, device_id=dev, device_id_type=MESH
        )

    column = []
    for da in range(2):
        for dz in range(4):
            if da + dz > 0:
                dd = d if da == 0 else sib[0]
                column.append((da * 4 + dz, (dd, (z + dz) % 4)))
    if inner:
        kx = k + 1 - 2 * (k % 2)
        ky = (k + 2) % 4
        kd = 3 - k
        xdev = (2 * kx + core, z)
        ydev = (2 * ky + core, z)
        ddev = (2 * kd + core, z)
        plane = [xdev, ydev, ddev]
    else:
        plane = []
    far = []
    if inner:
        for dk in range(4):
            for da in range(2):
                for dz in range(4):
                    if dk + da + dz > 0:
                        far.append((dk * 8 + da * 4 + dz, (2 * ((k + dk) % 4) + (core + da) % 2, (z + dz) % 4)))
    everyone = [dev for _, dev in far] if inner else [dev for _, dev in column]
    barrier = pltpu.get_barrier_semaphore()
    for dev in everyone:
        pl.semaphore_signal(barrier, inc=1, device_id=dev, device_id_type=MESH)
    pl.semaphore_wait(barrier, len(everyone))

    def in_remote(i):
        src = (x_in.at[li], ct_in.at[li], lens_s)[i]
        dst = (xs, cc, lens_v)[i]
        return rc(src, dst, in_s.at[i], in_r.at[i], sib)

    def in_local(i):
        src = (x_in.at[li], ct_in.at[li], lens_s)[i]
        dst = (xs, cc, lens_v)[i]
        return pltpu.make_async_copy(src, dst, loc.at[i])

    @pl.when(core == own)
    def _():
        for i in (2, 0, 1):
            in_remote(i).start()
            in_local(i).start()

    def piece(s):
        if isinstance(s, int):
            if s < 3:
                return 0, SUB * s
            return 1 + (s - 3) % 2, SUB * ((s - 3) // 2)
        return 1 + (s - 3) % 2, pl.multiple_of(((s - 3) // 2) * SUB, SUB)

    def rows_at(block, size):
        return pl.ds(pl.multiple_of(block * size, 16), size)

    def cols_at(e, col):
        if isinstance(e, int) and isinstance(col, int):
            return pl.ds(e * 768 + col, SUB)
        return pl.ds(pl.multiple_of(e * 768 + col, 128), SUB)

    def ag1(s, dz, a, e, dev):
        j, col = piece(s)
        src = pack.at[j, :, pl.ds(col, SUB)]
        dst = W.at[j, rows_at(2 * k + a, R), cols_at(e, col)]
        return rc(src, dst, s1s.at[s, dz], s1r.at[s, a * 2 + e], dev)

    def ag1_start(s):
        j, col = piece(s)
        for dz in range(1, 4):
            ag1(s, dz, core, li, (2 * k + own, (z + dz) % 4)).start()

        @pl.when(core == own)
        def _():
            pltpu.make_async_copy(
                pack.at[j, :, pl.ds(col, SUB)], W.at[j, rows_at(d, R), cols_at(li, col)], s1r.at[s, core * 2 + li]
            ).start()

        @pl.when(core != own)
        def _():
            ag1(s, 0, core, li, sib).start()

    def ag2(s, e, to, rows, dev, slot):
        j, col = piece(s)
        region = W.at[j, rows_at(rows, RC), cols_at(e, col)]
        return rc(region, region, a2s.at[s, e, to], a2r.at[s, e, slot], dev)

    def ag2_start(s):
        for a in range(2):
            for e in range(2):
                ag1(s, 1, a, e, sib).wait_recv()
        for e in range(2):
            ag2(s, e, 0, k, xdev, 0).start()
            ag2(s, e, 1, k, ydev, 1).start()

    def ag3_start(s):
        ag2(s, 0, 2, kx, ydev, 0).wait_recv()
        ag2(s, 0, 2, kx, ydev, 2).start()
        ag2(s, 1, 2, ky, xdev, 1).wait_recv()
        ag2(s, 1, 2, ky, xdev, 2).start()

    def ag_wait(s):
        if s == LAST:
            last_wait()
            return
        ag2(s, 0, 1, ky, ydev, 1).wait_recv()
        ag2(s, 0, 2, kd, ydev, 2).wait_recv()
        ag2(s, 1, 0, kx, xdev, 0).wait_recv()
        ag2(s, 1, 2, kd, xdev, 2).wait_recv()

    LAST = PIECES - 1

    def last_first(i):
        src = pack.at[2, :, pl.ds(2 * SUB, SUB)]
        return rc(src, part.at[k], las.at[i], lar.at[i], plane[i])

    def last_second(dz, a, e, kk, dev):
        dst = W.at[2, rows_at(2 * kk + a, R), cols_at(e, 2 * SUB)]
        return rc(part.at[kk], dst, lbs.at[dz, kk], lbr.at[a * 2 + e, kk], dev)

    def last_start():
        part[k] = pack[2, :, 2 * SUB :]
        for i in range(3):
            last_first(i).start()

    def last_forward():
        for i in range(3):
            last_first(i).wait_recv()
        for kk in range(4):
            for dz in range(1, 4):
                last_second(dz, core, li, kk, (2 * k + own, (z + dz) % 4)).start()

            @pl.when(core == own)
            def _(kk=kk):
                dst = W.at[2, rows_at(2 * kk + core, R), cols_at(li, 2 * SUB)]
                pltpu.make_async_copy(part.at[kk], dst, lbr.at[core * 2 + li, kk]).start()

            @pl.when(core != own)
            def _(kk=kk):
                last_second(0, core, li, kk, sib).start()

    def last_wait():
        for kk in range(4):
            for a in range(2):
                for e in range(2):
                    last_second(1, a, e, kk, sib).wait_recv()

    def last_drain():
        for i in range(3):
            last_first(i).wait_send()
        for kk in range(4):
            for dz in range(1, 4):
                last_second(dz, core, li, kk, sib).wait_send()

            @pl.when(core != own)
            def _(kk=kk):
                last_second(0, core, li, kk, sib).wait_send()

    def ag_drain(s):
        if s == LAST:
            last_drain()
            return
        for dz in range(1, 4):
            ag1(s, dz, core, li, sib).wait_send()

        @pl.when(core != own)
        def _():
            ag1(s, 0, core, li, sib).wait_send()

        for e in range(2):
            for to in range(3):
                ag2(s, e, to, k, xdev, to).wait_send()

    if inner:
        for copy in master_copies[:2]:
            copy.wait()
        out_t = jnp.concatenate([out_m[...], jnp.zeros((192, 128 - R), F32)], axis=1).T[:R]
        tail_q, tail_k, tail_v = (proj_m[j, :, 128:192] for j in range(3))
        for j in range(3):
            pack[0, :, 128 * j : 128 * j + 128] = proj_m[j, :, :128].astype(BF16)
        pack[0, :, 384:512] = jnp.concatenate([tail_q, tail_k], axis=1).astype(BF16)
        pack[0, :, 512:640] = jnp.concatenate([tail_v, out_t[:, 128:]], axis=1).astype(BF16)
        pack[0, :, 640:768] = out_t[:, :128].astype(BF16)
        for s in range(3):
            ag1_start(s)
        norm_copy.wait()
        nl[pl.ds(d, 1)] = jnp.zeros((1, 8, 128), F32)
        nl[pl.ds(d, 1), 0:4, 0:R] = norm_m[...].astype(BF16).astype(F32).reshape(1, 4, R)
        rc(nl.at[pl.ds(d, 1)], nl.at[pl.ds(d, 1)], n_s.at[0], n_r.at[0], sib).start()
        for copy in master_copies[2:]:
            copy.wait()
        pack[1] = up_m[...].astype(BF16)
        pack[2] = down_m[...].astype(BF16)
        last_start()
        for s in range(3, LAST):
            ag1_start(s)
        rc(nl.at[pl.ds(d, 1)], nl.at[pl.ds(sib[0], 1)], n_s.at[0], n_r.at[0], sib).wait()
        for i, dev in enumerate(plane):
            rc(nl.at[pl.ds(2 * k, 2)], nl.at[pl.ds(2 * k, 2)], n_s.at[1 + i], n_r.at[1 + i], dev).start()
        ag2_start(0)
        last_forward()
    else:
        w_copy = pltpu.make_async_copy(w_in, W, loc.at[3])
        w_copy.start()

    @pl.when(core == own)
    def _():
        for i in range(3):
            in_local(i).wait()

    @pl.when(core != own)
    def _():
        for i in range(3):
            in_remote(i).wait_recv()

    if inner:
        for i, kk in enumerate((kx, ky, kd)):
            rc(nl.at[pl.ds(2 * kk, 2)], nl.at[pl.ds(2 * kk, 2)], n_s.at[1 + i], n_r.at[1 + i], plane[i]).wait()
        nw[...] = jnp.concatenate([nl[i][:, :R] for i in range(8)], axis=1)
    else:
        norm_copy.wait()
        nw[...] = norm_m[...]

    length = lens_v[0:1, 0:1]

    def row_valid(start, rows):
        ids = (lax.broadcasted_iota(jnp.int32, (rows, 1), 0) + start).astype(F32)
        return ids < length

    def at(i, size=TB):
        return pl.ds(pl.multiple_of(i * size, size), size)

    def norm_one(i, carry):
        rows = at(i)
        n, _ = normalize(xs[rows, :].astype(F32))
        h = (n * nw[0:1, :] + nw[1:2, :]).astype(BF16)
        h1[rows, :] = h
        h1T[:, rows] = h.T
        return carry

    def mask_cotangent(i, carry):
        rows = at(i)
        c = jnp.where(row_valid(i * TB, TB), cc[rows, :].astype(F32), 0.0).astype(BF16)
        cc[rows, :] = c
        cT[:, rows] = c.T
        return carry

    if inner:
        ag2_start(1)
    run("norm_one", NB, norm_one)
    if inner:
        ag3_start(0)
    run("mask_cotangent", NB, mask_cotangent)
    table_copy.wait()
    if inner:
        ag3_start(1)
        ag2_start(2)
        ag2_start(3)
        ag_wait(0)
        ag_wait(1)
    else:
        w_copy.wait()

    lane = lanes(TB)
    low = lane < HD
    first = lane % HD < HD // 2

    def make_pair(p):
        if p < 2:
            raw = dot(h1[...], W[0, :, p * 768 : p * 768 + 384])
        else:
            r0 = dot(h1[...], W[0, :, 384:640])
            r1 = dot(h1[...], W[0, :, 768 + 384 : 768 + 640])
        for i in range(NB):
            rows = slice(i * TB, i * TB + TB)
            cos, sin = cos_ref[rows, :], sin_ref[rows, :]
            if p < 2:
                q = rope(raw[rows, :128], cos, sin, first)
                kk = rope(raw[rows, 128:256], cos, sin, first)
                v = raw[rows, 256:]
            else:
                ra = rope(r0[rows, :128], cos, sin, first)
                rb = rope(r1[rows, :128], cos, sin, first)
                q = jnp.where(low, ra, pltpu.roll(rb, 64, 1))
                kk = jnp.where(low, pltpu.roll(ra, 64, 1), rb)
                v = jnp.where(low, r0[rows, 128:], pltpu.roll(r1[rows, 128:], 64, 1))
            q = q * HD**-0.5
            bias = jnp.where(row_valid(i * TB, TB), 0.0, MASK_FILL)
            kT[p, :, rows] = kk.astype(BF16).T
            for half in range(2):
                mine = head_lanes(lane, half)
                base = HD - HD * half
                hh = 2 * p + half
                qe[hh, rows, :] = jnp.where(mine, q, jnp.where(lane == base, 1.0, 0.0)).astype(BF16)
                ke[hh, rows, :] = jnp.where(mine, kk, jnp.where(lane == base, bias, 1.0)).astype(BF16)
                ve[hh, rows, :] = jnp.where(mine, v, 1.0).astype(BF16)

    def attend(p, i):
        units = [(at(2 * i + b), 2 * p + half, half) for b in range(2) for half in range(2)]
        scores = [dot_t(qe[hh, rows, :], ke[hh]) for rows, hh, _ in units]
        outs = []
        for (rows, hh, half), s in zip(units, scores):
            mine = head_lanes(lane, half)
            base = HD - HD * half
            top = jnp.max(s, axis=-1, keepdims=True)
            ex = jnp.exp(s - top).astype(BF16)
            o = dot(ex, ve[hh])
            total = o[:, base : base + 1]
            outs.append(o * (1.0 / total))
            hi, mid, lo = three_parts(top + jnp.log(total))
            extra = spare_columns(lane, base, (1.0, -hi, -mid, -lo), 0.0)
            qe[hh, rows, :] = jnp.where(mine, qe[hh, rows, :].astype(F32), extra).astype(BF16)
        for b in range(2):
            opair[p, units[2 * b][0], :] = jnp.where(low, outs[2 * b], outs[2 * b + 1]).astype(BF16)

    def o_copy(p):
        return rc(opair.at[p], osib.at[p], o_s.at[p], o_r.at[p], sib)

    def ws_copy(e):
        return rc(W.at[0, :, pl.ds(e * 768 + 512, 256)], wsib.at[e], ws_s.at[e], ws_r.at[e], sib)

    for p in range(3):
        if inner and p == 2:
            ag_wait(2)
        if p == 2:
            for e in range(2):
                ws_copy(e).start()
        make_pair(p)

        def attend_two(i, carry, p=p):
            attend(p, i)
            return carry

        run("attend_two", NB // 2, attend_two)
        o_copy(p).start()
        if inner:
            ag3_start(2 + p)
            ag2_start(4 + p)

    def wide_o(pairs, e, rows):
        single = pairs[2, rows, :].astype(F32)
        if e == 0:
            single = pltpu.roll(single, 64, 1)
        single = jnp.where(low, 0.0, single).astype(BF16)
        return jnp.concatenate([single, pairs[e, rows, :]], axis=1)

    for p in range(3):
        o_copy(p).wait()
    for e in range(2):
        ws_copy(e).wait()

    def widen(i, carry):
        rows = at(i)
        for e in range(2):
            du[rows, e * 256 : e * 256 + 256] = wide_o(opair, e, rows)
            du[rows, e * 256 + 512 : e * 256 + 768] = wide_o(osib, e, rows)
        return carry

    run("widen", NB, widen)

    def project_out(i, carry):
        cols = pl.ds(pl.multiple_of(i * 256, 256), 256)
        acc = xs[:, cols].astype(F32)
        for e in range(2):
            acc = acc + dot_t(du[:, e * 256 : e * 256 + 256], W[0, cols, e * 768 + 512 : e * 768 + 768])
            acc = acc + dot_t(du[:, e * 256 + 512 : e * 256 + 768], wsib[e, cols, :])
        x1[:, cols] = acc
        return carry

    run("project_out", D // 256, project_out)

    def norm_two(i, carry):
        rows = at(i)
        n, _ = normalize(x1[rows, :])
        h = (n * nw[2:3, :] + nw[3:4, :]).astype(BF16)
        h2[rows, :] = h
        h2T[:, rows] = h.T
        return carry

    run("norm_two", NB, norm_two)

    def grad(s):
        return GA if isinstance(s, int) and s < 3 else W.at[piece(s)[0]]

    def ways(s, e):
        flip = isinstance(s, int) and s == 1
        one, two = ((kx, xdev), (ky, ydev)) if e == int(flip) else ((ky, ydev), (kx, xdev))
        return one, two

    def rs1(s, e, b, rows, dev):
        src = grad(s).at[rows_at(rows, RC), cols_at(e, piece(s)[1])]
        return rc(src, LX.at[s, e, b], r1s.at[s, e, b], r1r.at[s, e, b], dev)

    def rs1_half(s, e):
        (near, dev), _ = ways(s, e)
        rs1(s, e, 1, kd, dev).start()
        rs1(s, e, 0, near, dev).start()

    def rs2(s, e, dev):
        return rc(LX.at[s, e, 1], LY.at[s, e], r2s.at[s, e], r2r.at[s, e], dev)

    def rs2_half(s, e):
        _, (far, dev) = ways(s, e)
        rs1(s, e, 1, far, dev).wait_recv()
        mine = grad(s)[rows_at(far, RC), cols_at(e, piece(s)[1])].astype(F32)
        LX[s, e, 1] = (LX[s, e, 1].astype(F32) + mine).astype(BF16)
        rs2(s, e, dev).start()

    def rs3(s, e):
        near = z + 1 - 2 * li
        return rc(LX.at[s, e, 0], PZ.at[s], pzs.at[s], pzr.at[s], (d, near))

    def rs3_half(s, e):
        rs1(s, e, 0, k, xdev).wait_recv()
        rs2(s, e, ydev).wait_recv()
        mine = grad(s)[rows_at(k, RC), cols_at(e, piece(s)[1])].astype(F32)
        LX[s, e, 0] = (LX[s, e, 0].astype(F32) + LY[s, e].astype(F32) + mine).astype(BF16)

        @pl.when(li != e)
        def _():
            rs3(s, e).start()

    def to_owner(s, a):
        slot = jnp.where(core == own, 0, 1)
        src = LX.at[s, li, 0, pl.ds(a * R, R)]
        return src, slot, rc(src, ZL.at[s, slot], zss.at[s, a], zsr.at[s, slot], (2 * k + a, 2 * core + li))

    def rs3_second(s):
        rs3(s, 0).wait_recv()
        LX[s, li, 0] = (LX[s, li, 0].astype(F32) + PZ[s].astype(F32)).astype(BF16)
        for a in range(2):
            here = (core == a) & (core == own)

            @pl.when(here)
            def _(a=a):
                src, slot, _ = to_owner(s, a)
                pltpu.make_async_copy(src, ZL.at[s, slot], zsr.at[s, slot]).start()

            @pl.when(jnp.logical_not(here))
            def _(a=a):
                to_owner(s, a)[2].start()

    def rs1_start(s):
        for e in range(2):
            rs1_half(s, e)

    def rs2_start(s):
        for e in range(2):
            rs2_half(s, e)

    def rs3_start(s):
        for e in range(2):
            rs3_half(s, e)

    def rs4(s):
        j, col = piece(s)
        total = jnp.zeros((R, SUB), F32)
        for slot in range(2):
            src = LX.at[s, 0, 0, pl.ds(0, R)]
            rc(src, ZL.at[s, slot], zss.at[s, 0], zsr.at[s, slot], sib).wait_recv()
            total = total + ZL[s, slot].astype(F32)
        cols = pl.ds(col, SUB)
        gbuf = (ga_out, up_m, down_m)[j]
        gbuf[:, cols] = total
        pltpu.make_async_copy(gbuf.at[:, cols], g_out.at[j, :, cols], loc.at[10 + j]).start()
        return total

    def rs_drain(s):
        for e in range(2):
            for b in range(2):
                rs1(s, e, b, k, xdev).wait_send()
            rs2(s, e, ydev).wait_send()
        rs3(s, 0).wait_send()
        for a in range(2):

            @pl.when(jnp.logical_not((core == a) & (core == own)))
            def _(a=a):
                to_owner(s, a)[2].wait_send()

    PARTS = 4
    PR = T // 4 // PARTS

    def out_part(ref, which, qi, part, slot):
        src = stage.at[pl.ds(pl.multiple_of(qi * (T // 4) + part * PR, PR), PR), :]
        dst = ref.at[slot, pl.ds(part * PR, PR), :]
        return src, dst, out_s.at[which, qi, part], out_r.at[which, slot, part]

    def out_here(qi):
        return (core == own) & (li == qi)

    def out_start(ref, which, qi, parts=range(PARTS)):
        @pl.when(out_here(qi))
        def _():
            for part in parts:
                src, dst, _, rs = out_part(ref, which, qi, part, li)
                pltpu.make_async_copy(src, dst, rs).start()

        @pl.when(jnp.logical_not(out_here(qi)))
        def _():
            for part in parts:
                rc(*out_part(ref, which, qi, part, li), (2 * k + own, 2 * core + qi)).start()

    def out_recv(ref, which, slot):
        for part in range(PARTS):
            rc(*out_part(ref, which, 0, part, slot), sib).wait_recv()

    def out_sent(ref, which):
        for qi in range(2):
            pl.when(out_here(qi))(functools.partial(out_recv, ref, which, qi))

            @pl.when(jnp.logical_not(out_here(qi)))
            def _(qi=qi):
                for part in range(PARTS):
                    rc(*out_part(ref, which, qi, part, 0), sib).wait_send()

    def out_wait(ref, which):
        for slot in range(2):
            pl.when(jnp.logical_not(out_here(slot)))(functools.partial(out_recv, ref, which, slot))

    def step(op, *of):
        if op == "out":
            out_start(ig_out, 1, of[0] // PARTS, (of[0] % PARTS,))
        elif op == "norms":
            sum_second(gl1, gl2, 0)
        else:
            {
                "first": rs1_start,
                "first_half": rs1_half,
                "second": rs2_start,
                "second_half": rs2_half,
                "plane": rs3_start,
                "plane_half": rs3_half,
                "pair": rs3_second,
                "owner": four,
            }[op](*of)

    def at_slot(name):
        if inner:
            for op in SCHEDULE.get(name, ()):
                step(*op)

    def four(s):
        g = rs4(s)
        squares_ref[...] += g * g

    squares_ref[...] = jnp.zeros_like(squares_ref)

    def half_of(i):
        return pl.ds(pl.multiple_of(i * HALF, HALF), HALF)

    def d2_copy(i):
        return rc(h1.at[half_of(i), :], dh2r.at[half_of(i), :], d2_s.at[i], d2_r.at[i], sib)

    if inner:
        for s in range(3):
            ag_drain(s)

    for i3 in range(3):
        if inner:
            if i3 == 0:
                ag3_start(5)
                ag2_start(7)
            if i3 == 1:
                ag3_start(7)
                at_slot("start")
            ag_wait(3 + 2 * i3)
            ag_wait(4 + 2 * i3)
        wide_cols = [cols_at(e, SUB * i3) for e in range(2)]

        def hidden(e, carry, i3=i3):
            cols = cols_at(e, SUB * i3)
            here = pl.ds(pl.multiple_of(e * SUB, SUB), SUB)
            u = dot(h2[...], W[1, :, cols])
            dz = dot(cc[...], W[2, :, cols])
            cumulative = 0.5 * (1.0 + lax.erf(u * INV_ROOT_TWO))
            slope = cumulative + u * jnp.exp(-0.5 * u * u) * INV_ROOT_TWO_PI
            zb[:, here] = (u * cumulative).astype(BF16)
            du[:, here] = (dz * slope).astype(BF16)
            return carry

        run("hidden", 2, hidden)
        at_slot(f"hid{i3}")

        def back_two(i, carry, i3=i3, wide_cols=wide_cols):
            rows = half_of(i)
            v = dot_t(du[rows, 0:SUB], W[1, :, wide_cols[0]]) + dot_t(du[rows, SUB : 2 * SUB], W[1, :, wide_cols[1]])
            if i3 > 0:
                v = v + dh2[rows, :]
            dh2[rows, :] = v
            if i3 == 2:
                h1[rows, :] = v.astype(BF16)
                d2_copy(i).start()
            return carry

        run("back_two", 2, back_two)
        at_slot(f"bt{i3}")

        def ffn_part(i, carry, i3=i3, wide_cols=wide_cols):
            cols = pl.ds(pl.multiple_of(i * 256, 256), 256)
            f = dot_t(zb[:, 0:SUB], W[2, cols, wide_cols[0]]) + dot_t(zb[:, SUB : 2 * SUB], W[2, cols, wide_cols[1]])
            if i3 > 0:
                f = f + facc[:, cols]
            facc[:, cols] = f
            return carry

        run("ffn_part", D // 256, ffn_part)
        at_slot(f"fp{i3}")
        if inner and i3 == 0:
            ag3_start(6)
        if inner:
            ag_drain(3 + 2 * i3)
            ag_drain(4 + 2 * i3)

        def grad_ffn(e, carry, i3=i3):
            here = pl.ds(pl.multiple_of(e * SUB, SUB), SUB)
            W[1, :, cols_at(e, SUB * i3)] = dot(h2T[...], du[:, here]).astype(BF16)
            W[2, :, cols_at(e, SUB * i3)] = dot(cT[...], zb[:, here]).astype(BF16)
            return carry

        run("grad_ffn", 2, grad_ffn)
        at_slot(f"ch{i3}")

    other = 1 - core

    def half_rows(which, i):
        return pl.ds(pl.multiple_of(which * HALF + i * TB, TB), TB)

    def f_copy():
        return rc(fsend, frecv, f_s.at[0], f_r.at[0], sib)

    def ffn_other(i, carry):
        fsend[at(i), :] = facc[half_rows(other, i), :].astype(BF16)
        return carry

    run("ffn_other", NB // 2, ffn_other)
    f_copy().start()
    at_slot("fo")

    gn_out[...] = jnp.zeros_like(gn_out)

    def norm_back_two(i, carry):
        rows = at(i)
        e2 = dh2[rows, :] + dh2r[rows, :].astype(F32)
        n, r = normalize(x1[rows, :])
        m = e2 * nw[2:3, :]
        dx = cc[rows, :].astype(F32) + r * (m - row_mean(m) - n * row_mean(m * n))
        dh2[rows, :] = dx
        low_dx = dx.astype(BF16)
        h2[rows, :] = low_dx
        h2T[:, rows] = low_dx.T
        count = jnp.where(i // (NB // 2) == core, 1.0, 0.0)
        gn_out[2:3, :] += count * jnp.sum(e2 * n, axis=0, keepdims=True)
        gn_out[3:4, :] += count * jnp.sum(e2, axis=0, keepdims=True)
        return carry

    for i in range(2):
        d2_copy(i).wait()
        run("norm_back_two", NB // 2, lambda n, carry, i=i: norm_back_two(i * (NB // 2) + n, carry))
    da, daT, doe = h2, h2T, cc
    at_slot("nb2")

    parts = [dot(da[...], W[0, :, e * 768 + 512 : e * 768 + 768]) for e in range(2)]
    for i in range(NB):
        rows = slice(i * TB, i * TB + TB)
        for e in range(2):
            zb[rows, e * 256 : e * 256 + 256] = wide_o(opair, e, rows)
        singles = jnp.where(low, pltpu.roll(parts[0][rows, :128], 64, 1), parts[1][rows, :128])
        pairs = [parts[0][rows, 128:], parts[1][rows, 128:], singles]
        for p in range(3):
            g = pairs[p].astype(BF16).astype(F32)
            prod = g * opair[p, rows, :].astype(F32)
            for half in range(2):
                mine = head_lanes(lane, half)
                base = HD - HD * half
                hh = 2 * p + half
                delta = jnp.sum(jnp.where(mine, prod, 0.0), axis=-1, keepdims=True)
                hi, mid, lo = three_parts(delta)
                extra = spare_columns(lane, base + 1, (-hi, -mid, -lo), 0.0)
                doe[rows, hh * 128 : hh * 128 + 128] = jnp.where(mine, g, extra).astype(BF16)
    at_slot("do")
    f_copy().wait()

    def ffn_final(i, carry):
        rows = half_rows(core, i)
        y = x1[rows, :] + facc[rows, :] + frecv[at(i), :].astype(F32)
        stage[at(i), :] = y.astype(BF16)
        out_start(lo_out, 0, i)
        return carry

    run("ffn_final", NB // 2, ffn_final)
    at_slot("ff")


    def back_keys(p, i):
        rows = at(i)
        cos, sin = cos_ref[rows, :], sin_ref[rows, :]
        dks, dvs = [], []
        for half in range(2):
            hh = 2 * p + half
            sT = dot_t(ke[hh, rows, :], qe[hh])
            pT = jnp.exp(sT)
            do = doe[:, hh * 128 : hh * 128 + 128]
            dpT = dot_t(ve[hh, rows, :], do)
            dsT = (pT * dpT).astype(BF16)
            dvs.append(dot(pT.astype(BF16), do))
            dks.append(dot(dsT, qe[hh]))
            part = dot(kT[p, half * HD : half * HD + HD, rows], dsT)
            dqT[half * HD : half * HD + HD, :] += part
        dk = rope_back(jnp.where(low, dks[0], dks[1]), cos, sin, first)
        dv = jnp.where(low, dvs[0], dvs[1])
        put_draw(p, rows, None, dk, dv)

    def put_draw(p, rows, dq, dk, dv):
        if p < 2:
            for i, v in enumerate((dq, dk, dv)):
                if v is not None:
                    du[rows, p * 768 + 128 * i : p * 768 + 128 * i + 128] = v.astype(BF16)
            return
        if dk is not None:
            du[rows, 640:768] = dk.astype(BF16)
            du[rows, 512:640] = jnp.where(low, dv, 0.0).astype(BF16)
            du[rows, 768 + 512 : 768 + 640] = jnp.where(low, pltpu.roll(dv, 64, 1), 0.0).astype(BF16)
        if dq is not None:
            dk = du[rows, 640:768].astype(F32)
            du[rows, 384:512] = jnp.where(low, dq, pltpu.roll(dk, 64, 1)).astype(BF16)
            du[rows, 768 + 384 : 768 + 512] = jnp.where(low, pltpu.roll(dq, 64, 1), dk).astype(BF16)

    def put_queries(p):
        def block(i, carry):
            rows = at(i)
            cos, sin = cos_ref[rows, :], sin_ref[rows, :]
            dq = dqT[:, rows].T * HD**-0.5
            put_draw(p, rows, rope_back(dq, cos, sin, first), None, None)
            return carry

        run("put_queries", NB, block)

    def back_pair(p):
        dqT[...] = jnp.zeros_like(dqT)

        def between(i, half):
            for turn in range(NB // 2):
                slot = f"bk{p}{2 * turn + half}"
                if slot in SCHEDULE:
                    pl.when(i == turn)(functools.partial(at_slot, slot))

        def back_step(i, carry):
            back_keys(p, 2 * i)
            between(i, 0)
            back_keys(p, 2 * i + 1)
            between(i, 1)
            return carry

        run("back_step", NB // 2, back_step)
        put_queries(p)
        at_slot(f"pq{p}")

    back_pair(2)

    def grad_attn_two(e, carry):
        b = e * 768
        for col in (384, 512):
            here = pl.ds(pl.multiple_of(b + col, 128), 128)
            v = dot(h1T[...], du[:, here])
            if col == 512:
                wide = dot(daT[...], zb[:, pl.ds(pl.multiple_of(e * 256, 256), 256)])
                GA[:, pl.ds(pl.multiple_of(b + 640, 128), 128)] = wide[:, 128:].astype(BF16)
                v = v + wide[:, :128]
            GA[:, here] = v.astype(BF16)
        return carry

    run("grad_attn", 2, grad_attn_two)
    at_slot("ga2")

    def grad_attn(p):
        def one(i, carry, b=p * 768):
            GA[:, b : b + 384] = dot(h1T[...], du[:, b : b + 384]).astype(BF16)
            return carry

        run("grad_attn", 1, one)

    back_pair(0)
    grad_attn(0)
    at_slot("ga0")
    back_pair(1)
    grad_attn(1)
    at_slot("ga1")

    def back_one(rows):
        return dot_t(du[rows, 0:640], W[0, :, 0:640]) + dot_t(du[rows, 768 : 768 + 640], W[0, :, 768 : 768 + 640])

    def d1_copy(i):
        return rc(fsend.at[at(i), :], drecv.at[at(i), :], d1_s.at[i], d1_r.at[i], sib)

    def one_other(i, carry):
        fsend[...] = back_one(pl.ds(pl.multiple_of(other * HALF, HALF), HALF)).astype(BF16)
        return carry

    run("one_other", 1, one_other)
    for i in range(NB // 2):
        d1_copy(i).start()
    at_slot("oo")

    def one_mine(i, carry):
        rows = pl.ds(pl.multiple_of(core * HALF, HALF), HALF)
        x1[rows, :] = back_one(rows)
        return carry

    run("one_mine", 1, one_mine)
    at_slot("om")

    def norm_back_one(i, carry):
        rows = half_rows(core, i)
        e1 = x1[rows, :] + drecv[at(i), :].astype(F32)
        n, r = normalize(xs[rows, :].astype(F32))
        m = e1 * nw[0:1, :]
        dx = dh2[rows, :] + r * (m - row_mean(m) - n * row_mean(m * n))
        stage[at(i), :] = dx.astype(BF16)
        gn_out[0:1, :] += jnp.sum(e1 * n, axis=0, keepdims=True)
        gn_out[1:2, :] += jnp.sum(e1, axis=0, keepdims=True)
        return carry

    out_sent(lo_out, 0)
    d1_copy(0).wait()
    run("norm_back_one", 1, norm_back_one)
    at_slot("n0")
    for i in range(1, NB // 2):
        d1_copy(i).wait()
    run("norm_back_one", NB // 2 - 1, lambda i, carry: norm_back_one(i + 1, carry))

    def sum_first(l1, which):
        return [rc(l1.at[0], l1.at[slot], e_s.at[which, slot], e_r.at[which, slot], dev) for slot, dev in column]

    def sum_plane(l2, which):
        return [rc(l2.at[0], l2.at[1 + i], e_s.at[which, 8 + i], e_r.at[which, 8 + i], dev) for i, dev in enumerate(plane)]

    def sum_all():
        return [rc(sl.at[0], sl.at[slot], q_s.at[slot], q_r.at[slot], dev) for slot, dev in far]

    def sum_start(ref, l1, l2, which):
        l1[0] = jnp.concatenate([ref[0:4, : D // 2], ref[0:4, D // 2 :]], axis=0)
        for copy in sum_first(l1, which):
            copy.start()

    def sum_second(l1, l2, which):
        for copy in sum_first(l1, which):
            copy.wait()
        total = l1[0]
        for slot in range(1, 8):
            total = total + l1[slot]
        l2[0] = total
        for copy in sum_plane(l2, which):
            copy.start()

    def sum_end(ref, l1, l2, which):
        for copy in sum_plane(l2, which):
            copy.wait()
        total = l2[0]
        for i in range(1, 4):
            total = total + l2[i]
        ref[0:4, :] = jnp.concatenate([total[0:4], total[4:8]], axis=1)

    if inner:
        sum_start(gn_out, gl1, gl2, 0)
        at_slot("n1")
    else:
        out_start(ig_out, 1, 0)
        out_start(ig_out, 1, 1)
    if inner:
        total = jnp.sum(squares_ref[...], axis=0, keepdims=True)
        total = total[:, :128] + total[:, 128:]
        sl[0] = total
        for copy in sum_all():
            copy.start()
        sum_end(gn_out, gl1, gl2, 0)

        def drain_rs(s, carry):
            rs_drain(s)
            return carry

        for s in range(3):
            rs_drain(s)
        lax.fori_loop(3, PIECES, drain_rs, 0)
        for copy in sum_all():
            copy.wait()
        gn_out[4:5, 0:128] = jnp.sum(sl[...], axis=0)
        for j, gbuf in enumerate((ga_out, up_m, down_m)):
            pltpu.make_async_copy(gbuf, g_out.at[j], loc.at[10 + j]).wait()
    else:
        for j in range(3):
            g_copy = pltpu.make_async_copy(GA if j == 0 else W.at[j], g_out.at[j], loc.at[3 + j])
            g_copy.start()
            g_copy.wait()
    small_copy = pltpu.make_async_copy(gn_out, small_out, loc.at[13])
    small_copy.start()
    small_copy.wait()
    out_wait(lo_out, 0)
    out_sent(ig_out, 1)
    out_wait(ig_out, 1)

    @pl.when(core == own)
    def _():
        for i in range(3):
            in_remote(i).wait_send()


def rope_tables(length):
    places = np.arange(length, dtype=np.float32)
    rates = (ROPE_BASE ** (-(np.arange(HD // 2, dtype=np.float32) * 2.0 / HD))).astype(np.float32)
    angles = places[:, None] * rates[None, :]
    cos = np.tile(np.cos(angles), (1, 4)).astype(np.float32)
    sin = np.tile(np.sin(angles), (1, 4)).astype(np.float32)
    first = (np.arange(128) % HD < HD // 2)[None, :]
    return np.stack([cos, np.where(first, -sin, sin)]).astype(np.float32)


def adam_update(refs, outs, gradient, clip_factor, step_rate, decay_rate):
    master, first_old, second_old = (ref[...] for ref in refs)
    clipped = gradient * clip_factor
    first_new = BETA_FIRST * first_old + (1.0 - BETA_FIRST) * clipped
    second_new = BETA_SECOND * second_old + (1.0 - BETA_SECOND) * clipped * clipped
    fix_first = 1.0 - BETA_FIRST**STEP
    fix_second = 1.0 - BETA_SECOND**STEP
    normalized = first_new / fix_first / (jnp.sqrt(second_new / fix_second) + ADAM_EPSILON)
    master_new = master - step_rate * (normalized + decay_rate * master)
    for out, v in zip(outs, (master_new, first_new, second_new, master_new.astype(BF16))):
        out[...] = v


def update_kernel(R, shapes, g_in, small_in, lo_in, ig_in, *refs):
    param_ins, refs = refs[:15], refs[15:]
    lo_out, ig_out, norm_out = refs[:3]
    param_outs, refs = refs[3:23], refs[23:]
    g, small, params, outs, in_sems, out_sems = refs[0], refs[1], refs[2:17], refs[17:37], refs[37], refs[38]
    passing = [(lo_in, refs[39].at[0], lo_out), (ig_in, refs[39].at[1], ig_out)]
    copies = [pltpu.make_async_copy(src, via, in_sems.at[17 + i]) for i, (src, via, _) in enumerate(passing)]
    ins = [pltpu.make_async_copy(g_in, g, in_sems.at[15]), pltpu.make_async_copy(small_in, small, in_sems.at[16])]
    ins += [pltpu.make_async_copy(src, dst, in_sems.at[i]) for i, (src, dst) in enumerate(zip(param_ins, params))]
    for copy in ins[:2] + ins[8:11] + ins[11:] + ins[2:8] + copies:
        copy.start()
    for copy in ins[:2]:
        copy.wait()
    gn_all = small[0:4, :]
    squares = jnp.sum(small[4:5, 0:128], keepdims=True) + jnp.sum(gn_all * gn_all, keepdims=True)
    grad_norm = jnp.sqrt(squares)
    norm_out[...] = grad_norm
    clip_factor = jnp.minimum(1.0, CLIP_LIMIT / (grad_norm + 1e-06))

    def transposed(v):
        return jnp.concatenate([v, jnp.zeros((128 - R, v.shape[1]), F32)], axis=0).T[:, :R]

    a = g[0]
    g_proj = [jnp.concatenate([a[:, 128 * j : 128 * j + 128], a[:, 384 + 64 * j : 448 + 64 * j]], axis=1) for j in range(3)]
    g_out = transposed(jnp.concatenate([a[:, 640:], a[:, 576:640]], axis=1))
    D = gn_all.shape[1]
    first_row = lax.axis_index("dp") * R
    r_i = lax.broadcasted_iota(jnp.int32, (D, 128), 0)
    c_i = lax.broadcasted_iota(jnp.int32, (D, 128), 1)
    sel = jnp.where((r_i == c_i + first_row) & (c_i < R), 1.0, 0.0).astype(BF16)
    g_norm = sum(dot(part.astype(BF16), sel) for part in three_parts(small[...]))[:4, :R]

    arrivals = ins[2:]

    def update(i, gradient, rate, decay, index=None):
        ins, results = params[3 * i : 3 * i + 3], outs[4 * i : 4 * i + 4]
        if index is None or index == 0:
            for copy in arrivals[3 * i : 3 * i + 3]:
                copy.wait()
        if index is not None:
            ins, results = [r.at[index] for r in ins], [r.at[index] for r in results]
        adam_update(ins, results, gradient, clip_factor, rate, decay)
        if index is None or index == 2:
            for n in range(4 * i, 4 * i + 4):
                copies.append(pltpu.make_async_copy(outs[n], param_outs[n], out_sems.at[n]))
                copies[-1].start()

    update(2, g[1], RATE_MATRIX, WEIGHT_DECAY)
    update(3, g[2], RATE_MATRIX, WEIGHT_DECAY)
    for copy in copies[:2]:
        copy.wait()
    copies[:2] = [pltpu.make_async_copy(via, dst, out_sems.at[20 + i]) for i, (_, via, dst) in enumerate(passing)]
    for copy in copies[:2]:
        copy.start()
    for j in range(3):
        update(0, g_proj[j], RATE_MATRIX, WEIGHT_DECAY, j)
    update(1, g_out, RATE_MATRIX, WEIGHT_DECAY)
    update(4, g_norm, RATE_NORM, 0.0)
    for copy in copies:
        copy.wait()


def per_device(
    inputs,
    cotangent,
    lengths,
    proj_master,
    proj_first,
    proj_second,
    out_master,
    out_first,
    out_second,
    up_master,
    up_first,
    up_second,
    down_master,
    down_first,
    down_second,
    norm_master,
    norm_first,
    norm_second,
):
    _, T, D = inputs.shape
    R = proj_master.shape[1]
    n_dp = lax.axis_size("dp")
    inner = n_dp == 8
    d = lax.axis_index("dp")
    z = lax.axis_index("head")
    core = d % 2
    if inner:
        norm_in = norm_master
        extra = (proj_master, out_master, up_master, down_master.T)
    else:
        out_t = out_master.T
        attn = jnp.concatenate(
            [proj_master[0, :, :128], proj_master[1, :, :128], proj_master[2, :, :128]]
            + [proj_master[0, :, 128:], proj_master[1, :, 128:], proj_master[2, :, 128:]]
            + [out_t[:, 128:], out_t[:, :128]],
            axis=1,
        )
        pack = jnp.stack([attn, up_master, down_master.T]).astype(BF16)
        norm_in = jnp.pad(lax.all_gather(norm_master, "dp", axis=1, tiled=True), ((0, 4), (0, 0)))
        norm_in = norm_in.astype(BF16).astype(F32)
        full = lax.all_gather(pack, "dp", axis=1, tiled=True)
        every = lax.all_gather(full, "head", axis=0)
        pair = lax.dynamic_slice_in_dim(every, 2 * core, 2, 0)
        w_in = jnp.concatenate([pair[0], pair[1]], axis=2)
        extra = (w_in,)

    hbm = pl.BlockSpec(memory_space=pltpu.HBM)
    dma = pltpu.SemaphoreType.DMA
    quarter = T // 4
    g_shape = (3, R, 768) if inner else (3, D, 1536)
    out_shape = (
        jax.ShapeDtypeStruct((2, quarter, D), BF16),
        jax.ShapeDtypeStruct((2, quarter, D), BF16),
        jax.ShapeDtypeStruct(g_shape, F32 if inner else BF16),
        jax.ShapeDtypeStruct((8, D), F32),
    )
    HALF = T // 2
    NB = T // 256
    bf = lambda *s: pltpu.VMEM(s, BF16)
    ff = lambda *s: pltpu.VMEM(s, F32)
    RC = 2 * R
    pieces = PIECES if inner else 1
    lx_rows = RC if inner else 16
    zl_rows = R if inner else 16
    RL = R if inner else 8
    scratch = [
        bf(3, D, 1536), bf(D, 1536), bf(T, D), bf(T, D), bf(D, T), bf(T, D), bf(D, T), bf(T, D), bf(D, T), ff(T, D),
        bf(6, T, 128), bf(6, T, 128), bf(6, T, 128), bf(3, 128, T),
        bf(3, T, 128), bf(3, T, 128), bf(2, D, 256), bf(T, 2 * SUB), bf(T, 1536), ff(T, D), bf(T, D), ff(128, T), ff(T, D),
        bf(HALF, D), bf(HALF, D), bf(HALF, D), bf(HALF, D),
        ff(8, 128), ff(8, 128), bf(3, zl_rows, 768), ff(8, D), ff(8, 8, 128), ff(8, 8, D // 2), ff(4, 8, D // 2), ff(4 * n_dp, 1, 128),
        bf(pieces, 2, 2, lx_rows, SUB), bf(pieces, 2, lx_rows, SUB), bf(pieces, lx_rows, SUB), bf(pieces, 2, zl_rows, SUB),
        dma((3,)), dma((3,)), dma((3,)), dma((3,)), dma((2,)), dma((2,)), dma((NB,)), dma((NB,)),
        dma((1,)), dma((1,)), dma((NB,)), dma((NB,)), dma((2, 2, 4)), dma((2, 2, 4)), dma((4,)), dma((4,)), dma((1, 11)), dma((1, 11)), dma((4 * n_dp,)), dma((4 * n_dp,)),
        dma((3,)), dma((3,)), dma((4, 4)), dma((4, 4)), bf(4, zl_rows, SUB),
        dma((pieces, 4)), dma((pieces, 4)), dma((pieces, 2, 3)), dma((pieces, 2, 3)),
        dma((pieces, 2, 2)), dma((pieces, 2, 2)), dma((pieces, 2)), dma((pieces, 2)), dma((pieces,)), dma((pieces,)), dma((pieces, 2)), dma((pieces, 2)),
        dma((14,)),
        ff(2, T, 128), ff(*norm_in.shape), ff(3, RL, 192), ff(192, RL), ff(RL, 768), ff(RL, 768), ff(8, D), ff(RL, 768), ff(RL, SUB),
    ]
    layer_out, input_grad, grads, small = pl.pallas_call(
        functools.partial(layer_kernel, inner, T, D, R),
        out_shape=out_shape,
        in_specs=[hbm, hbm, pl.BlockSpec(memory_space=pltpu.SMEM)] + [hbm] * (2 + len(extra)),
        out_specs=(hbm,) * 4,
        scratch_shapes=scratch,
        compiler_params=pltpu.CompilerParams(
            collective_id=0, has_side_effects=True, vmem_limit_bytes=63 * 2**20
        ),
        name="layer",
    )(inputs, cotangent, lengths, jnp.asarray(rope_tables(T)), norm_in, *extra)

    if not inner:
        spread = jnp.stack([grads[:, :, :768], grads[:, :, 768:]]).astype(F32)
        empty = jnp.zeros((4,) + spread.shape[1:], F32)
        spread = lax.dynamic_update_slice_in_dim(empty, spread, 2 * core, 0)
        mine = lax.psum_scatter(spread, "head", scatter_dimension=0, tiled=False)
        grads = lax.psum_scatter(mine, "dp", scatter_dimension=1, tiled=True)
        squares = lax.psum(jnp.sum(grads * grads), ("dp", "head"))
        small = lax.psum(small, ("dp", "head")).at[4, 0].set(squares)
    params = (
        (proj_master, proj_first, proj_second),
        (out_master, out_first, out_second),
        (up_master, up_first, up_second),
        (down_master.T, down_first.T, down_second.T),
        (norm_master, norm_first, norm_second),
    )
    shapes = []
    for group in params:
        shapes += [(v.shape, F32) for v in group] + [(group[0].shape, BF16)]
    out_shapes = [((2, quarter, D), BF16)] * 2 + [((1, 1), F32)] + shapes
    flat = [v for group in params for v in group]
    outs = pl.pallas_call(
        functools.partial(update_kernel, R, shapes),
        out_shape=tuple(jax.ShapeDtypeStruct(*v) for v in out_shapes),
        in_specs=[hbm] * 19,
        out_specs=tuple([hbm] * 2 + [pl.BlockSpec(memory_space=pltpu.VMEM)] + [hbm] * 20),
        scratch_shapes=[ff(*grads.shape), ff(8, D)]
        + [ff(*v.shape) for v in flat]
        + [pltpu.VMEM(*v) for v in shapes]
        + [dma((19,)), dma((22,)), bf(2, 2, quarter, D)],
        compiler_params=pltpu.CompilerParams(vmem_limit_bytes=63 * 2**20),
        name="update",
    )(grads, small, layer_out, input_grad, *flat)
    down = tuple(v.T for v in outs[15:19])
    return tuple(outs[:2]) + (outs[2].reshape(()),) + tuple(outs[3:15]) + down + tuple(outs[19:])


def solution(mesh):
    proj, wide, tall, norms = P(None, "dp", "head"), P("dp", "head"), P("head", "dp"), P(None, "dp")
    tokens = P("dp", None, None)
    placed = (tokens, tokens, P("dp")) + (proj,) * 3 + (tall,) * 3 + (wide,) * 3 + (tall,) * 3 + (norms,) * 3
    quarters = P("dp", "head", None)
    return jax.shard_map(
        per_device,
        mesh=mesh,
        in_specs=placed,
        out_specs=(quarters, quarters, P()) + (proj,) * 4 + (tall,) * 4 + (wide,) * 4 + (tall,) * 4 + (norms,) * 4,
        check_vma=False,
    )
```

```python
import functools

import jax
import jax.numpy as jnp
import numpy as np
from jax import lax
from jax.experimental import pallas as pl
from jax.experimental.pallas import tpu as pltpu
from jax.sharding import PartitionSpec as P

HD = 64
STEP = 5
LN_EPSILON = 1e-05
MASK_FILL = -1e30
ROPE_BASE = 10000.0
CLIP_LIMIT = 1.0
BETA_FIRST = 0.9
BETA_SECOND = 0.95
ADAM_EPSILON = 1e-08
WEIGHT_DECAY = 0.1
RATE_MATRIX = 0.03
RATE_NORM = 0.3
INV_ROOT_TWO = 0.7071067811865476
INV_ROOT_TWO_PI = 0.3989422804014327

F32 = jnp.float32
BF16 = jnp.bfloat16
MESH = pl.DeviceIdType.MESH
SUB = 256
PIECES = 9


SCHEDULE = {
    "bt1": (("first", 3),),
    "ch1": (("first", 5),),
    "bt2": (("first", 4),),
    "fp2": (("second", 3),),
    "fo": (("second", 5), ("first", 6), ("first", 8),),
    "bk21": (("plane", 5), ("second", 4),),
    "pq2": (("second", 8),),
    "ga2": (("first", 2),),
    "bk01": (("plane", 3), ("plane", 4), ("second", 6),),
    "bk03": (("second", 2),),
    "pq0": (("plane", 8), ("first", 7),),
    "bk11": (("pair", 4), ("plane", 2), ("pair", 5), ("plane", 6),),
    "bk12": (("pair", 8), ("second", 7), ("pair", 3),),
    "oo": (("first_half", 1, 0), ("pair", 2),),
    "om": (("first_half", 1, 1), ("first_half", 0, 0), ("plane", 7), ("first_half", 0, 1), ("pair", 6), ("owner", 8),),
    "n0": (("out", 3),),
    "n1": (
        ("owner", 5),
        ("second_half", 1, 1),
        ("pair", 7),
        ("out", 0),
        ("owner", 4),
        ("owner", 3),
        ("out", 7),
        ("owner", 2),
        ("second_half", 1, 0),
        ("out", 4),
        ("second_half", 0, 0),
        ("owner", 6),
        ("second_half", 0, 1),
        ("plane_half", 1, 1),
        ("out", 5),
        ("owner", 7),
        ("plane_half", 0, 1),
        ("out", 2),
        ("plane_half", 1, 0),
        ("plane_half", 0, 0),
        ("pair", 1),
        ("norms",),
        ("pair", 0),
        ("out", 6),
        ("owner", 1),
        ("out", 1),
        ("owner", 0),
    ),
}


def dot(a, b):
    return lax.dot_general(a, b, (((1,), (0,)), ((), ())), preferred_element_type=F32)


def dot_t(a, b):
    return lax.dot_general(a, b, (((1,), (1,)), ((), ())), preferred_element_type=F32)


def row_mean(v):
    return jnp.mean(v, axis=-1, keepdims=True)


def normalize(v):
    center = v - row_mean(v)
    inverse = lax.rsqrt(row_mean(center * center) + LN_EPSILON)
    return center * inverse, inverse


def lanes(rows):
    return lax.broadcasted_iota(jnp.int32, (rows, 128), 1)


def head_lanes(lane, half):
    return lane < HD if half == 0 else lane >= HD


def three_parts(col):
    hi = col.astype(BF16).astype(F32)
    mid = (col - hi).astype(BF16).astype(F32)
    return hi, mid, col - hi - mid


def spare_columns(lane, base, values, other):
    out = other
    for i, v in reversed(list(enumerate(values))):
        out = jnp.where(lane == base + i, v, out)
    return out


def turned(v, first):
    return jnp.where(first, pltpu.roll(v, 96, 1), pltpu.roll(v, 32, 1))


def rope(v, cos, sin, first):
    return v * cos + turned(v, first) * sin


def rope_back(v, cos, sin, first):
    return v * cos - turned(v, first) * sin


def run(name, count, body):
    with jax.named_scope(name):
        lax.fori_loop(0, count, body, 0)


def layer_kernel(inner, T, D, R, *refs):
    (
        x_in, ct_in, lens_in, tables_in, norm_in, *rest
    ) = refs
    if inner:
        *masters_in, lo_out, ig_out, g_out, small_out = rest[:8]
        rest = rest[8:]
    else:
        w_in, lo_out, ig_out, g_out, small_out = rest[:5]
        rest = rest[5:]
    (
        W, GA, xs, cc, cT, h1, h1T, h2, h2T, x1, qe, ke, ve, kT,
        opair, osib, wsib, zb, du, dh2, dh2r, dqT, facc, fsend, frecv, drecv, stage,
        lens_s, lens_v, pack, nw, nl, gl1, gl2, sl, LX, LY, PZ, ZL,
        in_s, in_r, o_s, o_r, ws_s, ws_r, d2_s, d2_r, f_s, f_r, d1_s, d1_r, out_s, out_r, n_s, n_r, e_s, e_r, q_s, q_r, las, lar, lbs, lbr, part,
        s1s, s1r, a2s, a2r, r1s, r1r, r2s, r2r, pzs, pzr, zss, zsr, loc,
        tables, norm_m, proj_m, out_m, up_m, down_m, gn_out, ga_out, squares_ref,
    ) = rest
    RC = 2 * R
    TB = 256
    NB = T // TB
    HALF = T // 2
    d = lax.axis_index("dp")
    z = lax.axis_index("head")
    core = d % 2
    k = d // 2
    own = z // 2
    li = z % 2
    sib = (d + 1 - 2 * core, z)
    master_copies = []
    if inner:
        for i, (src, dst) in enumerate(zip(masters_in, (proj_m, out_m, up_m, down_m))):
            master_copies.append(pltpu.make_async_copy(src, dst, loc.at[4 + i]))
    norm_copy = pltpu.make_async_copy(norm_in, norm_m, loc.at[8])
    table_copy = pltpu.make_async_copy(tables_in, tables, loc.at[9])
    for copy in master_copies + [norm_copy, table_copy]:
        copy.start()
    cos_ref, sin_ref = tables.at[0], tables.at[1]
    lens_s[...] = jnp.full((8, 128), lens_in[li].astype(F32))

    def rc(src, dst, ss, rs, dev):
        return pltpu.make_async_remote_copy(
            src_ref=src, dst_ref=dst, send_sem=ss, recv_sem=rs, device_id=dev, device_id_type=MESH
        )

    column = []
    for da in range(2):
        for dz in range(4):
            if da + dz > 0:
                dd = d if da == 0 else sib[0]
                column.append((da * 4 + dz, (dd, (z + dz) % 4)))
    if inner:
        kx = k + 1 - 2 * (k % 2)
        ky = (k + 2) % 4
        kd = 3 - k
        xdev = (2 * kx + core, z)
        ydev = (2 * ky + core, z)
        ddev = (2 * kd + core, z)
        plane = [xdev, ydev, ddev]
    else:
        plane = []
    far = []
    if inner:
        for dk in range(4):
            for da in range(2):
                for dz in range(4):
                    if dk + da + dz > 0:
                        far.append((dk * 8 + da * 4 + dz, (2 * ((k + dk) % 4) + (core + da) % 2, (z + dz) % 4)))
    everyone = [dev for _, dev in far] if inner else [dev for _, dev in column]
    barrier = pltpu.get_barrier_semaphore()
    for dev in everyone:
        pl.semaphore_signal(barrier, inc=1, device_id=dev, device_id_type=MESH)
    pl.semaphore_wait(barrier, len(everyone))

    def in_remote(i):
        src = (x_in.at[li], ct_in.at[li], lens_s)[i]
        dst = (xs, cc, lens_v)[i]
        return rc(src, dst, in_s.at[i], in_r.at[i], sib)

    def in_local(i):
        src = (x_in.at[li], ct_in.at[li], lens_s)[i]
        dst = (xs, cc, lens_v)[i]
        return pltpu.make_async_copy(src, dst, loc.at[i])

    @pl.when(core == own)
    def _():
        for i in (2, 0, 1):
            in_remote(i).start()
            in_local(i).start()

    def piece(s):
        if isinstance(s, int):
            if s < 3:
                return 0, SUB * s
            return 1 + (s - 3) % 2, SUB * ((s - 3) // 2)
        return 1 + (s - 3) % 2, pl.multiple_of(((s - 3) // 2) * SUB, SUB)

    def rows_at(block, size):
        return pl.ds(pl.multiple_of(block * size, 16), size)

    def cols_at(e, col):
        if isinstance(e, int) and isinstance(col, int):
            return pl.ds(e * 768 + col, SUB)
        return pl.ds(pl.multiple_of(e * 768 + col, 128), SUB)

    def ag1(s, dz, a, e, dev):
        j, col = piece(s)
        src = pack.at[j, :, pl.ds(col, SUB)]
        dst = W.at[j, rows_at(2 * k + a, R), cols_at(e, col)]
        return rc(src, dst, s1s.at[s, dz], s1r.at[s, a * 2 + e], dev)

    def ag1_start(s):
        j, col = piece(s)
        for dz in range(1, 4):
            ag1(s, dz, core, li, (2 * k + own, (z + dz) % 4)).start()

        @pl.when(core == own)
        def _():
            pltpu.make_async_copy(
                pack.at[j, :, pl.ds(col, SUB)], W.at[j, rows_at(d, R), cols_at(li, col)], s1r.at[s, core * 2 + li]
            ).start()

        @pl.when(core != own)
        def _():
            ag1(s, 0, core, li, sib).start()

    def ag2(s, e, to, rows, dev, slot):
        j, col = piece(s)
        region = W.at[j, rows_at(rows, RC), cols_at(e, col)]
        return rc(region, region, a2s.at[s, e, to], a2r.at[s, e, slot], dev)

    def ag2_start(s):
        for a in range(2):
            for e in range(2):
                ag1(s, 1, a, e, sib).wait_recv()
        for e in range(2):
            ag2(s, e, 0, k, xdev, 0).start()
            ag2(s, e, 1, k, ydev, 1).start()

    def ag3_start(s):
        ag2(s, 0, 2, kx, ydev, 0).wait_recv()
        ag2(s, 0, 2, kx, ydev, 2).start()
        ag2(s, 1, 2, ky, xdev, 1).wait_recv()
        ag2(s, 1, 2, ky, xdev, 2).start()

    def ag_wait(s):
        if s == LAST:
            last_wait()
            return
        ag2(s, 0, 1, ky, ydev, 1).wait_recv()
        ag2(s, 0, 2, kd, ydev, 2).wait_recv()
        ag2(s, 1, 0, kx, xdev, 0).wait_recv()
        ag2(s, 1, 2, kd, xdev, 2).wait_recv()

    LAST = PIECES - 1

    def last_first(i):
        src = pack.at[2, :, pl.ds(2 * SUB, SUB)]
        return rc(src, part.at[k], las.at[i], lar.at[i], plane[i])

    def last_second(dz, a, e, kk, dev):
        dst = W.at[2, rows_at(2 * kk + a, R), cols_at(e, 2 * SUB)]
        return rc(part.at[kk], dst, lbs.at[dz, kk], lbr.at[a * 2 + e, kk], dev)

    def last_start():
        part[k] = pack[2, :, 2 * SUB :]
        for i in range(3):
            last_first(i).start()

    def last_forward():
        for i in range(3):
            last_first(i).wait_recv()
        for kk in range(4):
            for dz in range(1, 4):
                last_second(dz, core, li, kk, (2 * k + own, (z + dz) % 4)).start()

            @pl.when(core == own)
            def _(kk=kk):
                dst = W.at[2, rows_at(2 * kk + core, R), cols_at(li, 2 * SUB)]
                pltpu.make_async_copy(part.at[kk], dst, lbr.at[core * 2 + li, kk]).start()

            @pl.when(core != own)
            def _(kk=kk):
                last_second(0, core, li, kk, sib).start()

    def last_wait():
        for kk in range(4):
            for a in range(2):
                for e in range(2):
                    last_second(1, a, e, kk, sib).wait_recv()

    def last_drain():
        for i in range(3):
            last_first(i).wait_send()
        for kk in range(4):
            for dz in range(1, 4):
                last_second(dz, core, li, kk, sib).wait_send()

            @pl.when(core != own)
            def _(kk=kk):
                last_second(0, core, li, kk, sib).wait_send()

    def ag_drain(s):
        if s == LAST:
            last_drain()
            return
        for dz in range(1, 4):
            ag1(s, dz, core, li, sib).wait_send()

        @pl.when(core != own)
        def _():
            ag1(s, 0, core, li, sib).wait_send()

        for e in range(2):
            for to in range(3):
                ag2(s, e, to, k, xdev, to).wait_send()

    if inner:
        for copy in master_copies[:2]:
            copy.wait()
        out_t = jnp.concatenate([out_m[...], jnp.zeros((192, 128 - R), F32)], axis=1).T[:R]
        tail_q, tail_k, tail_v = (proj_m[j, :, 128:192] for j in range(3))
        for j in range(3):
            pack[0, :, 128 * j : 128 * j + 128] = proj_m[j, :, :128].astype(BF16)
        pack[0, :, 384:512] = jnp.concatenate([tail_q, tail_k], axis=1).astype(BF16)
        pack[0, :, 512:640] = jnp.concatenate([tail_v, out_t[:, 128:]], axis=1).astype(BF16)
        pack[0, :, 640:768] = out_t[:, :128].astype(BF16)
        for s in range(3):
            ag1_start(s)
        norm_copy.wait()
        nl[pl.ds(d, 1)] = jnp.zeros((1, 8, 128), F32)
        nl[pl.ds(d, 1), 0:4, 0:R] = norm_m[...].astype(BF16).astype(F32).reshape(1, 4, R)
        rc(nl.at[pl.ds(d, 1)], nl.at[pl.ds(d, 1)], n_s.at[0], n_r.at[0], sib).start()
        for copy in master_copies[2:]:
            copy.wait()
        pack[1] = up_m[...].astype(BF16)
        pack[2] = down_m[...].astype(BF16)
        last_start()
        for s in range(3, LAST):
            ag1_start(s)
        rc(nl.at[pl.ds(d, 1)], nl.at[pl.ds(sib[0], 1)], n_s.at[0], n_r.at[0], sib).wait()
        for i, dev in enumerate(plane):
            rc(nl.at[pl.ds(2 * k, 2)], nl.at[pl.ds(2 * k, 2)], n_s.at[1 + i], n_r.at[1 + i], dev).start()
        ag2_start(0)
        last_forward()
    else:
        w_copy = pltpu.make_async_copy(w_in, W, loc.at[3])
        w_copy.start()

    @pl.when(core == own)
    def _():
        for i in range(3):
            in_local(i).wait()

    @pl.when(core != own)
    def _():
        for i in range(3):
            in_remote(i).wait_recv()

    if inner:
        for i, kk in enumerate((kx, ky, kd)):
            rc(nl.at[pl.ds(2 * kk, 2)], nl.at[pl.ds(2 * kk, 2)], n_s.at[1 + i], n_r.at[1 + i], plane[i]).wait()
        nw[...] = jnp.concatenate([nl[i][:, :R] for i in range(8)], axis=1)
    else:
        norm_copy.wait()
        nw[...] = norm_m[...]

    length = lens_v[0:1, 0:1]

    def row_valid(start, rows):
        ids = (lax.broadcasted_iota(jnp.int32, (rows, 1), 0) + start).astype(F32)
        return ids < length

    def at(i, size=TB):
        return pl.ds(pl.multiple_of(i * size, size), size)

    def norm_one(i, carry):
        rows = at(i)
        n, _ = normalize(xs[rows, :].astype(F32))
        h = (n * nw[0:1, :] + nw[1:2, :]).astype(BF16)
        h1[rows, :] = h
        h1T[:, rows] = h.T
        return carry

    def mask_cotangent(i, carry):
        rows = at(i)
        c = jnp.where(row_valid(i * TB, TB), cc[rows, :].astype(F32), 0.0).astype(BF16)
        cc[rows, :] = c
        cT[:, rows] = c.T
        return carry

    if inner:
        ag2_start(1)
    run("norm_one", NB, norm_one)
    if inner:
        ag3_start(0)
    run("mask_cotangent", NB, mask_cotangent)
    table_copy.wait()
    if inner:
        ag3_start(1)
        ag2_start(2)
        ag2_start(3)
        ag_wait(0)
        ag_wait(1)
    else:
        w_copy.wait()

    lane = lanes(TB)
    low = lane < HD
    first = lane % HD < HD // 2

    def make_pair(p):
        if p < 2:
            raw = dot(h1[...], W[0, :, p * 768 : p * 768 + 384])
        else:
            r0 = dot(h1[...], W[0, :, 384:640])
            r1 = dot(h1[...], W[0, :, 768 + 384 : 768 + 640])
        for i in range(NB):
            rows = slice(i * TB, i * TB + TB)
            cos, sin = cos_ref[rows, :], sin_ref[rows, :]
            if p < 2:
                q = rope(raw[rows, :128], cos, sin, first)
                kk = rope(raw[rows, 128:256], cos, sin, first)
                v = raw[rows, 256:]
            else:
                ra = rope(r0[rows, :128], cos, sin, first)
                rb = rope(r1[rows, :128], cos, sin, first)
                q = jnp.where(low, ra, pltpu.roll(rb, 64, 1))
                kk = jnp.where(low, pltpu.roll(ra, 64, 1), rb)
                v = jnp.where(low, r0[rows, 128:], pltpu.roll(r1[rows, 128:], 64, 1))
            q = q * HD**-0.5
            bias = jnp.where(row_valid(i * TB, TB), 0.0, MASK_FILL)
            kT[p, :, rows] = kk.astype(BF16).T
            for half in range(2):
                mine = head_lanes(lane, half)
                base = HD - HD * half
                hh = 2 * p + half
                qe[hh, rows, :] = jnp.where(mine, q, jnp.where(lane == base, 1.0, 0.0)).astype(BF16)
                ke[hh, rows, :] = jnp.where(mine, kk, jnp.where(lane == base, bias, 1.0)).astype(BF16)
                ve[hh, rows, :] = jnp.where(mine, v, 1.0).astype(BF16)

    def attend(p, i):
        units = [(at(2 * i + b), 2 * p + half, half) for b in range(2) for half in range(2)]
        scores = [dot_t(qe[hh, rows, :], ke[hh]) for rows, hh, _ in units]
        outs = []
        for (rows, hh, half), s in zip(units, scores):
            mine = head_lanes(lane, half)
            base = HD - HD * half
            top = jnp.max(s, axis=-1, keepdims=True)
            ex = jnp.exp(s - top).astype(BF16)
            o = dot(ex, ve[hh])
            total = o[:, base : base + 1]
            outs.append(o * (1.0 / total))
            hi, mid, lo = three_parts(top + jnp.log(total))
            extra = spare_columns(lane, base, (1.0, -hi, -mid, -lo), 0.0)
            qe[hh, rows, :] = jnp.where(mine, qe[hh, rows, :].astype(F32), extra).astype(BF16)
        for b in range(2):
            opair[p, units[2 * b][0], :] = jnp.where(low, outs[2 * b], outs[2 * b + 1]).astype(BF16)

    def o_copy(p):
        return rc(opair.at[p], osib.at[p], o_s.at[p], o_r.at[p], sib)

    def ws_copy(e):
        return rc(W.at[0, :, pl.ds(e * 768 + 512, 256)], wsib.at[e], ws_s.at[e], ws_r.at[e], sib)

    for p in range(3):
        if inner and p == 2:
            ag_wait(2)
        if p == 2:
            for e in range(2):
                ws_copy(e).start()
        make_pair(p)

        def attend_two(i, carry, p=p):
            attend(p, i)
            return carry

        run("attend_two", NB // 2, attend_two)
        o_copy(p).start()
        if inner:
            ag3_start(2 + p)
            ag2_start(4 + p)

    def wide_o(pairs, e, rows):
        single = pairs[2, rows, :].astype(F32)
        if e == 0:
            single = pltpu.roll(single, 64, 1)
        single = jnp.where(low, 0.0, single).astype(BF16)
        return jnp.concatenate([single, pairs[e, rows, :]], axis=1)

    for p in range(3):
        o_copy(p).wait()
    for e in range(2):
        ws_copy(e).wait()

    def widen(i, carry):
        rows = at(i)
        for e in range(2):
            du[rows, e * 256 : e * 256 + 256] = wide_o(opair, e, rows)
            du[rows, e * 256 + 512 : e * 256 + 768] = wide_o(osib, e, rows)
        return carry

    run("widen", NB, widen)

    def project_out(i, carry):
        cols = pl.ds(pl.multiple_of(i * 256, 256), 256)
        acc = xs[:, cols].astype(F32)
        for e in range(2):
            acc = acc + dot_t(du[:, e * 256 : e * 256 + 256], W[0, cols, e * 768 + 512 : e * 768 + 768])
            acc = acc + dot_t(du[:, e * 256 + 512 : e * 256 + 768], wsib[e, cols, :])
        x1[:, cols] = acc
        return carry

    run("project_out", D // 256, project_out)

    def norm_two(i, carry):
        rows = at(i)
        n, _ = normalize(x1[rows, :])
        h = (n * nw[2:3, :] + nw[3:4, :]).astype(BF16)
        h2[rows, :] = h
        h2T[:, rows] = h.T
        return carry

    run("norm_two", NB, norm_two)

    def grad(s):
        return GA if isinstance(s, int) and s < 3 else W.at[piece(s)[0]]

    def ways(s, e):
        flip = isinstance(s, int) and s == 1
        one, two = ((kx, xdev), (ky, ydev)) if e == int(flip) else ((ky, ydev), (kx, xdev))
        return one, two

    def rs1(s, e, b, rows, dev):
        src = grad(s).at[rows_at(rows, RC), cols_at(e, piece(s)[1])]
        return rc(src, LX.at[s, e, b], r1s.at[s, e, b], r1r.at[s, e, b], dev)

    def rs1_half(s, e):
        (near, dev), _ = ways(s, e)
        rs1(s, e, 1, kd, dev).start()
        rs1(s, e, 0, near, dev).start()

    def rs2(s, e, dev):
        return rc(LX.at[s, e, 1], LY.at[s, e], r2s.at[s, e], r2r.at[s, e], dev)

    def rs2_half(s, e):
        _, (far, dev) = ways(s, e)
        rs1(s, e, 1, far, dev).wait_recv()
        mine = grad(s)[rows_at(far, RC), cols_at(e, piece(s)[1])].astype(F32)
        LX[s, e, 1] = (LX[s, e, 1].astype(F32) + mine).astype(BF16)
        rs2(s, e, dev).start()

    def rs3(s, e):
        near = z + 1 - 2 * li
        return rc(LX.at[s, e, 0], PZ.at[s], pzs.at[s], pzr.at[s], (d, near))

    def rs3_half(s, e):
        rs1(s, e, 0, k, xdev).wait_recv()
        rs2(s, e, ydev).wait_recv()
        mine = grad(s)[rows_at(k, RC), cols_at(e, piece(s)[1])].astype(F32)
        LX[s, e, 0] = (LX[s, e, 0].astype(F32) + LY[s, e].astype(F32) + mine).astype(BF16)

        @pl.when(li != e)
        def _():
            rs3(s, e).start()

    def to_owner(s, a):
        slot = jnp.where(core == own, 0, 1)
        src = LX.at[s, li, 0, pl.ds(a * R, R)]
        return src, slot, rc(src, ZL.at[s, slot], zss.at[s, a], zsr.at[s, slot], (2 * k + a, 2 * core + li))

    def rs3_second(s):
        rs3(s, 0).wait_recv()
        LX[s, li, 0] = (LX[s, li, 0].astype(F32) + PZ[s].astype(F32)).astype(BF16)
        for a in range(2):
            here = (core == a) & (core == own)

            @pl.when(here)
            def _(a=a):
                src, slot, _ = to_owner(s, a)
                pltpu.make_async_copy(src, ZL.at[s, slot], zsr.at[s, slot]).start()

            @pl.when(jnp.logical_not(here))
            def _(a=a):
                to_owner(s, a)[2].start()

    def rs1_start(s):
        for e in range(2):
            rs1_half(s, e)

    def rs2_start(s):
        for e in range(2):
            rs2_half(s, e)

    def rs3_start(s):
        for e in range(2):
            rs3_half(s, e)

    def rs4(s):
        j, col = piece(s)
        total = jnp.zeros((R, SUB), F32)
        for slot in range(2):
            src = LX.at[s, 0, 0, pl.ds(0, R)]
            rc(src, ZL.at[s, slot], zss.at[s, 0], zsr.at[s, slot], sib).wait_recv()
            total = total + ZL[s, slot].astype(F32)
        cols = pl.ds(col, SUB)
        gbuf = (ga_out, up_m, down_m)[j]
        gbuf[:, cols] = total
        pltpu.make_async_copy(gbuf.at[:, cols], g_out.at[j, :, cols], loc.at[10 + j]).start()
        return total

    def rs_drain(s):
        for e in range(2):
            for b in range(2):
                rs1(s, e, b, k, xdev).wait_send()
            rs2(s, e, ydev).wait_send()
        rs3(s, 0).wait_send()
        for a in range(2):

            @pl.when(jnp.logical_not((core == a) & (core == own)))
            def _(a=a):
                to_owner(s, a)[2].wait_send()

    PARTS = 4
    PR = T // 4 // PARTS

    def out_part(ref, which, qi, part, slot):
        src = stage.at[pl.ds(pl.multiple_of(qi * (T // 4) + part * PR, PR), PR), :]
        dst = ref.at[slot, pl.ds(part * PR, PR), :]
        return src, dst, out_s.at[which, qi, part], out_r.at[which, slot, part]

    def out_here(qi):
        return (core == own) & (li == qi)

    def out_start(ref, which, qi, parts=range(PARTS)):
        @pl.when(out_here(qi))
        def _():
            for part in parts:
                src, dst, _, rs = out_part(ref, which, qi, part, li)
                pltpu.make_async_copy(src, dst, rs).start()

        @pl.when(jnp.logical_not(out_here(qi)))
        def _():
            for part in parts:
                rc(*out_part(ref, which, qi, part, li), (2 * k + own, 2 * core + qi)).start()

    def out_recv(ref, which, slot):
        for part in range(PARTS):
            rc(*out_part(ref, which, 0, part, slot), sib).wait_recv()

    def out_sent(ref, which):
        for qi in range(2):
            pl.when(out_here(qi))(functools.partial(out_recv, ref, which, qi))

            @pl.when(jnp.logical_not(out_here(qi)))
            def _(qi=qi):
                for part in range(PARTS):
                    rc(*out_part(ref, which, qi, part, 0), sib).wait_send()

    def out_wait(ref, which):
        for slot in range(2):
            pl.when(jnp.logical_not(out_here(slot)))(functools.partial(out_recv, ref, which, slot))

    def step(op, *of):
        if op == "out":
            out_start(ig_out, 1, of[0] // PARTS, (of[0] % PARTS,))
        elif op == "norms":
            sum_second(gl1, gl2, 0)
        else:
            {
                "first": rs1_start,
                "first_half": rs1_half,
                "second": rs2_start,
                "second_half": rs2_half,
                "plane": rs3_start,
                "plane_half": rs3_half,
                "pair": rs3_second,
                "owner": four,
            }[op](*of)

    def at_slot(name):
        if inner:
            for op in SCHEDULE.get(name, ()):
                step(*op)

    def four(s):
        g = rs4(s)
        squares_ref[...] += g * g

    squares_ref[...] = jnp.zeros_like(squares_ref)

    def half_of(i):
        return pl.ds(pl.multiple_of(i * HALF, HALF), HALF)

    def d2_copy(i):
        return rc(h1.at[half_of(i), :], dh2r.at[half_of(i), :], d2_s.at[i], d2_r.at[i], sib)

    if inner:
        for s in range(3):
            ag_drain(s)

    for i3 in range(3):
        if inner:
            if i3 == 0:
                ag3_start(5)
                ag2_start(7)
            if i3 == 1:
                ag3_start(7)
                at_slot("start")
            ag_wait(3 + 2 * i3)
            ag_wait(4 + 2 * i3)
        wide_cols = [cols_at(e, SUB * i3) for e in range(2)]

        def hidden(e, carry, i3=i3):
            cols = cols_at(e, SUB * i3)
            here = pl.ds(pl.multiple_of(e * SUB, SUB), SUB)
            u = dot(h2[...], W[1, :, cols])
            dz = dot(cc[...], W[2, :, cols])
            cumulative = 0.5 * (1.0 + lax.erf(u * INV_ROOT_TWO))
            slope = cumulative + u * jnp.exp(-0.5 * u * u) * INV_ROOT_TWO_PI
            zb[:, here] = (u * cumulative).astype(BF16)
            du[:, here] = (dz * slope).astype(BF16)
            return carry

        run("hidden", 2, hidden)
        at_slot(f"hid{i3}")

        def back_two(i, carry, i3=i3, wide_cols=wide_cols):
            rows = half_of(i)
            v = dot_t(du[rows, 0:SUB], W[1, :, wide_cols[0]]) + dot_t(du[rows, SUB : 2 * SUB], W[1, :, wide_cols[1]])
            if i3 > 0:
                v = v + dh2[rows, :]
            dh2[rows, :] = v
            if i3 == 2:
                h1[rows, :] = v.astype(BF16)
                d2_copy(i).start()
            return carry

        run("back_two", 2, back_two)
        at_slot(f"bt{i3}")

        def ffn_part(i, carry, i3=i3, wide_cols=wide_cols):
            cols = pl.ds(pl.multiple_of(i * 256, 256), 256)
            f = dot_t(zb[:, 0:SUB], W[2, cols, wide_cols[0]]) + dot_t(zb[:, SUB : 2 * SUB], W[2, cols, wide_cols[1]])
            if i3 > 0:
                f = f + facc[:, cols]
            facc[:, cols] = f
            return carry

        run("ffn_part", D // 256, ffn_part)
        at_slot(f"fp{i3}")
        if inner and i3 == 0:
            ag3_start(6)
        if inner:
            ag_drain(3 + 2 * i3)
            ag_drain(4 + 2 * i3)

        def grad_ffn(e, carry, i3=i3):
            here = pl.ds(pl.multiple_of(e * SUB, SUB), SUB)
            W[1, :, cols_at(e, SUB * i3)] = dot(h2T[...], du[:, here]).astype(BF16)
            W[2, :, cols_at(e, SUB * i3)] = dot(cT[...], zb[:, here]).astype(BF16)
            return carry

        run("grad_ffn", 2, grad_ffn)
        at_slot(f"ch{i3}")

    other = 1 - core

    def half_rows(which, i):
        return pl.ds(pl.multiple_of(which * HALF + i * TB, TB), TB)

    def f_copy():
        return rc(fsend, frecv, f_s.at[0], f_r.at[0], sib)

    def ffn_other(i, carry):
        fsend[at(i), :] = facc[half_rows(other, i), :].astype(BF16)
        return carry

    run("ffn_other", NB // 2, ffn_other)
    f_copy().start()
    at_slot("fo")

    gn_out[...] = jnp.zeros_like(gn_out)

    def norm_back_two(i, carry):
        rows = at(i)
        for half in range(2):
            pl.when(i == half * (NB // 2))(lambda half=half: d2_copy(half).wait())
        e2 = dh2[rows, :] + dh2r[rows, :].astype(F32)
        n, r = normalize(x1[rows, :])
        m = e2 * nw[2:3, :]
        dx = cc[rows, :].astype(F32) + r * (m - row_mean(m) - n * row_mean(m * n))
        dh2[rows, :] = dx
        low_dx = dx.astype(BF16)
        h2[rows, :] = low_dx
        h2T[:, rows] = low_dx.T
        count = jnp.where(i // (NB // 2) == core, 1.0, 0.0)
        gn_out[2:3, :] += count * jnp.sum(e2 * n, axis=0, keepdims=True)
        gn_out[3:4, :] += count * jnp.sum(e2, axis=0, keepdims=True)
        return carry

    run("norm_back_two", NB, norm_back_two)
    da, daT, doe = h2, h2T, cc
    at_slot("nb2")

    parts = [dot(da[...], W[0, :, e * 768 + 512 : e * 768 + 768]) for e in range(2)]
    for i in range(NB):
        rows = slice(i * TB, i * TB + TB)
        for e in range(2):
            zb[rows, e * 256 : e * 256 + 256] = wide_o(opair, e, rows)
        singles = jnp.where(low, pltpu.roll(parts[0][rows, :128], 64, 1), parts[1][rows, :128])
        pairs = [parts[0][rows, 128:], parts[1][rows, 128:], singles]
        for p in range(3):
            g = pairs[p].astype(BF16).astype(F32)
            prod = g * opair[p, rows, :].astype(F32)
            for half in range(2):
                mine = head_lanes(lane, half)
                base = HD - HD * half
                hh = 2 * p + half
                delta = jnp.sum(jnp.where(mine, prod, 0.0), axis=-1, keepdims=True)
                hi, mid, lo = three_parts(delta)
                extra = spare_columns(lane, base + 1, (-hi, -mid, -lo), 0.0)
                doe[rows, hh * 128 : hh * 128 + 128] = jnp.where(mine, g, extra).astype(BF16)
    at_slot("do")
    f_copy().wait()

    def ffn_final(i, carry):
        rows = half_rows(core, i)
        y = x1[rows, :] + facc[rows, :] + frecv[at(i), :].astype(F32)
        stage[at(i), :] = y.astype(BF16)
        out_start(lo_out, 0, i)
        return carry

    run("ffn_final", NB // 2, ffn_final)
    at_slot("ff")


    def back_keys(p, i):
        rows = at(i)
        cos, sin = cos_ref[rows, :], sin_ref[rows, :]
        dks, dvs = [], []
        for half in range(2):
            hh = 2 * p + half
            sT = dot_t(ke[hh, rows, :], qe[hh])
            pT = jnp.exp(sT)
            do = doe[:, hh * 128 : hh * 128 + 128]
            dpT = dot_t(ve[hh, rows, :], do)
            dsT = (pT * dpT).astype(BF16)
            dvs.append(dot(pT.astype(BF16), do))
            dks.append(dot(dsT, qe[hh]))
            part = dot(kT[p, half * HD : half * HD + HD, rows], dsT)
            dqT[half * HD : half * HD + HD, :] += part
        dk = rope_back(jnp.where(low, dks[0], dks[1]), cos, sin, first)
        dv = jnp.where(low, dvs[0], dvs[1])
        put_draw(p, rows, None, dk, dv)

    def put_draw(p, rows, dq, dk, dv):
        if p < 2:
            for i, v in enumerate((dq, dk, dv)):
                if v is not None:
                    du[rows, p * 768 + 128 * i : p * 768 + 128 * i + 128] = v.astype(BF16)
            return
        if dk is not None:
            du[rows, 640:768] = dk.astype(BF16)
            du[rows, 512:640] = jnp.where(low, dv, 0.0).astype(BF16)
            du[rows, 768 + 512 : 768 + 640] = jnp.where(low, pltpu.roll(dv, 64, 1), 0.0).astype(BF16)
        if dq is not None:
            dk = du[rows, 640:768].astype(F32)
            du[rows, 384:512] = jnp.where(low, dq, pltpu.roll(dk, 64, 1)).astype(BF16)
            du[rows, 768 + 384 : 768 + 512] = jnp.where(low, pltpu.roll(dq, 64, 1), dk).astype(BF16)

    def put_queries(p):
        def block(i, carry):
            rows = at(i)
            cos, sin = cos_ref[rows, :], sin_ref[rows, :]
            dq = dqT[:, rows].T * HD**-0.5
            put_draw(p, rows, rope_back(dq, cos, sin, first), None, None)
            return carry

        run("put_queries", NB, block)

    def back_pair(p):
        dqT[...] = jnp.zeros_like(dqT)

        def back_step(i, carry):
            back_keys(p, i)
            for turn in range(NB):
                slot = f"bk{p}{turn}"
                if slot in SCHEDULE:
                    pl.when(i == turn)(functools.partial(at_slot, slot))
            return carry

        run("back_step", NB, back_step)
        put_queries(p)
        at_slot(f"pq{p}")

    back_pair(2)

    def grad_attn_two(e, carry):
        b = e * 768
        for col in (384, 512):
            here = pl.ds(pl.multiple_of(b + col, 128), 128)
            v = dot(h1T[...], du[:, here])
            if col == 512:
                wide = dot(daT[...], zb[:, pl.ds(pl.multiple_of(e * 256, 256), 256)])
                GA[:, pl.ds(pl.multiple_of(b + 640, 128), 128)] = wide[:, 128:].astype(BF16)
                v = v + wide[:, :128]
            GA[:, here] = v.astype(BF16)
        return carry

    run("grad_attn", 2, grad_attn_two)
    at_slot("ga2")

    def grad_attn(p):
        def one(i, carry, b=p * 768):
            GA[:, b : b + 384] = dot(h1T[...], du[:, b : b + 384]).astype(BF16)
            return carry

        run("grad_attn", 1, one)

    back_pair(0)
    grad_attn(0)
    at_slot("ga0")
    back_pair(1)
    grad_attn(1)
    at_slot("ga1")

    def back_one(rows):
        return dot_t(du[rows, 0:640], W[0, :, 0:640]) + dot_t(du[rows, 768 : 768 + 640], W[0, :, 768 : 768 + 640])

    def d1_copy(i):
        return rc(fsend.at[at(i), :], drecv.at[at(i), :], d1_s.at[i], d1_r.at[i], sib)

    def one_other(i, carry):
        fsend[...] = back_one(pl.ds(pl.multiple_of(other * HALF, HALF), HALF)).astype(BF16)
        return carry

    run("one_other", 1, one_other)
    for i in range(NB // 2):
        d1_copy(i).start()
    at_slot("oo")

    def one_mine(i, carry):
        rows = pl.ds(pl.multiple_of(core * HALF, HALF), HALF)
        x1[rows, :] = back_one(rows)
        return carry

    run("one_mine", 1, one_mine)
    at_slot("om")

    def norm_back_one(i, carry):
        rows = half_rows(core, i)
        e1 = x1[rows, :] + drecv[at(i), :].astype(F32)
        n, r = normalize(xs[rows, :].astype(F32))
        m = e1 * nw[0:1, :]
        dx = dh2[rows, :] + r * (m - row_mean(m) - n * row_mean(m * n))
        stage[at(i), :] = dx.astype(BF16)
        gn_out[0:1, :] += jnp.sum(e1 * n, axis=0, keepdims=True)
        gn_out[1:2, :] += jnp.sum(e1, axis=0, keepdims=True)
        return carry

    out_sent(lo_out, 0)
    d1_copy(0).wait()
    run("norm_back_one", 1, norm_back_one)
    at_slot("n0")
    for i in range(1, NB // 2):
        d1_copy(i).wait()
    run("norm_back_one", NB // 2 - 1, lambda i, carry: norm_back_one(i + 1, carry))

    def sum_first(l1, which):
        return [rc(l1.at[0], l1.at[slot], e_s.at[which, slot], e_r.at[which, slot], dev) for slot, dev in column]

    def sum_plane(l2, which):
        return [rc(l2.at[0], l2.at[1 + i], e_s.at[which, 8 + i], e_r.at[which, 8 + i], dev) for i, dev in enumerate(plane)]

    def sum_all():
        return [rc(sl.at[0], sl.at[slot], q_s.at[slot], q_r.at[slot], dev) for slot, dev in far]

    def sum_start(ref, l1, l2, which):
        l1[0] = jnp.concatenate([ref[0:4, : D // 2], ref[0:4, D // 2 :]], axis=0)
        for copy in sum_first(l1, which):
            copy.start()

    def sum_second(l1, l2, which):
        for copy in sum_first(l1, which):
            copy.wait()
        total = l1[0]
        for slot in range(1, 8):
            total = total + l1[slot]
        l2[0] = total
        for copy in sum_plane(l2, which):
            copy.start()

    def sum_end(ref, l1, l2, which):
        for copy in sum_plane(l2, which):
            copy.wait()
        total = l2[0]
        for i in range(1, 4):
            total = total + l2[i]
        ref[0:4, :] = jnp.concatenate([total[0:4], total[4:8]], axis=1)

    if inner:
        sum_start(gn_out, gl1, gl2, 0)
        at_slot("n1")
    else:
        out_start(ig_out, 1, 0)
        out_start(ig_out, 1, 1)
    if inner:
        total = jnp.sum(squares_ref[...], axis=0, keepdims=True)
        total = total[:, :128] + total[:, 128:]
        sl[0] = total
        for copy in sum_all():
            copy.start()
        sum_end(gn_out, gl1, gl2, 0)

        def drain_rs(s, carry):
            rs_drain(s)
            return carry

        for s in range(3):
            rs_drain(s)
        lax.fori_loop(3, PIECES, drain_rs, 0)
        for copy in sum_all():
            copy.wait()
        gn_out[4:5, 0:128] = jnp.sum(sl[...], axis=0)
        for j, gbuf in enumerate((ga_out, up_m, down_m)):
            pltpu.make_async_copy(gbuf, g_out.at[j], loc.at[10 + j]).wait()
    else:
        for j in range(3):
            g_copy = pltpu.make_async_copy(GA if j == 0 else W.at[j], g_out.at[j], loc.at[3 + j])
            g_copy.start()
            g_copy.wait()
    small_copy = pltpu.make_async_copy(gn_out, small_out, loc.at[13])
    small_copy.start()
    small_copy.wait()
    out_wait(lo_out, 0)
    out_sent(ig_out, 1)
    out_wait(ig_out, 1)

    @pl.when(core == own)
    def _():
        for i in range(3):
            in_remote(i).wait_send()


def rope_tables(length):
    places = np.arange(length, dtype=np.float32)
    rates = (ROPE_BASE ** (-(np.arange(HD // 2, dtype=np.float32) * 2.0 / HD))).astype(np.float32)
    angles = places[:, None] * rates[None, :]
    cos = np.tile(np.cos(angles), (1, 4)).astype(np.float32)
    sin = np.tile(np.sin(angles), (1, 4)).astype(np.float32)
    first = (np.arange(128) % HD < HD // 2)[None, :]
    return np.stack([cos, np.where(first, -sin, sin)]).astype(np.float32)


def adam_update(refs, outs, gradient, clip_factor, step_rate, decay_rate):
    master, first_old, second_old = (ref[...] for ref in refs)
    clipped = gradient * clip_factor
    first_new = BETA_FIRST * first_old + (1.0 - BETA_FIRST) * clipped
    second_new = BETA_SECOND * second_old + (1.0 - BETA_SECOND) * clipped * clipped
    fix_first = 1.0 - BETA_FIRST**STEP
    fix_second = 1.0 - BETA_SECOND**STEP
    normalized = first_new / fix_first / (jnp.sqrt(second_new / fix_second) + ADAM_EPSILON)
    master_new = master - step_rate * (normalized + decay_rate * master)
    for out, v in zip(outs, (master_new, first_new, second_new, master_new.astype(BF16))):
        out[...] = v


def update_kernel(R, shapes, g_in, small_in, lo_in, ig_in, *refs):
    param_ins, refs = refs[:15], refs[15:]
    lo_out, ig_out, norm_out = refs[:3]
    param_outs, refs = refs[3:23], refs[23:]
    g, small, params, outs, in_sems, out_sems = refs[0], refs[1], refs[2:17], refs[17:37], refs[37], refs[38]
    passing = [(lo_in, refs[39].at[0], lo_out), (ig_in, refs[39].at[1], ig_out)]
    copies = [pltpu.make_async_copy(src, via, in_sems.at[17 + i]) for i, (src, via, _) in enumerate(passing)]
    ins = [pltpu.make_async_copy(g_in, g, in_sems.at[15]), pltpu.make_async_copy(small_in, small, in_sems.at[16])]
    ins += [pltpu.make_async_copy(src, dst, in_sems.at[i]) for i, (src, dst) in enumerate(zip(param_ins, params))]
    for copy in ins[:2] + ins[8:11] + ins[11:] + ins[2:8] + copies:
        copy.start()
    for copy in ins[:2]:
        copy.wait()
    gn_all = small[0:4, :]
    squares = jnp.sum(small[4:5, 0:128], keepdims=True) + jnp.sum(gn_all * gn_all, keepdims=True)
    grad_norm = jnp.sqrt(squares)
    norm_out[...] = grad_norm
    clip_factor = jnp.minimum(1.0, CLIP_LIMIT / (grad_norm + 1e-06))

    def transposed(v):
        return jnp.concatenate([v, jnp.zeros((128 - R, v.shape[1]), F32)], axis=0).T[:, :R]

    a = g[0]
    g_proj = [jnp.concatenate([a[:, 128 * j : 128 * j + 128], a[:, 384 + 64 * j : 448 + 64 * j]], axis=1) for j in range(3)]
    g_out = transposed(jnp.concatenate([a[:, 640:], a[:, 576:640]], axis=1))
    D = gn_all.shape[1]
    first_row = lax.axis_index("dp") * R
    r_i = lax.broadcasted_iota(jnp.int32, (D, 128), 0)
    c_i = lax.broadcasted_iota(jnp.int32, (D, 128), 1)
    sel = jnp.where((r_i == c_i + first_row) & (c_i < R), 1.0, 0.0).astype(BF16)
    g_norm = sum(dot(part.astype(BF16), sel) for part in three_parts(small[...]))[:4, :R]

    arrivals = ins[2:]

    def update(i, gradient, rate, decay, index=None):
        ins, results = params[3 * i : 3 * i + 3], outs[4 * i : 4 * i + 4]
        if index is None or index == 0:
            for copy in arrivals[3 * i : 3 * i + 3]:
                copy.wait()
        if index is not None:
            ins, results = [r.at[index] for r in ins], [r.at[index] for r in results]
        adam_update(ins, results, gradient, clip_factor, rate, decay)
        if index is None or index == 2:
            for n in range(4 * i, 4 * i + 4):
                copies.append(pltpu.make_async_copy(outs[n], param_outs[n], out_sems.at[n]))
                copies[-1].start()

    update(2, g[1], RATE_MATRIX, WEIGHT_DECAY)
    update(3, g[2], RATE_MATRIX, WEIGHT_DECAY)
    for copy in copies[:2]:
        copy.wait()
    copies[:2] = [pltpu.make_async_copy(via, dst, out_sems.at[20 + i]) for i, (_, via, dst) in enumerate(passing)]
    for copy in copies[:2]:
        copy.start()
    for j in range(3):
        update(0, g_proj[j], RATE_MATRIX, WEIGHT_DECAY, j)
    update(1, g_out, RATE_MATRIX, WEIGHT_DECAY)
    update(4, g_norm, RATE_NORM, 0.0)
    for copy in copies:
        copy.wait()


def per_device(
    inputs,
    cotangent,
    lengths,
    proj_master,
    proj_first,
    proj_second,
    out_master,
    out_first,
    out_second,
    up_master,
    up_first,
    up_second,
    down_master,
    down_first,
    down_second,
    norm_master,
    norm_first,
    norm_second,
):
    _, T, D = inputs.shape
    R = proj_master.shape[1]
    n_dp = lax.axis_size("dp")
    inner = n_dp == 8
    d = lax.axis_index("dp")
    z = lax.axis_index("head")
    core = d % 2
    if inner:
        norm_in = norm_master
        extra = (proj_master, out_master, up_master, down_master.T)
    else:
        out_t = out_master.T
        attn = jnp.concatenate(
            [proj_master[0, :, :128], proj_master[1, :, :128], proj_master[2, :, :128]]
            + [proj_master[0, :, 128:], proj_master[1, :, 128:], proj_master[2, :, 128:]]
            + [out_t[:, 128:], out_t[:, :128]],
            axis=1,
        )
        pack = jnp.stack([attn, up_master, down_master.T]).astype(BF16)
        norm_in = jnp.pad(lax.all_gather(norm_master, "dp", axis=1, tiled=True), ((0, 4), (0, 0)))
        norm_in = norm_in.astype(BF16).astype(F32)
        full = lax.all_gather(pack, "dp", axis=1, tiled=True)
        every = lax.all_gather(full, "head", axis=0)
        pair = lax.dynamic_slice_in_dim(every, 2 * core, 2, 0)
        w_in = jnp.concatenate([pair[0], pair[1]], axis=2)
        extra = (w_in,)

    hbm = pl.BlockSpec(memory_space=pltpu.HBM)
    dma = pltpu.SemaphoreType.DMA
    quarter = T // 4
    g_shape = (3, R, 768) if inner else (3, D, 1536)
    out_shape = (
        jax.ShapeDtypeStruct((2, quarter, D), BF16),
        jax.ShapeDtypeStruct((2, quarter, D), BF16),
        jax.ShapeDtypeStruct(g_shape, F32 if inner else BF16),
        jax.ShapeDtypeStruct((8, D), F32),
    )
    HALF = T // 2
    NB = T // 256
    bf = lambda *s: pltpu.VMEM(s, BF16)
    ff = lambda *s: pltpu.VMEM(s, F32)
    RC = 2 * R
    pieces = PIECES if inner else 1
    lx_rows = RC if inner else 16
    zl_rows = R if inner else 16
    RL = R if inner else 8
    scratch = [
        bf(3, D, 1536), bf(D, 1536), bf(T, D), bf(T, D), bf(D, T), bf(T, D), bf(D, T), bf(T, D), bf(D, T), ff(T, D),
        bf(6, T, 128), bf(6, T, 128), bf(6, T, 128), bf(3, 128, T),
        bf(3, T, 128), bf(3, T, 128), bf(2, D, 256), bf(T, 2 * SUB), bf(T, 1536), ff(T, D), bf(T, D), ff(128, T), ff(T, D),
        bf(HALF, D), bf(HALF, D), bf(HALF, D), bf(HALF, D),
        ff(8, 128), ff(8, 128), bf(3, zl_rows, 768), ff(8, D), ff(8, 8, 128), ff(8, 8, D // 2), ff(4, 8, D // 2), ff(4 * n_dp, 1, 128),
        bf(pieces, 2, 2, lx_rows, SUB), bf(pieces, 2, lx_rows, SUB), bf(pieces, lx_rows, SUB), bf(pieces, 2, zl_rows, SUB),
        dma((3,)), dma((3,)), dma((3,)), dma((3,)), dma((2,)), dma((2,)), dma((NB,)), dma((NB,)),
        dma((1,)), dma((1,)), dma((NB,)), dma((NB,)), dma((2, 2, 4)), dma((2, 2, 4)), dma((4,)), dma((4,)), dma((1, 11)), dma((1, 11)), dma((4 * n_dp,)), dma((4 * n_dp,)),
        dma((3,)), dma((3,)), dma((4, 4)), dma((4, 4)), bf(4, zl_rows, SUB),
        dma((pieces, 4)), dma((pieces, 4)), dma((pieces, 2, 3)), dma((pieces, 2, 3)),
        dma((pieces, 2, 2)), dma((pieces, 2, 2)), dma((pieces, 2)), dma((pieces, 2)), dma((pieces,)), dma((pieces,)), dma((pieces, 2)), dma((pieces, 2)),
        dma((14,)),
        ff(2, T, 128), ff(*norm_in.shape), ff(3, RL, 192), ff(192, RL), ff(RL, 768), ff(RL, 768), ff(8, D), ff(RL, 768), ff(RL, SUB),
    ]
    layer_out, input_grad, grads, small = pl.pallas_call(
        functools.partial(layer_kernel, inner, T, D, R),
        out_shape=out_shape,
        in_specs=[hbm, hbm, pl.BlockSpec(memory_space=pltpu.SMEM)] + [hbm] * (2 + len(extra)),
        out_specs=(hbm,) * 4,
        scratch_shapes=scratch,
        compiler_params=pltpu.CompilerParams(
            collective_id=0, has_side_effects=True, vmem_limit_bytes=63 * 2**20
        ),
        name="layer",
    )(inputs, cotangent, lengths, jnp.asarray(rope_tables(T)), norm_in, *extra)

    if not inner:
        spread = jnp.stack([grads[:, :, :768], grads[:, :, 768:]]).astype(F32)
        empty = jnp.zeros((4,) + spread.shape[1:], F32)
        spread = lax.dynamic_update_slice_in_dim(empty, spread, 2 * core, 0)
        mine = lax.psum_scatter(spread, "head", scatter_dimension=0, tiled=False)
        grads = lax.psum_scatter(mine, "dp", scatter_dimension=1, tiled=True)
        squares = lax.psum(jnp.sum(grads * grads), ("dp", "head"))
        small = lax.psum(small, ("dp", "head")).at[4, 0].set(squares)
    params = (
        (proj_master, proj_first, proj_second),
        (out_master, out_first, out_second),
        (up_master, up_first, up_second),
        (down_master.T, down_first.T, down_second.T),
        (norm_master, norm_first, norm_second),
    )
    shapes = []
    for group in params:
        shapes += [(v.shape, F32) for v in group] + [(group[0].shape, BF16)]
    out_shapes = [((2, quarter, D), BF16)] * 2 + [((1, 1), F32)] + shapes
    flat = [v for group in params for v in group]
    outs = pl.pallas_call(
        functools.partial(update_kernel, R, shapes),
        out_shape=tuple(jax.ShapeDtypeStruct(*v) for v in out_shapes),
        in_specs=[hbm] * 19,
        out_specs=tuple([hbm] * 2 + [pl.BlockSpec(memory_space=pltpu.VMEM)] + [hbm] * 20),
        scratch_shapes=[ff(*grads.shape), ff(8, D)]
        + [ff(*v.shape) for v in flat]
        + [pltpu.VMEM(*v) for v in shapes]
        + [dma((19,)), dma((22,)), bf(2, 2, quarter, D)],
        compiler_params=pltpu.CompilerParams(vmem_limit_bytes=63 * 2**20),
        name="update",
    )(grads, small, layer_out, input_grad, *flat)
    down = tuple(v.T for v in outs[15:19])
    return tuple(outs[:2]) + (outs[2].reshape(()),) + tuple(outs[3:15]) + down + tuple(outs[19:])


def solution(mesh):
    proj, wide, tall, norms = P(None, "dp", "head"), P("dp", "head"), P("head", "dp"), P(None, "dp")
    tokens = P("dp", None, None)
    placed = (tokens, tokens, P("dp")) + (proj,) * 3 + (tall,) * 3 + (wide,) * 3 + (tall,) * 3 + (norms,) * 3
    quarters = P("dp", "head", None)
    return jax.shard_map(
        per_device,
        mesh=mesh,
        in_specs=placed,
        out_specs=(quarters, quarters, P()) + (proj,) * 4 + (tall,) * 4 + (wide,) * 4 + (tall,) * 4 + (norms,) * 4,
        check_vma=False,
    )
```
